128 devices in a mesh: row: 16 (over x, y_lo, core), col: 8 (over z, y_hi).
Axes of the slice: x: 4, y: 4 (y_hi: 2, y_lo: 2; y = y_hi * 2 + y_lo), z: 4, core: 2. Of those that a mesh axis runs over, the one named last changes fastest.
Arguments:
- covariance: float32 [16384, 16384], P('row', 'col'), as said below
- innovations: float32 [1024, 16, 1024], P('row', None, 'col'), may hold values from -6 to 6
- block_owner: int32 [64], replicated, may hold values from 0 to 63, as said below
- panel_index: int32 [1], replicated, may hold values from 0 to 31
Outputs:
- factor: float32 [16384, 16384], P('row', 'col')
- solved: float32 [1024, 16384], P('col', 'row')
The draws below stay inside these ranges and needn't reach their ends.
Inputs may be any that keep to these rules, and one draw needn't show every extreme that they name: Storage block s holds global block block_owner[s]; every global block appears once; the storage blocks s with one value of s // 4 hold the blocks of one residue modulo 16, rising with s. `covariance`: symmetric positive definite.
All inputs are finite; a program needn't handle non-finite values.
Results may differ from the reference program's by a relative error of at most 0.0016.
Values may be sent and summed in bfloat16 or wider, within the bound.
No kernel may reach another device: no remote copies, remote signals or barrier semaphores. Data moves between devices by JAX's collectives and lax.ppermute only.
A program may use at most 128 MiB of HBM per device.

```python
import jax
import jax.numpy as jnp
from jax import lax

B = 256
BR = 4
PANELS = 2
GROUPS = 16
ROWS_DEV = 1024
M = 16384
NBLK = 64
P_SIZE = 1024


def draw_covariance(key, part):
    base_key = jax.random.fold_in(key, 11)
    load_key, nugget_key = jax.random.split(base_key)
    shared_key = jax.random.fold_in(base_key, 37)
    latent = 2 * B
    loadings = jax.random.normal(load_key, (M, latent), jnp.float32)
    weights = jax.random.uniform(shared_key, (M,), jnp.float32, 0.7, 1.3)
    nugget = jnp.exp(jax.random.uniform(nugget_key, (M,), jnp.float32, -0.6931472, 0.6931472))
    row_block = jnp.arange(M, dtype=jnp.int32) // B
    indicator = (row_block[:, None] == jnp.arange(NBLK, dtype=jnp.int32)[None, :]).astype(jnp.float32)
    shared = indicator * (1.7320508 * weights)[:, None]
    combined = jnp.concatenate([loadings * (1.0 / latent ** 0.5), shared], axis=1)
    matrix = jnp.dot(combined, combined.T, precision=lax.Precision.HIGHEST)
    matrix = 0.5 * (matrix + matrix.T)
    return matrix + jnp.diag(nugget)


def draw_block_owner(key, part):
    row_order = jax.random.permutation(jax.random.fold_in(key, 23), GROUPS)
    positions = jnp.arange(NBLK, dtype=jnp.int32)
    return (positions % BR * GROUPS + row_order[positions // BR]).astype(jnp.int32)


def level_of(key, dims, cuts, least, largest):
    gain, own = 1.0, jax.random.fold_in(key, 6)
    for position, shards_of in cuts:
        steps = jnp.exp(jax.random.uniform(jax.random.fold_in(own, position), (shards_of,), jnp.float32, least / len(cuts), largest / len(cuts)))
        gain = gain * jnp.repeat(steps, dims[position] // shards_of).reshape([-1 if axis == position else 1 for axis in range(len(dims))])
    return gain


def bell_draw(own_key, extent, deviation, reach, cuts=(), held_as=jnp.bfloat16):
    entries = deviation * jax.random.normal(own_key, extent, jnp.float32)
    if cuts:
        entries = entries * level_of(own_key, extent, cuts, -0.22, 0.18)
    return jnp.clip(entries, -reach, reach).astype(held_as)


def setup_inputs(seed: int = 0) -> dict:
    splits = jax.random.split(jax.random.key(seed), 5)
    covariance = draw_covariance(jax.random.fold_in(splits[4], 71), 0)
    innovations = bell_draw(splits[1], (P_SIZE, GROUPS, ROWS_DEV), 1.0, 6.0, ((0, 16), (2, 8)), jnp.float32)
    block_owner = draw_block_owner(jax.random.fold_in(splits[4], 71), 0)
    panel_index = jax.random.randint(splits[3], (1,), 0, NBLK // 2).astype(jnp.int32)
    return dict(covariance=covariance, innovations=innovations, block_owner=block_owner, panel_index=panel_index)


CONTRACT_LAST = (((1,), (1,)), ((), ()))

def lower_solve(factor, right_side):
    return jax.scipy.linalg.solve_triangular(factor, right_side, lower=True)

def reference(covariance, innovations, block_owner, panel_index):
    matrix_order = covariance.shape[0]
    blocks = matrix_order // B
    matrix = covariance
    solved = innovations.reshape(innovations.shape[0], matrix_order)
    row_owner = jnp.repeat(block_owner, B)
    positions = jnp.arange(blocks, dtype=jnp.int32)
    for panel_turn in range(PANELS):
        target = panel_index[0] + panel_turn
        slot_index = jnp.sum(jnp.where(block_owner == target, positions, 0)).astype(jnp.int32)
        panel_start = slot_index * B
        column = lax.dynamic_slice_in_dim(matrix, panel_start, B, 1)
        diagonal = lax.dynamic_slice_in_dim(column, panel_start, B, 0)
        factor = jnp.linalg.cholesky(diagonal)
        live_rows = row_owner > target
        panel_rows = jnp.where(live_rows[:, None], lower_solve(factor, column.T).T, 0.0)
        panel_half = panel_rows.astype(jnp.bfloat16)
        matrix = matrix - lax.dot_general(panel_half.astype(jnp.float32), panel_half.astype(jnp.float32), CONTRACT_LAST, preferred_element_type=jnp.float32)
        innovation_block = lax.dynamic_slice_in_dim(solved, panel_start, B, 1)
        whitened = lower_solve(factor, innovation_block.T).T
        solved = solved - lax.dot_general(whitened.astype(jnp.bfloat16).astype(jnp.float32), panel_half.astype(jnp.float32), CONTRACT_LAST, preferred_element_type=jnp.float32)
        solved = lax.dynamic_update_slice_in_dim(solved, whitened, panel_start, 1)
        row_block = lax.dynamic_slice_in_dim(matrix, panel_start, B, 0)
        row_block = jnp.where(live_rows[None, :], 0.0, row_block)
        matrix = lax.dynamic_update_slice_in_dim(matrix, row_block, panel_start, 0)
        column_old = lax.dynamic_slice_in_dim(matrix, panel_start, B, 1)
        column_new = jnp.where(live_rows[:, None], panel_rows, column_old)
        column_new = lax.dynamic_update_slice_in_dim(column_new, factor, panel_start, 0)
        matrix = lax.dynamic_update_slice_in_dim(matrix, column_new, panel_start, 1)
    return (matrix, solved)
```

```python
import functools

import jax
import jax.numpy as jnp
from jax import lax
from jax.experimental import pallas as pl
from jax.experimental.pallas import tpu as pltpu
from jax.sharding import PartitionSpec as P

B = 256
S = 64
F32 = jnp.float32
BF16 = jnp.bfloat16
HIGH = lax.Precision.HIGHEST
VMEM_SPEC = pl.BlockSpec(memory_space=pltpu.VMEM)
SMEM_SPEC = pl.BlockSpec(memory_space=pltpu.SMEM)


def dot(a, b, dims, precision=None):
    return lax.dot_general(a, b, (dims, ((), ())), precision=precision, preferred_element_type=F32)


NN = ((1,), (0,))
NT = ((1,), (1,))
TN = ((0,), (0,))


def pick_kernel(slots, cov_ref, out_ref):
    out_ref[...] = cov_ref[...].reshape(out_ref.shape)


def pick_columns(slots, covariance, parts):
    rows = covariance.shape[0]
    blocks = rows // B
    part = B // parts
    return pl.pallas_call(
        pick_kernel,
        grid_spec=pltpu.PrefetchScalarGridSpec(
            num_scalar_prefetch=1,
            grid=(blocks, 2),
            in_specs=[pl.BlockSpec((B, B), lambda b, j, slots: (b, slots[j]))],
            out_specs=pl.BlockSpec((parts, 1, part, B), lambda b, j, slots: (0, b, 0, j)),
        ),
        out_shape=jax.ShapeDtypeStruct((parts, blocks, part, 2 * B), F32),
    )(slots, covariance)


def lanes(tile, j):
    return jnp.broadcast_to(tile[:, j : j + 1], (8, 128))


def eliminate(tiles):
    sub = lax.broadcasted_iota(jnp.int32, (8, 128), 0)
    scales = []
    for t in range(8):
        own = tiles[t]
        cols = [lanes(own, 8 * t + j) for j in range(8)]
        inv, cross = [], {}
        pivots = jnp.ones((8, 128), F32)
        for j in range(8):
            pivot = jnp.broadcast_to(cols[j][j : j + 1, :], (8, 128))
            pivots = jnp.where(sub == j, pivot, pivots)
            r = 1.0 / pivot
            inv.append(r)
            if j == 7:
                break
            m = jnp.where(sub > j, cols[j] * r, 0.0)
            for k in range(j + 1, 8):
                cross[j, k] = jnp.broadcast_to(cols[k][j : j + 1, :], (8, 128))
                cols[k] = cols[k] - m * cross[j, k]
            own = own - m * jnp.broadcast_to(own[j : j + 1, :], (8, 128))
        tiles[t] = own
        scales.append(lax.rsqrt(pivots))
        rows = [jnp.broadcast_to(own[j : j + 1, :], (8, 128)) for j in range(8)]
        for i in range(t + 1, 8):
            low = tiles[i]
            cols = [lanes(low, 8 * t + j) for j in range(8)]
            for j in range(8):
                m = cols[j] * inv[j]
                for k in range(j + 1, 8):
                    cols[k] = cols[k] - m * cross[j, k]
                low = low - m * rows[j]
            tiles[i] = low
    return tiles, scales


def factor_block(work, small, inverse_small):
    for b in range(B // S):
        lo, hi = b * S, (b + 1) * S
        small[:, 0:S] = work[lo:hi, lo:hi]
        row = lax.broadcasted_iota(jnp.int32, (S, S), 0)
        col = lax.broadcasted_iota(jnp.int32, (S, S), 1)
        small[:, S : 2 * S] = jnp.where(row == col, 1.0, 0.0)
        tiles, scales = eliminate([small[8 * i : 8 * i + 8, :] for i in range(8)])
        for i in range(8):
            small[8 * i : 8 * i + 8, :] = tiles[i] * scales[i]
        inverse_small[...] = small[:, S : 2 * S]
        top = dot(inverse_small[...], work[lo:hi, :], NN, HIGH)
        work[lo:hi, :] = top
        if hi < B:
            work[hi:B, :] = work[hi:B, :] - dot(top[:, hi:B], top, TN, HIGH)


def factor_kernel(diag_ref, x0_ref, x1_ref, l10t_ref, l00_ref, l11_ref, work, small, inverse_small):
    row = lax.broadcasted_iota(jnp.int32, (B, B), 0)
    col = lax.broadcasted_iota(jnp.int32, (B, B), 1)
    eye = jnp.where(row == col, 1.0, 0.0)
    work[:, 0:B] = diag_ref[:, 0:B]
    work[:, B : 2 * B] = eye
    factor_block(work, small, inverse_small)
    x0 = work[:, B : 2 * B]
    x0_ref[...] = x0
    l00_ref[...] = jnp.where(row <= col, work[:, 0:B], 0.0).T
    l10t = dot(x0, diag_ref[:, B : 2 * B], NN, HIGH).astype(BF16)
    l10t_ref[...] = l10t
    work[:, 0:B] = diag_ref[:, 2 * B : 3 * B] - dot(l10t, l10t, TN)
    work[:, B : 2 * B] = eye
    factor_block(work, small, inverse_small)
    x1_ref[...] = work[:, B : 2 * B]
    l11_ref[...] = jnp.where(row <= col, work[:, 0:B], 0.0).T


def factor_diagonal(diag):
    square = jax.ShapeDtypeStruct((B, B), F32)
    return pl.pallas_call(
        factor_kernel,
        in_specs=[VMEM_SPEC],
        out_specs=[VMEM_SPEC] * 5,
        out_shape=[square, square, jax.ShapeDtypeStruct((B, B), BF16), square, square],
        scratch_shapes=[pltpu.VMEM((B, 2 * B), F32), pltpu.VMEM((S, 2 * S), F32), pltpu.VMEM((S, S), F32)],
        cost_estimate=pl.CostEstimate(flops=2 * 10**10, bytes_accessed=80_000_000, transcendentals=0),
    )(diag)


def solve_rows(first, second, x0, x1, l10t):
    p0 = dot(first, x0, NT, HIGH)
    p1 = dot(second - dot(p0.astype(BF16), l10t, NN), x1, NT, HIGH)
    return p0, p1


def update_kernel(
    flags, cov_ref, across_ref, along_ref, x0_ref, x1_ref, l10t_ref, l00_ref, l11_ref, out_ref, rows_ref, pc
):
    i = pl.program_id(0)
    parts, part = along_ref.shape[0], along_ref.shape[2]
    column_blocks = pc.shape[0] // B
    blocks = column_blocks // 2

    @pl.when(i == 0)
    def _():
        @pl.loop(0, parts)
        def _(q):
            raw = [across_ref[pl.ds(2 * q, 2), j].reshape(2 * 128, 128) for j in range(4)]
            p0, p1 = solve_rows(
                jnp.concatenate(raw[:2], axis=1),
                jnp.concatenate(raw[2:], axis=1),
                x0_ref[...],
                x1_ref[...],
                l10t_ref[...],
            )
            p0, p1 = p0.astype(BF16), p1.astype(BF16)
            for n in range(column_blocks):
                place = pl.ds(pl.multiple_of(n * B + q * part, part), part)
                here = slice(n * part, (n + 1) * part)
                pc[place, 0:B] = jnp.where(flags[8 + n] > 0, p0[here], jnp.zeros_like(p0[here]))
                pc[place, B : 2 * B] = jnp.where(flags[8 + n] > 1, p1[here], jnp.zeros_like(p1[here]))

    level = flags[16 + i]
    raw = along_ref[:, 0].reshape(parts * part, 2 * B)
    p0, p1 = solve_rows(raw[:, 0:B], raw[:, B : 2 * B], x0_ref[...], x1_ref[...], l10t_ref[...])
    p0 = jnp.where(level > 0, p0, 0.0)
    p1 = jnp.where(level > 1, p1, 0.0)
    rows_ref[:, 0:B] = p0.astype(BF16)
    rows_ref[:, B : 2 * B] = p1.astype(BF16)
    for n in range(column_blocks):
        cut = slice(n * B, (n + 1) * B)
        out_ref[:, cut] = cov_ref[:, cut] - dot(rows_ref[...], pc[cut, :], NT)

    for panel, factor_ref, solved in ((0, l00_ref, p0), (1, l11_ref, p1)):
        is_row = i == flags[2 + panel]
        for n in range(column_blocks):

            @pl.when(is_row & (flags[8 + n] > panel))
            def _():
                out_ref[:, n * B : (n + 1) * B] = jnp.zeros((B, B), F32)

        column = flags[4 + panel]
        place = pl.ds(pl.multiple_of(jnp.maximum(column, 0) * B, B), B)

        @pl.when((column >= 0) & (level > panel))
        def _():
            out_ref[:, place] = solved

        @pl.when((column >= 0) & is_row)
        def _():
            out_ref[:, place] = factor_ref[...]


def update(flags, covariance, across, along, factors):
    rows, columns = covariance.shape
    blocks = rows // B
    parts = along.shape[0]
    part = B // parts
    whole = lambda *shape: pl.BlockSpec(shape, lambda i, flags: (0,) * len(shape))
    return pl.pallas_call(
        update_kernel,
        grid_spec=pltpu.PrefetchScalarGridSpec(
            num_scalar_prefetch=1,
            grid=(blocks,),
            in_specs=[
                pl.BlockSpec((B, columns), lambda i, flags: (i, 0)),
                whole(*across.shape),
                pl.BlockSpec((parts, 1, part, 2 * B), lambda i, flags: (0, i, 0, 0)),
            ]
            + [whole(B, B)] * 5,
            out_specs=[
                pl.BlockSpec((B, columns), lambda i, flags: (i, 0)),
                pl.BlockSpec((B, 2 * B), lambda i, flags: (i, 0)),
            ],
            scratch_shapes=[pltpu.VMEM((columns, 2 * B), BF16)],
        ),
        out_shape=[jax.ShapeDtypeStruct((rows, columns), F32), jax.ShapeDtypeStruct((rows, 2 * B), BF16)],
        compiler_params=pltpu.CompilerParams(vmem_limit_bytes=48 * 1024 * 1024),
        cost_estimate=pl.CostEstimate(flops=10**10, bytes_accessed=24_000_000, transcendentals=0),
    )(flags, covariance, across, along, *factors)


def forward_kernel(flags, relaid_ref, across_ref, rows_ref, x0_ref, x1_ref, l10t_ref, out_ref, white):
    half = relaid_ref.shape[1]
    width = relaid_ref.shape[2]
    raw = []
    for panel in range(2):
        first = flags[6 + panel]
        for h in range(2):
            for parity in range(2):
                piece = across_ref[first + 2 * h + parity, 4, panel * half : (panel + 1) * half, :]
                white[parity * half : (parity + 1) * half, panel * B + h * width : panel * B + (h + 1) * width] = piece
    w0, w1 = solve_rows(white[:, 0:B], white[:, B : 2 * B], x0_ref[...], x1_ref[...], l10t_ref[...])
    white[:, 0:B] = w0
    white[:, B : 2 * B] = w1
    product = dot(white[...].astype(BF16), rows_ref[...], NT)
    for n in range(relaid_ref.shape[0]):
        q, parity = n // 2, n % 2
        there = (slice(parity * half, (parity + 1) * half), slice(q * width, (q + 1) * width))
        out_ref[there] = relaid_ref[n] - product[there]
    for panel in range(2):
        block = flags[2 + panel]

        @pl.when(block >= 0)
        def _():
            place = pl.ds(pl.multiple_of(jnp.maximum(block, 0) * B, B), B)
            out_ref[:, place] = white[:, panel * B : (panel + 1) * B]


def forward(flags, relaid, across, rows, factors):
    particles = 2 * relaid.shape[1]
    return pl.pallas_call(
        forward_kernel,
        in_specs=[SMEM_SPEC] + [VMEM_SPEC] * 6,
        out_specs=VMEM_SPEC,
        out_shape=jax.ShapeDtypeStruct((particles, rows.shape[0]), F32),
        scratch_shapes=[pltpu.VMEM((particles, 2 * B), F32)],
        compiler_params=pltpu.CompilerParams(vmem_limit_bytes=32 * 1024 * 1024),
        cost_estimate=pl.CostEstimate(flops=10**9, bytes_accessed=8_000_000, transcendentals=0),
    )(flags, relaid, across, rows, *factors[:3])


def per_device(covariance, innovations, block_owner, panel_index, *, n_row, n_col):
    local_rows, local_cols = covariance.shape
    row_blocks, column_blocks = local_rows // B, local_cols // B
    r, c = lax.axis_index("row"), lax.axis_index("col")
    targets = panel_index[0] + jnp.arange(2, dtype=jnp.int32)
    positions = jnp.arange(block_owner.shape[0], dtype=jnp.int32)
    slot = jnp.sum(jnp.where(block_owner[None, :] == targets[:, None], positions[None, :], 0), axis=1)
    row_root, column_root = slot // row_blocks, slot // column_blocks
    row_slot, column_slot = slot % row_blocks, slot % column_blocks
    levels = jnp.sum((block_owner[:, None] > targets[None, :]).astype(jnp.int32), axis=1)
    flags = jnp.concatenate(
        [
            jnp.zeros((2,), jnp.int32),
            jnp.where(row_root == r, row_slot, -1),
            jnp.where(column_root == c, column_slot, -1),
            row_slot * 4,
            lax.dynamic_slice_in_dim(levels, c * column_blocks, column_blocks),
            lax.dynamic_slice_in_dim(levels, r * row_blocks, row_blocks),
        ]
    ).astype(jnp.int32)
    across_axes = [
        (a * n_col + b, (2 * b + a % 2) * n_col + a // 2) for a in range(n_row) for b in range(n_col)
    ]

    turned = lax.ppermute(jnp.transpose(innovations, (1, 0, 2)), ("row", "col"), across_axes)

    picked = pick_columns(column_slot.astype(jnp.int32), covariance, n_col)
    parts = lax.all_to_all(picked, "col", split_axis=0, concat_axis=0, tiled=True)
    piece = jnp.concatenate(
        [
            lax.dynamic_index_in_dim(parts[..., :B], column_root[0], 0, keepdims=False),
            lax.dynamic_index_in_dim(parts[..., B:], column_root[1], 0, keepdims=False),
        ],
        axis=-1,
    )
    part = piece.shape[1]

    chosen = jnp.where(r == row_root[0], row_slot[0], row_slot[1])
    mine = lax.dynamic_index_in_dim(piece, chosen, 0, keepdims=False)
    spread = lax.all_to_all(
        jnp.broadcast_to(mine[None], (n_row,) + mine.shape), "row", split_axis=0, concat_axis=0, tiled=True
    )
    upper = lax.dynamic_index_in_dim(spread, row_root[0], 0, keepdims=False)
    lower = lax.dynamic_index_in_dim(spread[..., B:], row_root[1], 0, keepdims=False)
    strip = jnp.concatenate([upper, lower], axis=-1)
    diag = lax.all_to_all(
        jnp.broadcast_to(strip[None], (n_col,) + strip.shape), "col", split_axis=0, concat_axis=0, tiled=True
    ).reshape(B, 3 * B)

    tiled = jnp.transpose(piece.reshape(row_blocks * part, 4, 128), (1, 0, 2))
    tiled = lax.ppermute(tiled, ("row", "col"), across_axes)
    wanted = jnp.concatenate(
        [
            lax.dynamic_index_in_dim(turned, row_root[0], 0, keepdims=False),
            lax.dynamic_index_in_dim(turned, row_root[1], 0, keepdims=False),
        ],
        axis=0,
    )
    across = lax.all_gather(jnp.concatenate([tiled, wanted[None]], axis=0), "row", axis=0)

    factors = factor_diagonal(diag)

    along = lax.all_to_all(
        jnp.broadcast_to(piece[None], (n_col,) + piece.shape), "col", split_axis=0, concat_axis=0, tiled=True
    )
    relaid = lax.all_to_all(turned, "row", split_axis=0, concat_axis=0, tiled=True)

    matrix, rows = update(flags, covariance, across, along, factors)
    solved = forward(flags, relaid, across, rows, factors)
    return matrix, solved


def solution(mesh):
    placed = (P("row", "col"), P("row", None, "col"), P(), P())
    return jax.shard_map(
        functools.partial(per_device, n_row=mesh.shape["row"], n_col=mesh.shape["col"]),
        mesh=mesh,
        in_specs=placed,
        out_specs=(P("row", "col"), P("col", "row")),
        check_vma=False,
    )
```

```python
import functools

import jax
import jax.numpy as jnp
from jax import lax
from jax.experimental import pallas as pl
from jax.experimental.pallas import tpu as pltpu
from jax.sharding import PartitionSpec as P

B = 256
S = 64
VMEM_BYTES = 60 * 1024 * 1024
F32 = jnp.float32
BF16 = jnp.bfloat16
HIGH = lax.Precision.HIGHEST
VMEM_SPEC = pl.BlockSpec(memory_space=pltpu.VMEM)
SMEM_SPEC = pl.BlockSpec(memory_space=pltpu.SMEM)


def dot(a, b, dims, precision=None):
    return lax.dot_general(a, b, (dims, ((), ())), precision=precision, preferred_element_type=F32)


NN = ((1,), (0,))
NT = ((1,), (1,))
TN = ((0,), (0,))


def pick_kernel(slots, cov_ref, out_ref):
    parts, blocks, part, width = out_ref.shape
    for b in range(blocks):
        out_ref[:, b] = cov_ref[b * B : (b + 1) * B, :].reshape(parts, part, width)


def pick_columns(slots, covariance, parts):
    rows = covariance.shape[0]
    blocks = rows // B
    part = B // parts
    return pl.pallas_call(
        pick_kernel,
        grid_spec=pltpu.PrefetchScalarGridSpec(
            num_scalar_prefetch=1,
            grid=(2, blocks // 2),
            in_specs=[pl.BlockSpec((2 * B, B), lambda j, b, slots: (b, slots[j]))],
            out_specs=pl.BlockSpec((parts, 2, part, B), lambda j, b, slots: (0, b, 0, j)),
        ),
        out_shape=jax.ShapeDtypeStruct((parts, blocks, part, 2 * B), F32),
    )(slots, covariance)


def lanes(tile, j):
    return jnp.broadcast_to(tile[:, j : j + 1], (8, 128))


def eliminate(tiles):
    sub = lax.broadcasted_iota(jnp.int32, (8, 128), 0)
    scales = []
    for t in range(8):
        own = tiles[t]
        cols = [lanes(own, 8 * t + j) for j in range(8)]
        inv, cross = [], {}
        pivots = jnp.ones((8, 128), F32)
        for j in range(8):
            pivot = jnp.broadcast_to(cols[j][j : j + 1, :], (8, 128))
            pivots = jnp.where(sub == j, pivot, pivots)
            r = 1.0 / pivot
            inv.append(r)
            if j == 7:
                break
            m = jnp.where(sub > j, cols[j] * r, 0.0)
            for k in range(j + 1, 8):
                cross[j, k] = jnp.broadcast_to(cols[k][j : j + 1, :], (8, 128))
                cols[k] = cols[k] - m * cross[j, k]
            own = own - m * jnp.broadcast_to(own[j : j + 1, :], (8, 128))
        tiles[t] = own
        scales.append(lax.rsqrt(pivots))
        rows = [jnp.broadcast_to(own[j : j + 1, :], (8, 128)) for j in range(8)]
        for i in range(t + 1, 8):
            low = tiles[i]
            cols = [lanes(low, 8 * t + j) for j in range(8)]
            for j in range(8):
                m = cols[j] * inv[j]
                for k in range(j + 1, 8):
                    cols[k] = cols[k] - m * cross[j, k]
                low = low - m * rows[j]
            tiles[i] = low
    return tiles, scales


def factor_block(work, small, inverse_small):
    for b in range(B // S):
        lo, hi = b * S, (b + 1) * S
        small[:, 0:S] = work[lo:hi, lo:hi]
        row = lax.broadcasted_iota(jnp.int32, (S, S), 0)
        col = lax.broadcasted_iota(jnp.int32, (S, S), 1)
        small[:, S : 2 * S] = jnp.where(row == col, 1.0, 0.0)
        tiles, scales = eliminate([small[8 * i : 8 * i + 8, :] for i in range(8)])
        for i in range(8):
            small[8 * i : 8 * i + 8, :] = tiles[i] * scales[i]
        inverse_small[...] = small[:, S : 2 * S]
        top = dot(inverse_small[...], work[lo:hi, :], NN, HIGH)
        work[lo:hi, :] = top
        if hi < B:
            work[hi:B, :] = work[hi:B, :] - dot(top[:, hi:B], top, TN, HIGH)


def factor_kernel(diag_ref, packed_ref, l10t_ref, work, small, inverse_small):
    row = lax.broadcasted_iota(jnp.int32, (B, B), 0)
    col = lax.broadcasted_iota(jnp.int32, (B, B), 1)
    eye = jnp.where(row == col, 1.0, 0.0)
    work[:, 0:B] = diag_ref[:, 0:B]
    work[:, B : 2 * B] = eye
    factor_block(work, small, inverse_small)
    x0 = work[:, B : 2 * B]
    packed_ref[:, 0:B] = x0
    packed_ref[:, 2 * B : 3 * B] = jnp.where(row <= col, work[:, 0:B], 0.0).T
    l10t = dot(x0, diag_ref[:, B : 2 * B], NN, HIGH).astype(BF16)
    l10t_ref[...] = l10t
    work[:, 0:B] = diag_ref[:, 2 * B : 3 * B] - dot(l10t, l10t, TN)
    work[:, B : 2 * B] = eye
    factor_block(work, small, inverse_small)
    packed_ref[:, B : 2 * B] = work[:, B : 2 * B]
    packed_ref[:, 3 * B : 4 * B] = jnp.where(row <= col, work[:, 0:B], 0.0).T


def factor_diagonal(diag):
    return pl.pallas_call(
        factor_kernel,
        in_specs=[VMEM_SPEC],
        out_specs=[VMEM_SPEC] * 2,
        out_shape=[jax.ShapeDtypeStruct((B, 4 * B), F32), jax.ShapeDtypeStruct((B, B), BF16)],
        scratch_shapes=[pltpu.VMEM((B, 2 * B), F32), pltpu.VMEM((S, 2 * S), F32), pltpu.VMEM((S, S), F32)],
        compiler_params=pltpu.CompilerParams(vmem_limit_bytes=VMEM_BYTES),
        cost_estimate=pl.CostEstimate(flops=2 * 10**10, bytes_accessed=80_000_000, transcendentals=0),
    )(diag)


def solve_rows(first, second, packed_ref, l10t_ref):
    p0 = dot(first, packed_ref[:, 0:B], NT, HIGH)
    p1 = dot(second - dot(p0.astype(BF16), l10t_ref[...], NN), packed_ref[:, B : 2 * B], NT, HIGH)
    return p0, p1


def across_kernel(flags, across_ref, packed_ref, l10t_ref, pc_ref, white_ref, raw):
    k = pl.program_id(0)
    pairs, part = pc_ref.shape[2], pc_ref.shape[3]
    blocks = pc_ref.shape[1]
    held = blocks * part
    half = raw.shape[0] // 2
    fold = half // 2

    p0, p1 = solve_rows(
        across_ref[:, 0:held, 0:B].reshape(4 * held, B),
        across_ref[:, 0:held, B : 2 * B].reshape(4 * held, B),
        packed_ref,
        l10t_ref,
    )
    p0, p1 = p0.astype(BF16), p1.astype(BF16)
    for n in range(4):
        h, parity = n // 2, n % 2
        for b in range(blocks):
            here = slice(n * held + b * part, n * held + (b + 1) * part)
            level = flags[8 + parity * blocks + b]
            pc_ref[parity, b, h, :, 0:B] = jnp.where(level > 0, p0[here], jnp.zeros_like(p0[here]))
            pc_ref[parity, b, h, :, B : 2 * B] = jnp.where(level > 1, p1[here], jnp.zeros_like(p1[here]))

    for panel in range(2):

        @pl.when(k == flags[6 + panel])
        def _():
            for n in range(4):
                h, parity = n // 2, n % 2
                for f in range(2):
                    lane = (2 * f + panel) * 128
                    raw[
                        parity * half + f * fold : parity * half + (f + 1) * fold,
                        panel * B + h * 128 : panel * B + (h + 1) * 128,
                    ] = across_ref[n, held : held + fold, lane : lane + 128]

    @pl.when(k == pl.num_programs(0) - 1)
    def _():
        w0, w1 = solve_rows(raw[:, 0:B], raw[:, B : 2 * B], packed_ref, l10t_ref)
        white_ref[:, 0:B] = w0
        white_ref[:, B : 2 * B] = w1


def whole(*shape):
    return pl.BlockSpec(shape, lambda i, flags: (0,) * len(shape))


def solve_across(flags, across, packed, l10t, blocks, parts, particles):
    part = B // parts
    steps = across.shape[0] // 4
    return pl.pallas_call(
        across_kernel,
        grid_spec=pltpu.PrefetchScalarGridSpec(
            num_scalar_prefetch=1,
            grid=(steps,),
            in_specs=[
                pl.BlockSpec((4,) + across.shape[1:], lambda k, flags: (k, 0, 0)),
                whole(*packed.shape),
                whole(*l10t.shape),
            ],
            out_specs=[
                pl.BlockSpec(
                    (2, blocks, 2, part, 2 * B), lambda k, flags: (0, 0, lax.rem(k + steps - flags[0], steps), 0, 0)
                ),
                whole(particles, 2 * B),
            ],
            scratch_shapes=[pltpu.VMEM((particles, 2 * B), F32)],
        ),
        out_shape=[
            jax.ShapeDtypeStruct((2, blocks, parts, part, 2 * B), BF16),
            jax.ShapeDtypeStruct((particles, 2 * B), F32),
        ],
        compiler_params=pltpu.CompilerParams(vmem_limit_bytes=VMEM_BYTES),
        cost_estimate=pl.CostEstimate(flops=6 * 10**9, bytes_accessed=8_000_000, transcendentals=0),
    )(flags, across, packed, l10t)


def update_kernel(flags, cov_ref, along_ref, pc_ref, white_ref, packed_ref, l10t_ref, out_ref, product_ref):
    i = pl.program_id(0)
    parts, part = along_ref.shape[0], along_ref.shape[2]
    column_blocks = pc_ref.shape[0] // B

    level = flags[16 + i]
    raw = along_ref[:, 0].reshape(parts * part, 2 * B)
    p0, p1 = solve_rows(raw[:, 0:B], raw[:, B : 2 * B], packed_ref, l10t_ref)
    p0 = jnp.where(level > 0, p0, 0.0)
    p1 = jnp.where(level > 1, p1, 0.0)
    rows = jnp.concatenate([p0.astype(BF16), p1.astype(BF16)], axis=1)
    for n in range(column_blocks):
        cut = slice(n * B, (n + 1) * B)
        out_ref[:, cut] = cov_ref[:, cut] - dot(rows, pc_ref[cut, :], NT)
    product_ref[...] = dot(white_ref[...].astype(BF16), rows, NT)

    for panel, solved in ((0, p0), (1, p1)):
        is_row = i == flags[2 + panel]
        for n in range(column_blocks):

            @pl.when(is_row & (flags[8 + n] > panel))
            def _():
                out_ref[:, n * B : (n + 1) * B] = jnp.zeros((B, B), F32)

        column = flags[4 + panel]
        place = pl.ds(pl.multiple_of(jnp.maximum(column, 0) * B, B), B)

        @pl.when((column >= 0) & (level > panel))
        def _():
            out_ref[:, place] = solved

        @pl.when((column >= 0) & is_row)
        def _():
            out_ref[:, place] = packed_ref[:, (2 + panel) * B : (3 + panel) * B]


def update(flags, covariance, along, pc, white, packed, l10t):
    rows, columns = covariance.shape
    blocks = rows // B
    parts = along.shape[0]
    part = B // parts
    particles = white.shape[0]
    return pl.pallas_call(
        update_kernel,
        grid_spec=pltpu.PrefetchScalarGridSpec(
            num_scalar_prefetch=1,
            grid=(blocks,),
            in_specs=[
                pl.BlockSpec((B, columns), lambda i, flags: (i, 0)),
                pl.BlockSpec((parts, 1, part, 2 * B), lambda i, flags: (0, i, 0, 0)),
                whole(*pc.shape),
                whole(*white.shape),
                whole(*packed.shape),
                whole(*l10t.shape),
            ],
            out_specs=[
                pl.BlockSpec((B, columns), lambda i, flags: (i, 0)),
                pl.BlockSpec((particles, B), lambda i, flags: (0, i)),
            ],
        ),
        out_shape=[jax.ShapeDtypeStruct((rows, columns), F32), jax.ShapeDtypeStruct((particles, rows), F32)],
        compiler_params=pltpu.CompilerParams(vmem_limit_bytes=VMEM_BYTES),
        cost_estimate=pl.CostEstimate(flops=5 * 10**9, bytes_accessed=20_000_000, transcendentals=0),
    )(flags, covariance, along, pc, white, packed, l10t)


def forward_kernel(flags, relaid_ref, product_ref, white_ref, out_ref):
    half, width = relaid_ref.shape[1:]
    steps = relaid_ref.shape[0] // 4
    for q in range(relaid_ref.shape[0] // 2):
        first = lax.rem(q // 2 + flags[0], steps) * 4 + q % 2 * 2
        for parity in range(2):
            there = (slice(parity * half, (parity + 1) * half), slice(q * width, (q + 1) * width))
            out_ref[there] = relaid_ref[first + parity] - product_ref[there]
    for panel in range(2):
        block = flags[2 + panel]

        @pl.when(block >= 0)
        def _():
            place = pl.ds(pl.multiple_of(jnp.maximum(block, 0) * B, B), B)
            out_ref[:, place] = white_ref[:, panel * B : (panel + 1) * B]


def forward(flags, relaid, product, white):
    return pl.pallas_call(
        forward_kernel,
        in_specs=[SMEM_SPEC] + [VMEM_SPEC] * 3,
        out_specs=VMEM_SPEC,
        out_shape=jax.ShapeDtypeStruct(product.shape, F32),
        compiler_params=pltpu.CompilerParams(vmem_limit_bytes=VMEM_BYTES),
        cost_estimate=pl.CostEstimate(flops=10**6, bytes_accessed=2_000_000, transcendentals=0),
    )(flags, relaid, product, white)


def per_device(covariance, innovations, block_owner, panel_index, *, n_row, n_col):
    local_rows, local_cols = covariance.shape
    row_blocks, column_blocks = local_rows // B, local_cols // B
    r, c = lax.axis_index("row"), lax.axis_index("col")
    targets = panel_index[0] + jnp.arange(2, dtype=jnp.int32)
    positions = jnp.arange(block_owner.shape[0], dtype=jnp.int32)
    slot = jnp.sum(jnp.where(block_owner[None, :] == targets[:, None], positions[None, :], 0), axis=1)
    row_root, column_root = slot // row_blocks, slot // column_blocks
    row_slot, column_slot = slot % row_blocks, slot % column_blocks
    levels = jnp.sum((block_owner[:, None] > targets[None, :]).astype(jnp.int32), axis=1)
    steps = n_row // 4
    shift = c // 2
    flags = jnp.concatenate(
        [
            jnp.full((2,), shift, jnp.int32),
            jnp.where(row_root == r, row_slot, -1),
            jnp.where(column_root == c, column_slot, -1),
            (row_slot + shift) % steps,
            lax.dynamic_slice_in_dim(levels, c * column_blocks, column_blocks),
            lax.dynamic_slice_in_dim(levels, r * row_blocks, row_blocks),
        ]
    ).astype(jnp.int32)
    across_axes = [
        (a * n_col + b, ((b // 2 + a // 4) % steps * 4 + b % 2 * 2 + a % 2) * n_col + a // 2)
        for a in range(n_row)
        for b in range(n_col)
    ]

    turned = lax.ppermute(jnp.transpose(innovations, (1, 0, 2)), ("row", "col"), across_axes)

    picked = pick_columns(column_slot.astype(jnp.int32), covariance, n_col)
    parts = lax.all_to_all(picked, "col", split_axis=0, concat_axis=0, tiled=True)
    part = parts.shape[2]
    piece = jnp.concatenate(
        [
            lax.dynamic_slice(parts, (column_root[n], 0, 0, n * B), (1, row_blocks, part, B))[0]
            for n in range(2)
        ],
        axis=-1,
    )

    chosen = jnp.where(r == row_root[0], row_slot[0], row_slot[1])
    mine = lax.dynamic_index_in_dim(piece, chosen, 0, keepdims=False)
    spread = lax.all_to_all(
        jnp.broadcast_to(mine[None], (n_row,) + mine.shape), "row", split_axis=0, concat_axis=0, tiled=True
    )
    upper = lax.dynamic_slice(spread, (row_root[0], 0, 0), (1, part, 2 * B))[0]
    lower = lax.dynamic_slice(spread, (row_root[1], 0, B), (1, part, B))[0]
    strip = jnp.concatenate([upper, lower], axis=-1)
    diag = lax.all_to_all(
        jnp.broadcast_to(strip[None], (n_col,) + strip.shape), "col", split_axis=0, concat_axis=0, tiled=True
    ).reshape(B, 3 * B)

    tiled = lax.ppermute(piece.reshape(row_blocks * part, 2 * B), ("row", "col"), across_axes)
    wanted = [lax.dynamic_index_in_dim(turned, row_root[n], 0, keepdims=False) for n in range(2)]
    fold = wanted[0].shape[0] // 2
    wanted = jnp.concatenate([wanted[0][:fold], wanted[1][:fold], wanted[0][fold:], wanted[1][fold:]], axis=1)
    payload, _ = lax.optimization_barrier((jnp.concatenate([tiled, wanted], axis=0), spread))
    across = lax.all_gather(payload, "row", axis=0)

    packed, l10t = factor_diagonal(diag)

    along = lax.all_to_all(
        jnp.broadcast_to(piece[None], (n_col,) + piece.shape), "col", split_axis=0, concat_axis=0, tiled=True
    )
    relaid = lax.all_to_all(turned, "row", split_axis=0, concat_axis=0, tiled=True)

    pc, white = solve_across(flags, across, packed, l10t, row_blocks, n_col, 2 * turned.shape[1])
    matrix, product = update(flags, covariance, along, pc.reshape(local_cols, 2 * B), white, packed, l10t)
    solved = forward(flags, relaid, product, white)
    return matrix, solved


def solution(mesh):
    placed = (P("row", "col"), P("row", None, "col"), P(), P())
    return jax.shard_map(
        functools.partial(per_device, n_row=mesh.shape["row"], n_col=mesh.shape["col"]),
        mesh=mesh,
        in_specs=placed,
        out_specs=(P("row", "col"), P("col", "row")),
        check_vma=False,
    )
```

```python
import functools

import jax
import jax.numpy as jnp
from jax import lax
from jax.experimental import pallas as pl
from jax.experimental.pallas import tpu as pltpu
from jax.sharding import PartitionSpec as P

B = 256
S = 64
VMEM_BYTES = 60 * 1024 * 1024
F32 = jnp.float32
BF16 = jnp.bfloat16
HIGH = lax.Precision.HIGHEST
VMEM_SPEC = pl.BlockSpec(memory_space=pltpu.VMEM)
SMEM_SPEC = pl.BlockSpec(memory_space=pltpu.SMEM)


def dot(a, b, dims, precision=None):
    return lax.dot_general(a, b, (dims, ((), ())), precision=precision, preferred_element_type=F32)


NN = ((1,), (0,))
NT = ((1,), (1,))
TN = ((0,), (0,))


def pick_kernel(slots, cov_ref, out_ref):
    parts, blocks, part, width = out_ref.shape
    for b in range(blocks):
        out_ref[:, b] = cov_ref[b * B : (b + 1) * B, :].reshape(parts, part, width)


def pick_columns(slots, covariance, parts):
    rows = covariance.shape[0]
    blocks = rows // B
    part = B // parts
    return pl.pallas_call(
        pick_kernel,
        grid_spec=pltpu.PrefetchScalarGridSpec(
            num_scalar_prefetch=1,
            grid=(2, blocks // 2),
            in_specs=[pl.BlockSpec((2 * B, B), lambda j, b, slots: (b, slots[j]))],
            out_specs=pl.BlockSpec((parts, 2, part, B), lambda j, b, slots: (0, b, 0, j)),
        ),
        out_shape=jax.ShapeDtypeStruct((parts, blocks, part, 2 * B), F32),
    )(slots, covariance)


def lanes(tile, j):
    return jnp.broadcast_to(tile[:, j : j + 1], (8, 128))


def eliminate(tiles):
    sub = lax.broadcasted_iota(jnp.int32, (8, 128), 0)
    scales = []
    for t in range(8):
        own = tiles[t]
        cols = [lanes(own, 8 * t + j) for j in range(8)]
        inv, cross = [], {}
        pivots = jnp.ones((8, 128), F32)
        for j in range(8):
            pivot = jnp.broadcast_to(cols[j][j : j + 1, :], (8, 128))
            pivots = jnp.where(sub == j, pivot, pivots)
            r = 1.0 / pivot
            inv.append(r)
            if j == 7:
                break
            m = jnp.where(sub > j, cols[j] * r, 0.0)
            for k in range(j + 1, 8):
                cross[j, k] = jnp.broadcast_to(cols[k][j : j + 1, :], (8, 128))
                cols[k] = cols[k] - m * cross[j, k]
            own = own - m * jnp.broadcast_to(own[j : j + 1, :], (8, 128))
        tiles[t] = own
        scales.append(lax.rsqrt(pivots))
        rows = [jnp.broadcast_to(own[j : j + 1, :], (8, 128)) for j in range(8)]
        for i in range(t + 1, 8):
            low = tiles[i]
            cols = [lanes(low, 8 * t + j) for j in range(8)]
            for j in range(8):
                m = cols[j] * inv[j]
                for k in range(j + 1, 8):
                    cols[k] = cols[k] - m * cross[j, k]
                low = low - m * rows[j]
            tiles[i] = low
    return tiles, scales


def factor_block(work, small, inverse_small):
    for b in range(B // S):
        lo, hi = b * S, (b + 1) * S
        small[:, 0:S] = work[lo:hi, lo:hi]
        row = lax.broadcasted_iota(jnp.int32, (S, S), 0)
        col = lax.broadcasted_iota(jnp.int32, (S, S), 1)
        small[:, S : 2 * S] = jnp.where(row == col, 1.0, 0.0)
        tiles, scales = eliminate([small[8 * i : 8 * i + 8, :] for i in range(8)])
        for i in range(8):
            small[8 * i : 8 * i + 8, :] = tiles[i] * scales[i]
        inverse_small[...] = small[:, S : 2 * S]
        top = dot(inverse_small[...], work[lo:hi, :], NN, HIGH)
        work[lo:hi, :] = top
        if hi < B:
            work[hi:B, :] = work[hi:B, :] - dot(top[:, hi:B], top, TN, HIGH)


def split(a):
    high = a.astype(BF16)
    rest = a - high.astype(F32)
    middle = rest.astype(BF16)
    return high, middle, (rest - middle.astype(F32)).astype(BF16)


def write_left(ref, a):
    high, middle, low = split(a)
    for n, term in enumerate((high, high, middle, high, low, middle)):
        ref[:, n * B : (n + 1) * B] = term


def write_right(ref, start, a):
    high, middle, low = split(a)
    for n, term in enumerate((high, middle, high, low, high, middle)):
        ref[:, start + n * B : start + (n + 1) * B] = term


def factor_kernel(diag_ref, inverse_ref, l10t_ref, lower_ref, work, small, inverse_small):
    row = lax.broadcasted_iota(jnp.int32, (B, B), 0)
    col = lax.broadcasted_iota(jnp.int32, (B, B), 1)
    eye = jnp.where(row == col, 1.0, 0.0)
    work[:, 0:B] = diag_ref[:, 0:B]
    work[:, B : 2 * B] = eye
    factor_block(work, small, inverse_small)
    x0 = work[:, B : 2 * B]
    write_right(inverse_ref, 0, x0)
    lower_ref[:, 0:B] = jnp.where(row <= col, work[:, 0:B], 0.0).T
    l10t = dot(x0, diag_ref[:, B : 2 * B], NN, HIGH).astype(BF16)
    l10t_ref[...] = l10t
    work[:, 0:B] = diag_ref[:, 2 * B : 3 * B] - dot(l10t, l10t, TN)
    work[:, B : 2 * B] = eye
    factor_block(work, small, inverse_small)
    write_right(inverse_ref, 6 * B, work[:, B : 2 * B])
    lower_ref[:, B : 2 * B] = jnp.where(row <= col, work[:, 0:B], 0.0).T


def factor_diagonal(diag):
    return pl.pallas_call(
        factor_kernel,
        in_specs=[VMEM_SPEC],
        out_specs=[VMEM_SPEC] * 3,
        out_shape=[
            jax.ShapeDtypeStruct((B, 12 * B), BF16),
            jax.ShapeDtypeStruct((B, B), BF16),
            jax.ShapeDtypeStruct((B, 2 * B), F32),
        ],
        scratch_shapes=[pltpu.VMEM((B, 2 * B), F32), pltpu.VMEM((S, 2 * S), F32), pltpu.VMEM((S, S), F32)],
        compiler_params=pltpu.CompilerParams(vmem_limit_bytes=VMEM_BYTES),
        cost_estimate=pl.CostEstimate(flops=2 * 10**10, bytes_accessed=80_000_000, transcendentals=0),
    )(diag)


def solve_rows(first, second, wide, inverse_ref, l10t_ref):
    write_left(wide, first)
    p0 = dot(wide[...], inverse_ref[:, 0 : 6 * B], NT)
    write_left(wide, second - dot(p0.astype(BF16), l10t_ref[...], NN))
    p1 = dot(wide[...], inverse_ref[:, 6 * B : 12 * B], NT)
    return p0, p1


def across_kernel(flags, across_ref, inverse_ref, l10t_ref, pc_ref, white_ref, raw, wide, wide_white):
    k = pl.program_id(0)
    part = pc_ref.shape[3]
    blocks = pc_ref.shape[1]
    held = blocks * part
    half = raw.shape[0] // 2
    fold = half // 2

    p0, p1 = solve_rows(
        across_ref[:, 0:held, 0:B].reshape(4 * held, B),
        across_ref[:, 0:held, B : 2 * B].reshape(4 * held, B),
        wide,
        inverse_ref,
        l10t_ref,
    )
    p0, p1 = p0.astype(BF16), p1.astype(BF16)
    for n in range(4):
        h, parity = n // 2, n % 2
        for b in range(blocks):
            here = slice(n * held + b * part, n * held + (b + 1) * part)
            level = flags[8 + parity * blocks + b]
            pc_ref[parity, b, h, :, 0:B] = jnp.where(level > 0, p0[here], jnp.zeros_like(p0[here]))
            pc_ref[parity, b, h, :, B : 2 * B] = jnp.where(level > 1, p1[here], jnp.zeros_like(p1[here]))

    for panel in range(2):

        @pl.when(k == flags[6 + panel])
        def _():
            for n in range(4):
                h, parity = n // 2, n % 2
                for f in range(2):
                    lane = (2 * f + panel) * 128
                    raw[
                        parity * half + f * fold : parity * half + (f + 1) * fold,
                        panel * B + h * 128 : panel * B + (h + 1) * 128,
                    ] = across_ref[n, held : held + fold, lane : lane + 128]

    @pl.when(k == pl.num_programs(0) - 1)
    def _():
        w0, w1 = solve_rows(raw[:, 0:B], raw[:, B : 2 * B], wide_white, inverse_ref, l10t_ref)
        white_ref[:, 0:B] = w0
        white_ref[:, B : 2 * B] = w1


def whole(*shape):
    return pl.BlockSpec(shape, lambda i, flags: (0,) * len(shape))


def solve_across(flags, across, inverse, l10t, blocks, parts, particles):
    part = B // parts
    steps = across.shape[0] // 4
    return pl.pallas_call(
        across_kernel,
        grid_spec=pltpu.PrefetchScalarGridSpec(
            num_scalar_prefetch=1,
            grid=(steps,),
            in_specs=[
                pl.BlockSpec((4,) + across.shape[1:], lambda k, flags: (k, 0, 0)),
                whole(*inverse.shape),
                whole(*l10t.shape),
            ],
            out_specs=[
                pl.BlockSpec(
                    (2, blocks, 2, part, 2 * B), lambda k, flags: (0, 0, lax.rem(k + steps - flags[0], steps), 0, 0)
                ),
                whole(particles, 2 * B),
            ],
            scratch_shapes=[
                pltpu.VMEM((particles, 2 * B), F32),
                pltpu.VMEM((4 * blocks * part, 6 * B), BF16),
                pltpu.VMEM((particles, 6 * B), BF16),
            ],
        ),
        out_shape=[
            jax.ShapeDtypeStruct((2, blocks, parts, part, 2 * B), BF16),
            jax.ShapeDtypeStruct((particles, 2 * B), F32),
        ],
        compiler_params=pltpu.CompilerParams(vmem_limit_bytes=VMEM_BYTES),
        cost_estimate=pl.CostEstimate(flops=6 * 10**9, bytes_accessed=8_000_000, transcendentals=0),
    )(flags, across, inverse, l10t)


def update_kernel(
    flags, cov_ref, along_ref, pc_ref, relaid_ref, white_ref, inverse_ref, l10t_ref, lower_ref, out_ref, solved_ref, wide
):
    i = pl.program_id(0)
    parts, part = along_ref.shape[0], along_ref.shape[2]
    column_blocks = pc_ref.shape[0] // B
    fold = relaid_ref.shape[1]

    level = flags[16 + i]
    raw = along_ref[:, 0].reshape(parts * part, 2 * B)
    p0, p1 = solve_rows(raw[:, 0:B], raw[:, B : 2 * B], wide, inverse_ref, l10t_ref)
    p0 = jnp.where(level > 0, p0, 0.0)
    p1 = jnp.where(level > 1, p1, 0.0)
    rows = jnp.concatenate([p0.astype(BF16), p1.astype(BF16)], axis=1)
    for n in range(column_blocks):
        cut = slice(n * B, (n + 1) * B)
        out_ref[:, cut] = cov_ref[:, cut] - dot(rows, pc_ref[cut, :], NT)

    for panel, solved in ((0, p0), (1, p1)):
        is_row = i == flags[2 + panel]
        for n in range(column_blocks):

            @pl.when(is_row & (flags[8 + n] > panel))
            def _():
                out_ref[:, n * B : (n + 1) * B] = jnp.zeros((B, B), F32)

        column = flags[4 + panel]
        place = pl.ds(pl.multiple_of(jnp.maximum(column, 0) * B, B), B)

        @pl.when((column >= 0) & (level > panel))
        def _():
            out_ref[:, place] = solved

        @pl.when((column >= 0) & is_row)
        def _():
            out_ref[:, place] = lower_ref[:, panel * B : (panel + 1) * B]

    product = dot(white_ref[...].astype(BF16), rows, NT)
    for n in range(4):
        h, parity = n // 2, n % 2
        for f in range(4):
            top = parity * 4 * fold + f * fold
            there = (slice(top, top + fold), slice(h * 128, (h + 1) * 128))
            solved_ref[there] = relaid_ref[n, :, f * 128 : (f + 1) * 128] - product[there]
    for panel in range(2):

        @pl.when(i == flags[2 + panel])
        def _():
            solved_ref[...] = white_ref[:, panel * B : (panel + 1) * B]


def update(flags, covariance, along, pc, exchanged, white, inverse, l10t, lower):
    rows, columns = covariance.shape
    blocks = rows // B
    parts = along.shape[0]
    part = B // parts
    particles = white.shape[0]
    fold = particles // 8
    below = exchanged.shape[1] // fold - 1
    return pl.pallas_call(
        update_kernel,
        grid_spec=pltpu.PrefetchScalarGridSpec(
            num_scalar_prefetch=1,
            grid=(blocks,),
            in_specs=[
                pl.BlockSpec((B, columns), lambda i, flags: (i, 0)),
                pl.BlockSpec((parts, 1, part, 2 * B), lambda i, flags: (0, i, 0, 0)),
                whole(*pc.shape),
                pl.BlockSpec((4, fold, 2 * B), lambda i, flags: (lax.rem(i + flags[0], blocks), below, 0)),
                whole(*white.shape),
                whole(*inverse.shape),
                whole(*l10t.shape),
                whole(*lower.shape),
            ],
            out_specs=[
                pl.BlockSpec((B, columns), lambda i, flags: (i, 0)),
                pl.BlockSpec((particles, B), lambda i, flags: (0, i)),
            ],
            scratch_shapes=[pltpu.VMEM((B, 6 * B), BF16)],
        ),
        out_shape=[jax.ShapeDtypeStruct((rows, columns), F32), jax.ShapeDtypeStruct((particles, rows), F32)],
        compiler_params=pltpu.CompilerParams(vmem_limit_bytes=VMEM_BYTES),
        cost_estimate=pl.CostEstimate(flops=5 * 10**9, bytes_accessed=20_000_000, transcendentals=0),
    )(flags, covariance, along, pc, exchanged, white, inverse, l10t, lower)


def per_device(covariance, innovations, block_owner, panel_index, *, n_row, n_col):
    local_rows, local_cols = covariance.shape
    row_blocks, column_blocks = local_rows // B, local_cols // B
    r, c = lax.axis_index("row"), lax.axis_index("col")
    targets = panel_index[0] + jnp.arange(2, dtype=jnp.int32)
    positions = jnp.arange(block_owner.shape[0], dtype=jnp.int32)
    slot = jnp.sum(jnp.where(block_owner[None, :] == targets[:, None], positions[None, :], 0), axis=1)
    row_root, column_root = slot // row_blocks, slot // column_blocks
    row_slot, column_slot = slot % row_blocks, slot % column_blocks
    levels = jnp.sum((block_owner[:, None] > targets[None, :]).astype(jnp.int32), axis=1)
    steps = n_row // 4
    shift = c // 2
    flags = jnp.concatenate(
        [
            jnp.full((2,), shift, jnp.int32),
            jnp.where(row_root == r, row_slot, -1),
            jnp.where(column_root == c, column_slot, -1),
            (row_slot + shift) % steps,
            lax.dynamic_slice_in_dim(levels, c * column_blocks, column_blocks),
            lax.dynamic_slice_in_dim(levels, r * row_blocks, row_blocks),
        ]
    ).astype(jnp.int32)
    across_axes = [
        (a * n_col + b, ((b // 2 + a // 4) % steps * 4 + b % 2 * 2 + a % 2) * n_col + a // 2)
        for a in range(n_row)
        for b in range(n_col)
    ]

    turned = lax.ppermute(jnp.transpose(innovations, (1, 0, 2)), ("row", "col"), across_axes)

    picked = pick_columns(column_slot.astype(jnp.int32), covariance, n_col)
    parts = lax.all_to_all(picked, "col", split_axis=0, concat_axis=0, tiled=True)
    part = parts.shape[2]
    piece = jnp.concatenate(
        [
            lax.dynamic_slice(parts, (column_root[n], 0, 0, n * B), (1, row_blocks, part, B))[0]
            for n in range(2)
        ],
        axis=-1,
    )

    chosen = jnp.where(r == row_root[0], row_slot[0], row_slot[1])
    mine = lax.dynamic_index_in_dim(piece, chosen, 0, keepdims=False)
    fold = turned.shape[1] // 4
    groups = jnp.concatenate([turned[:, f * fold : (f + 1) * fold] for f in range(4)], axis=2)
    sent = jnp.concatenate([jnp.broadcast_to(mine[None], (n_row,) + mine.shape), groups], axis=1)
    exchanged = lax.all_to_all(sent, "row", split_axis=0, concat_axis=0, tiled=True)
    upper = lax.dynamic_slice(exchanged, (row_root[0], 0, 0), (1, part, 2 * B))[0]
    lower = lax.dynamic_slice(exchanged, (row_root[1], 0, B), (1, part, B))[0]
    strip = jnp.concatenate([upper, lower], axis=-1)
    diag = lax.all_to_all(
        jnp.broadcast_to(strip[None], (n_col,) + strip.shape), "col", split_axis=0, concat_axis=0, tiled=True
    ).reshape(B, 3 * B)

    tiled = lax.ppermute(piece.reshape(row_blocks * part, 2 * B), ("row", "col"), across_axes)
    wanted = [lax.dynamic_index_in_dim(turned, row_root[n], 0, keepdims=False) for n in range(2)]
    wanted = jnp.concatenate(
        [w[h * 2 * fold : (h + 1) * 2 * fold] for h in range(2) for w in wanted], axis=1
    )
    payload, _ = lax.optimization_barrier((jnp.concatenate([tiled, wanted], axis=0), exchanged))
    across = lax.all_gather(payload, "row", axis=0)

    inverse, l10t, lower = factor_diagonal(diag)

    along = lax.all_to_all(
        jnp.broadcast_to(piece[None], (n_col,) + piece.shape), "col", split_axis=0, concat_axis=0, tiled=True
    )

    pc, white = solve_across(flags, across, inverse, l10t, row_blocks, n_col, 2 * turned.shape[1])
    return update(
        flags, covariance, along, pc.reshape(local_cols, 2 * B), exchanged, white, inverse, l10t, lower
    )


def solution(mesh):
    placed = (P("row", "col"), P("row", None, "col"), P(), P())
    return jax.shard_map(
        functools.partial(per_device, n_row=mesh.shape["row"], n_col=mesh.shape["col"]),
        mesh=mesh,
        in_specs=placed,
        out_specs=(P("row", "col"), P("col", "row")),
        check_vma=False,
    )
```

```python
import functools

import jax
import jax.numpy as jnp
from jax import lax
from jax.experimental import pallas as pl
from jax.experimental.pallas import tpu as pltpu
from jax.sharding import PartitionSpec as P

B = 256
S = 64
VMEM_BYTES = 60 * 1024 * 1024
F32 = jnp.float32
BF16 = jnp.bfloat16
HIGH = lax.Precision.HIGHEST
VMEM_SPEC = pl.BlockSpec(memory_space=pltpu.VMEM)
SMEM_SPEC = pl.BlockSpec(memory_space=pltpu.SMEM)


def dot(a, b, dims, precision=None):
    return lax.dot_general(a, b, (dims, ((), ())), precision=precision, preferred_element_type=F32)


NN = ((1,), (0,))
NT = ((1,), (1,))
TN = ((0,), (0,))


def pick_kernel(slots, cov_ref, out_ref):
    parts, blocks, part, width = out_ref.shape
    for b in range(blocks):
        out_ref[:, b] = cov_ref[b * B : (b + 1) * B, :].reshape(parts, part, width)


def pick_columns(slots, covariance, parts):
    rows = covariance.shape[0]
    blocks = rows // B
    part = B // parts
    return pl.pallas_call(
        pick_kernel,
        grid_spec=pltpu.PrefetchScalarGridSpec(
            num_scalar_prefetch=1,
            grid=(2, blocks // 2),
            in_specs=[pl.BlockSpec((2 * B, B), lambda j, b, slots: (b, slots[j]))],
            out_specs=pl.BlockSpec((parts, 2, part, B), lambda j, b, slots: (0, b, 0, j)),
        ),
        out_shape=jax.ShapeDtypeStruct((parts, blocks, part, 2 * B), F32),
    )(slots, covariance)


def lanes(tile, j):
    return jnp.broadcast_to(tile[:, j : j + 1], (8, 128))


def eliminate(tiles):
    sub = lax.broadcasted_iota(jnp.int32, (8, 128), 0)
    scales = []
    for t in range(8):
        own = tiles[t]
        cols = [lanes(own, 8 * t + j) for j in range(8)]
        inv, cross = [], {}
        pivots = jnp.ones((8, 128), F32)
        for j in range(8):
            pivot = jnp.broadcast_to(cols[j][j : j + 1, :], (8, 128))
            pivots = jnp.where(sub == j, pivot, pivots)
            r = 1.0 / pivot
            inv.append(r)
            if j == 7:
                break
            m = jnp.where(sub > j, cols[j] * r, 0.0)
            for k in range(j + 1, 8):
                cross[j, k] = jnp.broadcast_to(cols[k][j : j + 1, :], (8, 128))
                cols[k] = cols[k] - m * cross[j, k]
            own = own - m * jnp.broadcast_to(own[j : j + 1, :], (8, 128))
        tiles[t] = own
        scales.append(lax.rsqrt(pivots))
        rows = [jnp.broadcast_to(own[j : j + 1, :], (8, 128)) for j in range(8)]
        for i in range(t + 1, 8):
            low = tiles[i]
            cols = [lanes(low, 8 * t + j) for j in range(8)]
            for j in range(8):
                m = cols[j] * inv[j]
                for k in range(j + 1, 8):
                    cols[k] = cols[k] - m * cross[j, k]
                low = low - m * rows[j]
            tiles[i] = low
    return tiles, scales


def factor_block(work, small, inverse_small):
    for b in range(B // S):
        lo, hi = b * S, (b + 1) * S
        small[:, 0:S] = work[lo:hi, lo:hi]
        row = lax.broadcasted_iota(jnp.int32, (S, S), 0)
        col = lax.broadcasted_iota(jnp.int32, (S, S), 1)
        small[:, S : 2 * S] = jnp.where(row == col, 1.0, 0.0)
        tiles, scales = eliminate([small[8 * i : 8 * i + 8, :] for i in range(8)])
        for i in range(8):
            small[8 * i : 8 * i + 8, :] = tiles[i] * scales[i]
        inverse_small[...] = small[:, S : 2 * S]
        top = dot(inverse_small[...], work[lo:hi, :], NN, HIGH)
        work[lo:hi, :] = top
        if hi < B:
            work[hi:B, :] = work[hi:B, :] - dot(top[:, hi:B], top, TN, HIGH)


def split(a):
    high = a.astype(BF16)
    rest = a - high.astype(F32)
    middle = rest.astype(BF16)
    return high, middle, (rest - middle.astype(F32)).astype(BF16)


def write_left(ref, a):
    high, middle, low = split(a)
    for n, term in enumerate((high, high, middle, high, low, middle)):
        ref[:, n * B : (n + 1) * B] = term


def write_right(ref, start, a):
    high, middle, low = split(a)
    for n, term in enumerate((high, middle, high, low, high, middle)):
        ref[:, start + n * B : start + (n + 1) * B] = term


def factor_kernel(flags, near_ref, far_ref, inverse_ref, l10t_ref, lower_ref, diag_ref, work, small, inverse_small):
    parts, part = near_ref.shape[:2]
    for ref, first in ((near_ref, flags[1] * part), (far_ref, (1 - flags[1]) * part)):
        for q in range(parts):
            diag_ref[pl.ds(pl.multiple_of(q * 2 * part + first, part), part), :] = ref[q]
    row = lax.broadcasted_iota(jnp.int32, (B, B), 0)
    col = lax.broadcasted_iota(jnp.int32, (B, B), 1)
    eye = jnp.where(row == col, 1.0, 0.0)
    work[:, 0:B] = diag_ref[:, 0:B]
    work[:, B : 2 * B] = eye
    factor_block(work, small, inverse_small)
    x0 = work[:, B : 2 * B]
    write_right(inverse_ref, 0, x0)
    lower_ref[:, 0:B] = jnp.where(row <= col, work[:, 0:B], 0.0).T
    l10t = dot(x0, diag_ref[:, B : 2 * B], NN, HIGH).astype(BF16)
    l10t_ref[...] = l10t
    work[:, 0:B] = diag_ref[:, 2 * B : 3 * B] - dot(l10t, l10t, TN)
    work[:, B : 2 * B] = eye
    factor_block(work, small, inverse_small)
    write_right(inverse_ref, 6 * B, work[:, B : 2 * B])
    lower_ref[:, B : 2 * B] = jnp.where(row <= col, work[:, 0:B], 0.0).T


def factor_diagonal(flags, near, far):
    return pl.pallas_call(
        factor_kernel,
        in_specs=[SMEM_SPEC] + [VMEM_SPEC] * 2,
        out_specs=[VMEM_SPEC] * 3,
        out_shape=[
            jax.ShapeDtypeStruct((B, 12 * B), BF16),
            jax.ShapeDtypeStruct((B, B), BF16),
            jax.ShapeDtypeStruct((B, 2 * B), F32),
        ],
        scratch_shapes=[
            pltpu.VMEM((B, 3 * B), F32),
            pltpu.VMEM((B, 2 * B), F32),
            pltpu.VMEM((S, 2 * S), F32),
            pltpu.VMEM((S, S), F32),
        ],
        compiler_params=pltpu.CompilerParams(vmem_limit_bytes=VMEM_BYTES),
        cost_estimate=pl.CostEstimate(flops=2 * 10**10, bytes_accessed=80_000_000, transcendentals=0),
    )(flags, near, far)


def solve_rows(first, second, wide, inverse_ref, l10t_ref):
    write_left(wide, first)
    p0 = dot(wide[...], inverse_ref[:, 0 : 6 * B], NT)
    write_left(wide, second - dot(p0.astype(BF16), l10t_ref[...], NN))
    p1 = dot(wide[...], inverse_ref[:, 6 * B : 12 * B], NT)
    return p0, p1


def across_kernel(flags, across_ref, inverse_ref, l10t_ref, pc_ref, white_ref, raw, wide, wide_white):
    blocks, parts, part = pc_ref.shape[:3]
    held = blocks * part
    half = raw.shape[0]
    fold = half // 2
    steps = parts // 2

    for k in range(steps):
        two = slice(2 * k, 2 * k + 2)
        p0, p1 = solve_rows(
            across_ref[two, 0:held, 0:B].reshape(2 * held, B),
            across_ref[two, 0:held, B : 2 * B].reshape(2 * held, B),
            wide.at[k],
            inverse_ref,
            l10t_ref,
        )
        p0, p1 = p0.astype(BF16), p1.astype(BF16)
        for h in range(2):
            q = lax.rem(k + steps - flags[0], steps) * 2 + h
            for b in range(blocks):
                here = slice(h * held + b * part, h * held + (b + 1) * part)
                level = flags[8 + flags[1] * blocks + b]
                pc_ref[b, q, :, 0:B] = jnp.where(level > 0, p0[here], jnp.zeros_like(p0[here]))
                pc_ref[b, q, :, B : 2 * B] = jnp.where(level > 1, p1[here], jnp.zeros_like(p1[here]))

    for panel in range(2):
        for h in range(2):
            for f in range(2):
                lane = (2 * f + panel) * 128
                raw[f * fold : (f + 1) * fold, panel * B + h * 128 : panel * B + (h + 1) * 128] = across_ref[
                    2 * flags[6 + panel] + h, held : held + fold, lane : lane + 128
                ]
    w0, w1 = solve_rows(raw[:, 0:B], raw[:, B : 2 * B], wide_white, inverse_ref, l10t_ref)
    white_ref[:, 0:B] = w0
    white_ref[:, B : 2 * B] = w1


def solve_across(flags, across, inverse, l10t, blocks, particles):
    parts = across.shape[0]
    part = B // parts
    return pl.pallas_call(
        across_kernel,
        in_specs=[SMEM_SPEC] + [VMEM_SPEC] * 3,
        out_specs=[VMEM_SPEC] * 2,
        scratch_shapes=[
            pltpu.VMEM((particles, 2 * B), F32),
            pltpu.VMEM((parts // 2, 2 * blocks * part, 6 * B), BF16),
            pltpu.VMEM((particles, 6 * B), BF16),
        ],
        out_shape=[
            jax.ShapeDtypeStruct((blocks, parts, part, 2 * B), BF16),
            jax.ShapeDtypeStruct((particles, 2 * B), F32),
        ],
        compiler_params=pltpu.CompilerParams(vmem_limit_bytes=VMEM_BYTES),
        cost_estimate=pl.CostEstimate(flops=3 * 10**9, bytes_accessed=4_000_000, transcendentals=0),
    )(flags, across, inverse, l10t)


def whole(*shape):
    return pl.BlockSpec(shape, lambda i, flags: (0,) * len(shape))


def update_kernel(
    flags,
    cov_ref,
    along_ref,
    near_ref,
    far_ref,
    relaid_ref,
    near_white_ref,
    far_white_ref,
    inverse_ref,
    l10t_ref,
    lower_ref,
    out_ref,
    solved_ref,
    panels,
    rows,
    wide,
):
    i = pl.program_id(0)
    parts, blocks, part = along_ref.shape[:3]
    column_blocks = 2 * near_ref.shape[0] // B
    half = relaid_ref.shape[1]

    @pl.when(i == 0)
    def _():
        for b in range(blocks):
            raw = along_ref[:, b].reshape(parts * part, 2 * B)
            p0, p1 = solve_rows(raw[:, 0:B], raw[:, B : 2 * B], wide.at[b], inverse_ref, l10t_ref)
            for panel, p in ((0, p0), (1, p1)):
                p = jnp.where(flags[16 + b] > panel, p, 0.0)
                panels[b, :, panel * B : (panel + 1) * B] = p
                rows[b, :, panel * B : (panel + 1) * B] = p.astype(BF16)

    level = flags[16 + i]
    own = rows[i]
    for side, ref in ((flags[1], near_ref), (1 - flags[1], far_ref)):
        for n in range(column_blocks // 2):
            place = pl.ds(pl.multiple_of((side * (column_blocks // 2) + n) * B, B), B)
            out_ref[:, place] = cov_ref[:, place] - dot(own, ref[n * B : (n + 1) * B, :], NT)

    for panel in range(2):
        is_row = i == flags[2 + panel]
        for n in range(column_blocks):

            @pl.when(is_row & (flags[8 + n] > panel))
            def _():
                out_ref[:, n * B : (n + 1) * B] = jnp.zeros((B, B), F32)

        column = flags[4 + panel]
        place = pl.ds(pl.multiple_of(jnp.maximum(column, 0) * B, B), B)

        @pl.when((column >= 0) & (level > panel))
        def _():
            out_ref[:, place] = panels[i, :, panel * B : (panel + 1) * B]

        @pl.when((column >= 0) & is_row)
        def _():
            out_ref[:, place] = lower_ref[:, panel * B : (panel + 1) * B]

    for side, ref in ((flags[1], near_white_ref), (1 - flags[1], far_white_ref)):
        place = pl.ds(pl.multiple_of(side * half, half), half)
        product = dot(ref[...].astype(BF16), own, NT)
        for h in range(2):
            cut = slice(h * 128, (h + 1) * 128)
            solved_ref[place, cut] = relaid_ref[2 * h + side] - product[:, cut]
        for panel in range(2):

            @pl.when(i == flags[2 + panel])
            def _():
                solved_ref[place, :] = ref[:, panel * B : (panel + 1) * B]


def update(flags, covariance, along, near, far, relaid, near_white, far_white, inverse, l10t, lower):
    rows, columns = covariance.shape
    blocks = rows // B
    half = relaid.shape[1]
    return pl.pallas_call(
        update_kernel,
        grid_spec=pltpu.PrefetchScalarGridSpec(
            num_scalar_prefetch=1,
            grid=(blocks,),
            in_specs=[
                pl.BlockSpec((B, columns), lambda i, flags: (i, 0)),
                whole(*along.shape),
                whole(*near.shape),
                whole(*far.shape),
                pl.BlockSpec((4, half, 128), lambda i, flags: (lax.rem(i + flags[0], blocks), 0, 0)),
                whole(*near_white.shape),
                whole(*far_white.shape),
                whole(*inverse.shape),
                whole(*l10t.shape),
                whole(*lower.shape),
            ],
            out_specs=[
                pl.BlockSpec((B, columns), lambda i, flags: (i, 0)),
                pl.BlockSpec((2 * half, B), lambda i, flags: (0, i)),
            ],
            scratch_shapes=[
                pltpu.VMEM((blocks, B, 2 * B), F32),
                pltpu.VMEM((blocks, B, 2 * B), BF16),
                pltpu.VMEM((blocks, B, 6 * B), BF16),
            ],
        ),
        out_shape=[jax.ShapeDtypeStruct((rows, columns), F32), jax.ShapeDtypeStruct((2 * half, rows), F32)],
        compiler_params=pltpu.CompilerParams(vmem_limit_bytes=VMEM_BYTES),
        cost_estimate=pl.CostEstimate(flops=5 * 10**9, bytes_accessed=20_000_000, transcendentals=0),
    )(flags, covariance, along, near, far, relaid, near_white, far_white, inverse, l10t, lower)


def per_device(covariance, innovations, block_owner, panel_index, *, n_row, n_col):
    local_rows, local_cols = covariance.shape
    row_blocks, column_blocks = local_rows // B, local_cols // B
    r, c = lax.axis_index("row"), lax.axis_index("col")
    targets = panel_index[0] + jnp.arange(2, dtype=jnp.int32)
    positions = jnp.arange(block_owner.shape[0], dtype=jnp.int32)
    slot = jnp.sum(jnp.where(block_owner[None, :] == targets[:, None], positions[None, :], 0), axis=1)
    row_root, column_root = slot // row_blocks, slot // column_blocks
    row_slot, column_slot = slot % row_blocks, slot % column_blocks
    levels = jnp.sum((block_owner[:, None] > targets[None, :]).astype(jnp.int32), axis=1)
    steps = n_row // 4
    shift, core = c // 2, r % 2
    pairs = [(a, a ^ 1) for a in range(n_row)]
    same_core = [[a for a in range(n_row) if a % 2 == k] for k in range(2)]
    flags = jnp.concatenate(
        [
            shift[None],
            core[None],
            jnp.where(row_root == r, row_slot, -1),
            jnp.where(column_root == c, column_slot, -1),
            (row_slot + shift) % steps,
            lax.dynamic_slice_in_dim(levels, c * column_blocks, column_blocks),
            lax.dynamic_slice_in_dim(levels, r * row_blocks, row_blocks),
        ]
    ).astype(jnp.int32)
    across_axes = [
        (a * n_col + b, ((b // 2 + a // 4) % steps * 4 + b % 2 * 2 + a % 2) * n_col + a // 2)
        for a in range(n_row)
        for b in range(n_col)
    ]

    picked = pick_columns(column_slot.astype(jnp.int32), covariance, n_col)
    parts = lax.all_to_all(picked, "col", split_axis=0, concat_axis=0, tiled=True)
    part = parts.shape[2]
    piece = jnp.concatenate(
        [
            lax.dynamic_slice(parts, (column_root[n], 0, 0, n * B), (1, row_blocks, part, B))[0]
            for n in range(2)
        ],
        axis=-1,
    )

    chosen = jnp.where(r == row_root[0], row_slot[0], row_slot[1])
    mine = lax.dynamic_index_in_dim(piece, chosen, 0, keepdims=False)
    half = part // 2
    kept = lax.dynamic_slice_in_dim(mine, core * half, half, 0)
    given = lax.ppermute(lax.dynamic_slice_in_dim(mine, (1 - core) * half, half, 0), "row", pairs)
    both = jnp.concatenate([jnp.where(core == 0, kept, given), jnp.where(core == 0, given, kept)], axis=0)

    fold = innovations.shape[0] // 2
    wanted = [lax.dynamic_index_in_dim(innovations, row_root[n], 1, keepdims=False) for n in range(2)]
    wanted = jnp.concatenate([w[h * fold : (h + 1) * fold] for h in range(2) for w in wanted], axis=1)
    payload = jnp.concatenate([piece.reshape(row_blocks * part, 2 * B), wanted], axis=0)
    payload, both = lax.optimization_barrier((payload, both))
    payload = lax.ppermute(payload, ("row", "col"), across_axes)

    spread = lax.all_to_all(
        jnp.broadcast_to(both[None], (n_row // 2,) + both.shape),
        "row",
        split_axis=0,
        concat_axis=0,
        tiled=True,
        axis_index_groups=same_core,
    )
    upper = lax.dynamic_slice(spread, (row_root[0] // 2, row_root[0] % 2 * half, 0), (1, half, 2 * B))[0]
    lower = lax.dynamic_slice(spread, (row_root[1] // 2, row_root[1] % 2 * half, B), (1, half, B))[0]
    strip = jnp.concatenate([upper, lower], axis=-1)
    near = lax.all_to_all(
        jnp.broadcast_to(strip[None], (n_col,) + strip.shape), "col", split_axis=0, concat_axis=0, tiled=True
    )
    far = lax.ppermute(near, "row", pairs)

    payload, _ = lax.optimization_barrier((payload, spread))
    across = lax.all_gather(payload, "row", axis=0, axis_index_groups=same_core)

    inverse, l10t, lower = factor_diagonal(flags, near, far)

    along = lax.all_to_all(
        jnp.broadcast_to(piece[None], (n_col,) + piece.shape), "col", split_axis=0, concat_axis=0, tiled=True
    )

    groups, _ = lax.optimization_barrier((jnp.transpose(innovations, (1, 0, 2)), near))
    turned = lax.ppermute(groups, ("row", "col"), across_axes)
    across, turned = lax.optimization_barrier((across, turned))
    turned, _ = lax.optimization_barrier((turned, along))
    relaid = lax.all_to_all(turned, "row", split_axis=0, concat_axis=0, tiled=True)

    near_rows, near_white = solve_across(flags, across, inverse, l10t, row_blocks, innovations.shape[0])
    near_rows = near_rows.reshape(local_cols // 2, 2 * B)
    far_rows, far_white = lax.ppermute(near_rows, "row", pairs), lax.ppermute(near_white, "row", pairs)
    return update(
        flags, covariance, along, near_rows, far_rows, relaid, near_white, far_white, inverse, l10t, lower
    )


def solution(mesh):
    placed = (P("row", "col"), P("row", None, "col"), P(), P())
    return jax.shard_map(
        functools.partial(per_device, n_row=mesh.shape["row"], n_col=mesh.shape["col"]),
        mesh=mesh,
        in_specs=placed,
        out_specs=(P("row", "col"), P("col", "row")),
        check_vma=False,
    )
```

```python
import functools

import jax
import jax.numpy as jnp
from jax import lax
from jax.experimental import pallas as pl
from jax.experimental.pallas import tpu as pltpu
from jax.sharding import PartitionSpec as P

B = 256
S = 64
VMEM_BYTES = 60 * 1024 * 1024
F32 = jnp.float32
BF16 = jnp.bfloat16
HIGH = lax.Precision.HIGHEST
VMEM_SPEC = pl.BlockSpec(memory_space=pltpu.VMEM)
SMEM_SPEC = pl.BlockSpec(memory_space=pltpu.SMEM)


def dot(a, b, dims, precision=None):
    return lax.dot_general(a, b, (dims, ((), ())), precision=precision, preferred_element_type=F32)


NN = ((1,), (0,))
NT = ((1,), (1,))
TN = ((0,), (0,))


def pick_kernel(slots, cov_ref, out_ref):
    parts, blocks, part, width = out_ref.shape
    for b in range(blocks):
        out_ref[:, b] = cov_ref[b * B : (b + 1) * B, :].reshape(parts, part, width)


def pick_columns(slots, covariance, parts):
    rows = covariance.shape[0]
    blocks = rows // B
    part = B // parts
    return pl.pallas_call(
        pick_kernel,
        grid_spec=pltpu.PrefetchScalarGridSpec(
            num_scalar_prefetch=1,
            grid=(2, blocks // 2),
            in_specs=[pl.BlockSpec((2 * B, B), lambda j, b, slots: (b, slots[j]))],
            out_specs=pl.BlockSpec((parts, 2, part, B), lambda j, b, slots: (0, b, 0, j)),
        ),
        out_shape=jax.ShapeDtypeStruct((parts, blocks, part, 2 * B), F32),
    )(slots, covariance)


def lanes(tile, j):
    return jnp.broadcast_to(tile[:, j : j + 1], (8, 128))


def eliminate(tiles):
    sub = lax.broadcasted_iota(jnp.int32, (8, 128), 0)
    scales = []
    for t in range(8):
        own = tiles[t]
        cols = [lanes(own, 8 * t + j) for j in range(8)]
        inv, cross = [], {}
        pivots = jnp.ones((8, 128), F32)
        for j in range(8):
            pivot = jnp.broadcast_to(cols[j][j : j + 1, :], (8, 128))
            pivots = jnp.where(sub == j, pivot, pivots)
            r = 1.0 / pivot
            inv.append(r)
            if j == 7:
                break
            m = jnp.where(sub > j, cols[j] * r, 0.0)
            for k in range(j + 1, 8):
                cross[j, k] = jnp.broadcast_to(cols[k][j : j + 1, :], (8, 128))
                cols[k] = cols[k] - m * cross[j, k]
            own = own - m * jnp.broadcast_to(own[j : j + 1, :], (8, 128))
        tiles[t] = own
        scales.append(lax.rsqrt(pivots))
        rows = [jnp.broadcast_to(own[j : j + 1, :], (8, 128)) for j in range(8)]
        for i in range(t + 1, 8):
            low = tiles[i]
            cols = [lanes(low, 8 * t + j) for j in range(8)]
            for j in range(8):
                m = cols[j] * inv[j]
                for k in range(j + 1, 8):
                    cols[k] = cols[k] - m * cross[j, k]
                low = low - m * rows[j]
            tiles[i] = low
    return tiles, scales


def factor_block(work, small, inverse_small):
    for b in range(B // S):
        lo, hi = b * S, (b + 1) * S
        small[:, 0:S] = work[lo:hi, lo:hi]
        row = lax.broadcasted_iota(jnp.int32, (S, S), 0)
        col = lax.broadcasted_iota(jnp.int32, (S, S), 1)
        small[:, S : 2 * S] = jnp.where(row == col, 1.0, 0.0)
        tiles, scales = eliminate([small[8 * i : 8 * i + 8, :] for i in range(8)])
        for i in range(8):
            small[8 * i : 8 * i + 8, :] = tiles[i] * scales[i]
        inverse_small[...] = small[:, S : 2 * S]
        top = dot(inverse_small[...], work[lo:hi, :], NN, HIGH)
        work[lo:hi, :] = top
        if hi < B:
            work[hi:B, :] = work[hi:B, :] - dot(top[:, hi:B], top, TN, HIGH)


def split(a):
    high = a.astype(BF16)
    rest = a - high.astype(F32)
    middle = rest.astype(BF16)
    return high, middle, (rest - middle.astype(F32)).astype(BF16)


def write_left(ref, a):
    high, middle, low = split(a)
    for n, term in enumerate((high, high, middle, high, low, middle)):
        ref[:, n * B : (n + 1) * B] = term


def write_right(ref, start, a):
    high, middle, low = split(a)
    for n, term in enumerate((high, middle, high, low, high, middle)):
        ref[:, start + n * B : start + (n + 1) * B] = term


def factor_kernel(flags, near_ref, far_ref, inverse_ref, l10t_ref, lower_ref, diag_ref, work, small, inverse_small):
    parts, part = near_ref.shape[:2]
    for ref, first in ((near_ref, flags[1] * part), (far_ref, (1 - flags[1]) * part)):
        for q in range(parts):
            diag_ref[pl.ds(pl.multiple_of(q * 2 * part + first, part), part), :] = ref[q]
    row = lax.broadcasted_iota(jnp.int32, (B, B), 0)
    col = lax.broadcasted_iota(jnp.int32, (B, B), 1)
    eye = jnp.where(row == col, 1.0, 0.0)
    work[:, 0:B] = diag_ref[:, 0:B]
    work[:, B : 2 * B] = eye
    factor_block(work, small, inverse_small)
    x0 = work[:, B : 2 * B]
    write_right(inverse_ref, 0, x0)
    lower_ref[:, 0:B] = jnp.where(row <= col, work[:, 0:B], 0.0).T
    l10t = dot(x0, diag_ref[:, B : 2 * B], NN, HIGH).astype(BF16)
    l10t_ref[...] = l10t
    work[:, 0:B] = diag_ref[:, 2 * B : 3 * B] - dot(l10t, l10t, TN)
    work[:, B : 2 * B] = eye
    factor_block(work, small, inverse_small)
    write_right(inverse_ref, 6 * B, work[:, B : 2 * B])
    lower_ref[:, B : 2 * B] = jnp.where(row <= col, work[:, 0:B], 0.0).T


def factor_diagonal(flags, near, far):
    return pl.pallas_call(
        factor_kernel,
        in_specs=[SMEM_SPEC] + [VMEM_SPEC] * 2,
        out_specs=[VMEM_SPEC] * 3,
        out_shape=[
            jax.ShapeDtypeStruct((B, 12 * B), BF16),
            jax.ShapeDtypeStruct((B, B), BF16),
            jax.ShapeDtypeStruct((B, 2 * B), F32),
        ],
        scratch_shapes=[
            pltpu.VMEM((B, 3 * B), F32),
            pltpu.VMEM((B, 2 * B), F32),
            pltpu.VMEM((S, 2 * S), F32),
            pltpu.VMEM((S, S), F32),
        ],
        compiler_params=pltpu.CompilerParams(vmem_limit_bytes=VMEM_BYTES),
        cost_estimate=pl.CostEstimate(flops=2 * 10**10, bytes_accessed=80_000_000, transcendentals=0),
    )(flags, near, far)


def solve_rows(first, second, wide, inverse_ref, l10t_ref):
    write_left(wide, first)
    p0 = dot(wide[...], inverse_ref[:, 0 : 6 * B], NT)
    write_left(wide, second - dot(p0.astype(BF16), l10t_ref[...], NN))
    p1 = dot(wide[...], inverse_ref[:, 6 * B : 12 * B], NT)
    return p0, p1


def piece_kernel(
    flags, piece_ref, turned_ref, seen_ref, inverse_ref, l10t_ref, along_ref, across_ref, white_ref, raw, wide
):
    blocks, part = piece_ref.shape[:2]
    held = blocks * part
    fold = seen_ref.shape[1]
    raw[0:held, :] = piece_ref[...].reshape(held, 2 * B)
    raw[held : 2 * held, :] = turned_ref[...].reshape(held, 2 * B)
    for panel in range(2):
        for h in range(2):
            for parity in range(2):
                for f in range(2):
                    lane = (2 * f + panel) * 128
                    top = 2 * held + (2 * parity + f) * fold
                    raw[top : top + fold, panel * B + h * 128 : panel * B + (h + 1) * 128] = seen_ref[
                        4 * flags[6 + panel] + 2 * h + parity, :, lane : lane + 128
                    ]
    for panel, p in enumerate(solve_rows(raw[:, 0:B], raw[:, B : 2 * B], wide, inverse_ref, l10t_ref)):
        cut = slice(panel * B, (panel + 1) * B)
        white_ref[:, cut] = p[2 * held :]
        for b in range(blocks):
            mine = p[b * part : (b + 1) * part].astype(BF16)
            mine = jnp.where(flags[16 + b] > panel, mine, jnp.zeros_like(mine))
            for q in range(along_ref.shape[0]):
                along_ref[q, b, :, cut] = mine
            theirs = p[held + b * part : held + (b + 1) * part].astype(BF16)
            level = flags[8 + flags[1] * blocks + b]
            across_ref[b, :, cut] = jnp.where(level > panel, theirs, jnp.zeros_like(theirs))


def solve_pieces(flags, piece, turned, seen, inverse, l10t, parts):
    held = piece.shape[0] * piece.shape[1]
    particles = 4 * seen.shape[1]
    return pl.pallas_call(
        piece_kernel,
        in_specs=[SMEM_SPEC] + [VMEM_SPEC] * 5,
        out_specs=[VMEM_SPEC] * 3,
        scratch_shapes=[
            pltpu.VMEM((2 * held + particles, 2 * B), F32),
            pltpu.VMEM((2 * held + particles, 6 * B), BF16),
        ],
        out_shape=[
            jax.ShapeDtypeStruct((parts,) + piece.shape, BF16),
            jax.ShapeDtypeStruct(piece.shape, BF16),
            jax.ShapeDtypeStruct((particles, 2 * B), F32),
        ],
        compiler_params=pltpu.CompilerParams(vmem_limit_bytes=VMEM_BYTES),
        cost_estimate=pl.CostEstimate(flops=10**9, bytes_accessed=4_000_000, transcendentals=0),
    )(flags, piece, turned, seen, inverse, l10t)


def whole(*shape):
    return pl.BlockSpec(shape, lambda i, flags: (0,) * len(shape))


def panel_kernel(flags, first_ref, second_ref, along_ref, inverse_ref, l10t_ref, out_ref, wide):
    level = flags[16 + pl.program_id(0)]
    parts, _, part = along_ref.shape[:3]

    @pl.when(flags[4] >= 0)
    def _():
        write_left(wide, first_ref[...])
        p = dot(wide[...], inverse_ref[:, 0 : 6 * B], NT)
        out_ref[:, 0:B] = jnp.where(level > 0, p, 0.0)

    @pl.when(flags[5] >= 0)
    def _():
        before = along_ref[:, 0, :, 0:B].reshape(parts * part, B)
        write_left(wide, second_ref[...] - dot(before, l10t_ref[...], NN))
        p = dot(wide[...], inverse_ref[:, 6 * B : 12 * B], NT)
        out_ref[:, B : 2 * B] = jnp.where(level > 1, p, 0.0)


def solve_panels(flags, covariance, along, inverse, l10t):
    rows = covariance.shape[0]
    parts, blocks, part, width = along.shape
    return pl.pallas_call(
        panel_kernel,
        grid_spec=pltpu.PrefetchScalarGridSpec(
            num_scalar_prefetch=1,
            grid=(blocks,),
            in_specs=[
                pl.BlockSpec((B, B), lambda i, flags: (i, jnp.maximum(flags[4], 0))),
                pl.BlockSpec((B, B), lambda i, flags: (i, jnp.maximum(flags[5], 0))),
                pl.BlockSpec((parts, 1, part, width), lambda i, flags: (0, i, 0, 0)),
                whole(*inverse.shape),
                whole(*l10t.shape),
            ],
            out_specs=pl.BlockSpec((B, 2 * B), lambda i, flags: (i, 0)),
            scratch_shapes=[pltpu.VMEM((B, 6 * B), BF16)],
        ),
        out_shape=jax.ShapeDtypeStruct((rows, 2 * B), F32),
        compiler_params=pltpu.CompilerParams(vmem_limit_bytes=VMEM_BYTES),
        cost_estimate=pl.CostEstimate(flops=10**9, bytes_accessed=4_000_000, transcendentals=0),
    )(flags, covariance, covariance, along, inverse, l10t)


def update_kernel(
    flags, cov_ref, along_ref, across_ref, relaid_ref, white_ref, panel_ref, lower_ref, out_ref, solved_ref, columns
):
    i = pl.program_id(0)
    parts, _, part = along_ref.shape[:3]
    blocks = across_ref.shape[1]
    steps = parts // 2
    column_blocks = 2 * blocks
    half = relaid_ref.shape[1]

    @pl.when(i == 0)
    def _():
        for q in range(parts):
            first = 4 * lax.rem(q // 2 + flags[0], steps) + 2 * (q % 2)
            for parity in range(2):
                for b in range(blocks):
                    top = (parity * blocks + b) * B + q * part
                    columns[top : top + part, :] = across_ref[first + parity, b]

    level = flags[16 + i]
    own = along_ref[:, 0].reshape(parts * part, 2 * B)
    for n in range(column_blocks):
        cut = slice(n * B, (n + 1) * B)
        out_ref[:, cut] = cov_ref[:, cut] - dot(own, columns[cut, :], NT)

    for panel in range(2):
        is_row = i == flags[2 + panel]
        for n in range(column_blocks):

            @pl.when(is_row & (flags[8 + n] > panel))
            def _():
                out_ref[:, n * B : (n + 1) * B] = jnp.zeros((B, B), F32)

        column = flags[4 + panel]
        place = pl.ds(pl.multiple_of(jnp.maximum(column, 0) * B, B), B)

        @pl.when((column >= 0) & (level > panel))
        def _():
            out_ref[:, place] = panel_ref[:, panel * B : (panel + 1) * B]

        @pl.when((column >= 0) & is_row)
        def _():
            out_ref[:, place] = lower_ref[:, panel * B : (panel + 1) * B]

    product = dot(white_ref[...].astype(BF16), own, NT)
    for parity in range(2):
        for h in range(2):
            there = (slice(parity * half, (parity + 1) * half), slice(h * 128, (h + 1) * 128))
            solved_ref[there] = relaid_ref[2 * h + parity] - product[there]
    for panel in range(2):

        @pl.when(i == flags[2 + panel])
        def _():
            solved_ref[...] = white_ref[:, panel * B : (panel + 1) * B]


def update(flags, covariance, along, across, relaid, white, panels, lower):
    rows, columns = covariance.shape
    parts, blocks, part, width = along.shape
    half = relaid.shape[1]
    return pl.pallas_call(
        update_kernel,
        grid_spec=pltpu.PrefetchScalarGridSpec(
            num_scalar_prefetch=1,
            grid=(blocks,),
            in_specs=[
                pl.BlockSpec((B, columns), lambda i, flags: (i, 0)),
                pl.BlockSpec((parts, 1, part, width), lambda i, flags: (0, i, 0, 0)),
                whole(*across.shape),
                pl.BlockSpec((4, half, 128), lambda i, flags: (lax.rem(i + flags[0], blocks), 0, 0)),
                whole(*white.shape),
                pl.BlockSpec((B, width), lambda i, flags: (i, 0)),
                whole(*lower.shape),
            ],
            out_specs=[
                pl.BlockSpec((B, columns), lambda i, flags: (i, 0)),
                pl.BlockSpec((2 * half, B), lambda i, flags: (0, i)),
            ],
            scratch_shapes=[pltpu.VMEM((columns, width), BF16)],
        ),
        out_shape=[jax.ShapeDtypeStruct((rows, columns), F32), jax.ShapeDtypeStruct((2 * half, rows), F32)],
        compiler_params=pltpu.CompilerParams(vmem_limit_bytes=VMEM_BYTES),
        cost_estimate=pl.CostEstimate(flops=5 * 10**9, bytes_accessed=20_000_000, transcendentals=0),
    )(flags, covariance, along, across, relaid, white, panels, lower)


def per_device(covariance, innovations, block_owner, panel_index, *, n_row, n_col):
    local_rows, local_cols = covariance.shape
    row_blocks, column_blocks = local_rows // B, local_cols // B
    r, c = lax.axis_index("row"), lax.axis_index("col")
    targets = panel_index[0] + jnp.arange(2, dtype=jnp.int32)
    positions = jnp.arange(block_owner.shape[0], dtype=jnp.int32)
    slot = jnp.sum(jnp.where(block_owner[None, :] == targets[:, None], positions[None, :], 0), axis=1)
    row_root, column_root = slot // row_blocks, slot // column_blocks
    row_slot, column_slot = slot % row_blocks, slot % column_blocks
    levels = jnp.sum((block_owner[:, None] > targets[None, :]).astype(jnp.int32), axis=1)
    steps = n_row // 4
    shift, core = c // 2, r % 2
    pairs = [(a, a ^ 1) for a in range(n_row)]
    same_core = [[a for a in range(n_row) if a % 2 == k] for k in range(2)]
    flags = jnp.concatenate(
        [
            shift[None],
            core[None],
            jnp.where(row_root == r, row_slot, -1),
            jnp.where(column_root == c, column_slot, -1),
            (row_slot + shift) % steps,
            lax.dynamic_slice_in_dim(levels, c * column_blocks, column_blocks),
            lax.dynamic_slice_in_dim(levels, r * row_blocks, row_blocks),
        ]
    ).astype(jnp.int32)
    across_axes = [
        (a * n_col + b, ((b // 2 + a // 4) % steps * 4 + b % 2 * 2 + a % 2) * n_col + a // 2)
        for a in range(n_row)
        for b in range(n_col)
    ]

    fold = innovations.shape[0] // 2
    wanted = [lax.dynamic_index_in_dim(innovations, row_root[n], 1, keepdims=False) for n in range(2)]
    wanted = jnp.concatenate([w[h * fold : (h + 1) * fold] for h in range(2) for w in wanted], axis=1)
    seen = lax.all_gather(lax.ppermute(wanted, ("row", "col"), across_axes), "row", axis=0)

    picked = pick_columns(column_slot.astype(jnp.int32), covariance, n_col)
    parts = lax.all_to_all(picked, "col", split_axis=0, concat_axis=0, tiled=True)
    part = parts.shape[2]
    piece = jnp.concatenate(
        [
            lax.dynamic_slice(parts, (column_root[n], 0, 0, n * B), (1, row_blocks, part, B))[0]
            for n in range(2)
        ],
        axis=-1,
    )

    chosen = jnp.where(r == row_root[0], row_slot[0], row_slot[1])
    mine = lax.dynamic_index_in_dim(piece, chosen, 0, keepdims=False)
    half = part // 2
    kept = lax.dynamic_slice_in_dim(mine, core * half, half, 0)
    given = lax.ppermute(lax.dynamic_slice_in_dim(mine, (1 - core) * half, half, 0), "row", pairs)
    both = jnp.concatenate([jnp.where(core == 0, kept, given), jnp.where(core == 0, given, kept)], axis=0)

    spread = lax.all_to_all(
        jnp.broadcast_to(both[None], (n_row // 2,) + both.shape),
        "row",
        split_axis=0,
        concat_axis=0,
        tiled=True,
        axis_index_groups=same_core,
    )
    upper = lax.dynamic_slice(spread, (row_root[0] // 2, row_root[0] % 2 * half, 0), (1, half, 2 * B))[0]
    lower = lax.dynamic_slice(spread, (row_root[1] // 2, row_root[1] % 2 * half, B), (1, half, B))[0]
    strip = jnp.concatenate([upper, lower], axis=-1)
    strip, seen = lax.optimization_barrier((strip, seen))
    near = lax.all_to_all(
        jnp.broadcast_to(strip[None], (n_col,) + strip.shape), "col", split_axis=0, concat_axis=0, tiled=True
    )
    far = lax.ppermute(near, "row", pairs)

    sent, groups, _ = lax.optimization_barrier((piece, jnp.transpose(innovations, (1, 0, 2)), near))
    turned = lax.ppermute(sent, ("row", "col"), across_axes)
    groups = lax.ppermute(groups, ("row", "col"), across_axes)
    inverse, l10t, lower = factor_diagonal(flags, near, far)
    inverse, groups = lax.optimization_barrier((inverse, groups))

    along, across, white = solve_pieces(flags, piece, turned, seen, inverse, l10t, n_col)
    across = lax.all_gather(across, "row", axis=0)
    along = lax.all_to_all(along, "col", split_axis=0, concat_axis=0, tiled=True)
    groups, along = lax.optimization_barrier((groups, along))
    relaid = lax.all_to_all(groups, "row", split_axis=0, concat_axis=0, tiled=True)
    panels = solve_panels(flags, covariance, along, inverse, l10t)
    return update(flags, covariance, along, across, relaid, white, panels, lower)


def solution(mesh):
    placed = (P("row", "col"), P("row", None, "col"), P(), P())
    return jax.shard_map(
        functools.partial(per_device, n_row=mesh.shape["row"], n_col=mesh.shape["col"]),
        mesh=mesh,
        in_specs=placed,
        out_specs=(P("row", "col"), P("col", "row")),
        check_vma=False,
    )
```

```python
import functools

import jax
import jax.numpy as jnp
from jax import lax
from jax.experimental import pallas as pl
from jax.experimental.pallas import tpu as pltpu
from jax.sharding import PartitionSpec as P

B = 256
S = 64
VMEM_BYTES = 60 * 1024 * 1024
F32 = jnp.float32
BF16 = jnp.bfloat16
HIGH = lax.Precision.HIGHEST
VMEM_SPEC = pl.BlockSpec(memory_space=pltpu.VMEM)
SMEM_SPEC = pl.BlockSpec(memory_space=pltpu.SMEM)


def dot(a, b, dims, precision=None):
    return lax.dot_general(a, b, (dims, ((), ())), precision=precision, preferred_element_type=F32)


NN = ((1,), (0,))
NT = ((1,), (1,))
TN = ((0,), (0,))


def pick_kernel(slots, cov_ref, out_ref):
    parts, blocks, part, width = out_ref.shape
    for b in range(blocks):
        out_ref[:, b] = cov_ref[b * B : (b + 1) * B, :].reshape(parts, part, width)


def pick_columns(slots, covariance, parts):
    rows = covariance.shape[0]
    blocks = rows // B
    part = B // parts
    return pl.pallas_call(
        pick_kernel,
        grid_spec=pltpu.PrefetchScalarGridSpec(
            num_scalar_prefetch=1,
            grid=(2, blocks // 2),
            in_specs=[pl.BlockSpec((2 * B, B), lambda j, b, slots: (b, slots[j]))],
            out_specs=pl.BlockSpec((parts, 2, part, B), lambda j, b, slots: (0, b, 0, j)),
        ),
        out_shape=jax.ShapeDtypeStruct((parts, blocks, part, 2 * B), F32),
    )(slots, covariance)


def tiles_kernel(where, cov_ref, out_ref):
    for i in range(B // 8):
        for j in range(2):
            out_ref[i, j] = cov_ref[8 * i : 8 * i + 8, 128 * j : 128 * j + 128]


def pick_tiles(where, covariance):
    return pl.pallas_call(
        tiles_kernel,
        grid_spec=pltpu.PrefetchScalarGridSpec(
            num_scalar_prefetch=1,
            grid=(2,),
            in_specs=[pl.BlockSpec((B, B), lambda j, where: (where[0], where[1 + j]))],
            out_specs=pl.BlockSpec((B // 8, 2, 8, 128), lambda j, where: (0, j, 0, 0)),
        ),
        out_shape=jax.ShapeDtypeStruct((B // 8, 4, 8, 128), F32),
    )(where, covariance)


def lanes(tile, j):
    return jnp.broadcast_to(tile[:, j : j + 1], (8, 128))


def eliminate(tiles):
    sub = lax.broadcasted_iota(jnp.int32, (8, 128), 0)
    scales = []
    for t in range(8):
        own = tiles[t]
        cols = [lanes(own, 8 * t + j) for j in range(8)]
        inv, cross = [], {}
        pivots = jnp.ones((8, 128), F32)
        for j in range(8):
            pivot = jnp.broadcast_to(cols[j][j : j + 1, :], (8, 128))
            pivots = jnp.where(sub == j, pivot, pivots)
            r = 1.0 / pivot
            inv.append(r)
            if j == 7:
                break
            m = jnp.where(sub > j, cols[j] * r, 0.0)
            for k in range(j + 1, 8):
                cross[j, k] = jnp.broadcast_to(cols[k][j : j + 1, :], (8, 128))
                cols[k] = cols[k] - m * cross[j, k]
            own = own - m * jnp.broadcast_to(own[j : j + 1, :], (8, 128))
        tiles[t] = own
        scales.append(lax.rsqrt(pivots))
        rows = [jnp.broadcast_to(own[j : j + 1, :], (8, 128)) for j in range(8)]
        for i in range(t + 1, 8):
            low = tiles[i]
            cols = [lanes(low, 8 * t + j) for j in range(8)]
            for j in range(8):
                m = cols[j] * inv[j]
                for k in range(j + 1, 8):
                    cols[k] = cols[k] - m * cross[j, k]
                low = low - m * rows[j]
            tiles[i] = low
    return tiles, scales


def factor_block(work, small, inverse_small):
    for b in range(B // S):
        lo, hi = b * S, (b + 1) * S
        small[:, 0:S] = work[lo:hi, lo:hi]
        row = lax.broadcasted_iota(jnp.int32, (S, S), 0)
        col = lax.broadcasted_iota(jnp.int32, (S, S), 1)
        small[:, S : 2 * S] = jnp.where(row == col, 1.0, 0.0)
        tiles, scales = eliminate([small[8 * i : 8 * i + 8, :] for i in range(8)])
        for i in range(8):
            small[8 * i : 8 * i + 8, :] = tiles[i] * scales[i]
        inverse_small[...] = small[:, S : 2 * S]
        top = dot(inverse_small[...], work[lo:hi, :], NN, HIGH)
        work[lo:hi, :] = top
        if hi < B:
            work[hi:B, :] = work[hi:B, :] - dot(top[:, hi:B], top, TN, HIGH)


def split(a):
    high = a.astype(BF16)
    rest = a - high.astype(F32)
    middle = rest.astype(BF16)
    return high, middle, (rest - middle.astype(F32)).astype(BF16)


def write_left(ref, a):
    high, middle, low = split(a)
    for n, term in enumerate((high, high, middle, high, low, middle)):
        ref[:, n * B : (n + 1) * B] = term


def write_right(ref, start, a):
    high, middle, low = split(a)
    for n, term in enumerate((high, middle, high, low, high, middle)):
        ref[:, start + n * B : start + (n + 1) * B] = term


def factor_kernel(tiles_ref, inverse_ref, l10t_ref, lower_ref, diag_ref, work, small, inverse_small):
    for i in range(B // 8):
        for j in range(4):
            diag_ref[8 * i : 8 * i + 8, 128 * j : 128 * j + 128] = tiles_ref[4 * i + j, 0:8]
        for j in range(2):
            diag_ref[8 * i : 8 * i + 8, 512 + 128 * j : 640 + 128 * j] = tiles_ref[4 * i + 2 + j, 8:16]
    row = lax.broadcasted_iota(jnp.int32, (B, B), 0)
    col = lax.broadcasted_iota(jnp.int32, (B, B), 1)
    eye = jnp.where(row == col, 1.0, 0.0)
    work[:, 0:B] = diag_ref[:, 0:B]
    work[:, B : 2 * B] = eye
    factor_block(work, small, inverse_small)
    x0 = work[:, B : 2 * B]
    write_right(inverse_ref, 0, x0)
    lower_ref[:, 0:B] = jnp.where(row <= col, work[:, 0:B], 0.0).T
    l10t = dot(x0, diag_ref[:, B : 2 * B], NN, HIGH).astype(BF16)
    l10t_ref[...] = l10t
    work[:, 0:B] = diag_ref[:, 2 * B : 3 * B] - dot(l10t, l10t, TN)
    work[:, B : 2 * B] = eye
    factor_block(work, small, inverse_small)
    write_right(inverse_ref, 6 * B, work[:, B : 2 * B])
    lower_ref[:, B : 2 * B] = jnp.where(row <= col, work[:, 0:B], 0.0).T


def factor_diagonal(tiles):
    return pl.pallas_call(
        factor_kernel,
        in_specs=[VMEM_SPEC],
        out_specs=[VMEM_SPEC] * 3,
        out_shape=[
            jax.ShapeDtypeStruct((B, 12 * B), BF16),
            jax.ShapeDtypeStruct((B, B), BF16),
            jax.ShapeDtypeStruct((B, 2 * B), F32),
        ],
        scratch_shapes=[
            pltpu.VMEM((B, 3 * B), F32),
            pltpu.VMEM((B, 2 * B), F32),
            pltpu.VMEM((S, 2 * S), F32),
            pltpu.VMEM((S, S), F32),
        ],
        compiler_params=pltpu.CompilerParams(vmem_limit_bytes=VMEM_BYTES),
        cost_estimate=pl.CostEstimate(flops=2 * 10**10, bytes_accessed=80_000_000, transcendentals=0),
    )(tiles)


def solve_rows(first, second, wide, inverse_ref, l10t_ref):
    write_left(wide, first)
    p0 = dot(wide[...], inverse_ref[:, 0 : 6 * B], NT)
    write_left(wide, second - dot(p0.astype(BF16), l10t_ref[...], NN))
    p1 = dot(wide[...], inverse_ref[:, 6 * B : 12 * B], NT)
    return p0, p1


def piece_kernel(flags, piece_ref, inverse_ref, l10t_ref, along_ref, across_ref, wide):
    blocks, part = piece_ref.shape[:2]
    raw = piece_ref[...].reshape(blocks * part, 2 * B)
    for panel, p in enumerate(solve_rows(raw[:, 0:B], raw[:, B : 2 * B], wide, inverse_ref, l10t_ref)):
        cut = slice(panel * B, (panel + 1) * B)
        for b in range(blocks):
            mine = p[b * part : (b + 1) * part].astype(BF16)
            mine = jnp.where(flags[16 + b] > panel, mine, jnp.zeros_like(mine))
            across_ref[b, :, cut] = mine
            for q in range(along_ref.shape[0]):
                along_ref[q, b, :, cut] = mine


def solve_piece(flags, piece, inverse, l10t, parts):
    return pl.pallas_call(
        piece_kernel,
        in_specs=[SMEM_SPEC] + [VMEM_SPEC] * 3,
        out_specs=[VMEM_SPEC] * 2,
        scratch_shapes=[pltpu.VMEM((piece.shape[0] * piece.shape[1], 6 * B), BF16)],
        out_shape=[
            jax.ShapeDtypeStruct((parts,) + piece.shape, BF16),
            jax.ShapeDtypeStruct(piece.shape, BF16),
        ],
        compiler_params=pltpu.CompilerParams(vmem_limit_bytes=VMEM_BYTES),
        cost_estimate=pl.CostEstimate(flops=10**9, bytes_accessed=4_000_000, transcendentals=0),
    )(flags, piece, inverse, l10t)


def whole(*shape):
    return pl.BlockSpec(shape, lambda i, flags: (0,) * len(shape))


def panel_kernel(flags, first_ref, second_ref, along_ref, inverse_ref, l10t_ref, out_ref, wide):
    level = flags[16 + pl.program_id(0)]
    parts, _, part = along_ref.shape[:3]

    @pl.when(flags[4] >= 0)
    def _():
        write_left(wide, first_ref[...])
        p = dot(wide[...], inverse_ref[:, 0 : 6 * B], NT)
        out_ref[:, 0:B] = jnp.where(level > 0, p, 0.0)

    @pl.when(flags[5] >= 0)
    def _():
        before = along_ref[:, 0, :, 0:B].reshape(parts * part, B)
        write_left(wide, second_ref[...] - dot(before, l10t_ref[...], NN))
        p = dot(wide[...], inverse_ref[:, 6 * B : 12 * B], NT)
        out_ref[:, B : 2 * B] = jnp.where(level > 1, p, 0.0)


def solve_panels(flags, covariance, along, inverse, l10t):
    rows = covariance.shape[0]
    parts, blocks, part, width = along.shape
    return pl.pallas_call(
        panel_kernel,
        grid_spec=pltpu.PrefetchScalarGridSpec(
            num_scalar_prefetch=1,
            grid=(blocks,),
            in_specs=[
                pl.BlockSpec((B, B), lambda i, flags: (i, jnp.maximum(flags[4], 0))),
                pl.BlockSpec((B, B), lambda i, flags: (i, jnp.maximum(flags[5], 0))),
                pl.BlockSpec((parts, 1, part, width), lambda i, flags: (0, i, 0, 0)),
                whole(*inverse.shape),
                whole(*l10t.shape),
            ],
            out_specs=pl.BlockSpec((B, 2 * B), lambda i, flags: (i, 0)),
            scratch_shapes=[pltpu.VMEM((B, 6 * B), BF16)],
        ),
        out_shape=jax.ShapeDtypeStruct((rows, 2 * B), F32),
        compiler_params=pltpu.CompilerParams(vmem_limit_bytes=VMEM_BYTES),
        cost_estimate=pl.CostEstimate(flops=10**9, bytes_accessed=4_000_000, transcendentals=0),
    )(flags, covariance, covariance, along, inverse, l10t)


def update_kernel(
    flags,
    cov_ref,
    along_ref,
    across_ref,
    relaid_ref,
    panel_ref,
    lower_ref,
    inverse_ref,
    l10t_ref,
    out_ref,
    solved_ref,
    columns,
    white_ref,
    wide,
):
    i = pl.program_id(0)
    parts, _, part = along_ref.shape[:3]
    blocks = across_ref.shape[1] - 3
    steps = parts // 2
    column_blocks = 2 * blocks
    half = relaid_ref.shape[1]
    fold = half // 2

    @pl.when(i == 0)
    def _():
        for q in range(parts):
            first = 4 * lax.rem(q // 2 + flags[0], steps) + 2 * (q % 2)
            for parity in range(2):
                for b in range(blocks):
                    top = (parity * blocks + b) * B + q * part
                    columns[top : top + part, :] = across_ref[first + parity, b]
        for panel in range(2):
            for h in range(2):
                for parity in range(2):
                    for f in range(2):
                        lane = (2 * f + panel) * 128
                        terms = [
                            across_ref[4 * flags[6 + panel] + 2 * h + parity, blocks + t, :, lane : lane + 128].astype(F32)
                            for t in range(3)
                        ]
                        top = (2 * parity + f) * fold
                        white_ref[top : top + fold, panel * B + h * 128 : panel * B + (h + 1) * 128] = (
                            terms[0] + terms[1]
                        ) + terms[2]
        w0, w1 = solve_rows(white_ref[:, 0:B], white_ref[:, B : 2 * B], wide, inverse_ref, l10t_ref)
        white_ref[:, 0:B] = w0
        white_ref[:, B : 2 * B] = w1

    level = flags[16 + i]
    own = along_ref[:, 0].reshape(parts * part, 2 * B)
    for n in range(column_blocks):
        cut = slice(n * B, (n + 1) * B)
        out_ref[:, cut] = cov_ref[:, cut] - dot(own, columns[cut, :], NT)

    for panel in range(2):
        is_row = i == flags[2 + panel]
        for n in range(column_blocks):

            @pl.when(is_row & (flags[8 + n] > panel))
            def _():
                out_ref[:, n * B : (n + 1) * B] = jnp.zeros((B, B), F32)

        column = flags[4 + panel]
        place = pl.ds(pl.multiple_of(jnp.maximum(column, 0) * B, B), B)

        @pl.when((column >= 0) & (level > panel))
        def _():
            out_ref[:, place] = panel_ref[:, panel * B : (panel + 1) * B]

        @pl.when((column >= 0) & is_row)
        def _():
            out_ref[:, place] = lower_ref[:, panel * B : (panel + 1) * B]

    product = dot(white_ref[...].astype(BF16), own, NT)
    for parity in range(2):
        for h in range(2):
            there = (slice(parity * half, (parity + 1) * half), slice(h * 128, (h + 1) * 128))
            solved_ref[there] = relaid_ref[2 * h + parity] - product[there]
    for panel in range(2):

        @pl.when(i == flags[2 + panel])
        def _():
            solved_ref[...] = white_ref[:, panel * B : (panel + 1) * B]


def update(flags, covariance, along, across, relaid, panels, lower, inverse, l10t):
    rows, columns = covariance.shape
    parts, blocks, part, width = along.shape
    half = relaid.shape[1]
    return pl.pallas_call(
        update_kernel,
        grid_spec=pltpu.PrefetchScalarGridSpec(
            num_scalar_prefetch=1,
            grid=(blocks,),
            in_specs=[
                pl.BlockSpec((B, columns), lambda i, flags: (i, 0)),
                pl.BlockSpec((parts, 1, part, width), lambda i, flags: (0, i, 0, 0)),
                whole(*across.shape),
                pl.BlockSpec((4, half, 128), lambda i, flags: (lax.rem(i + flags[0], blocks), 0, 0)),
                pl.BlockSpec((B, width), lambda i, flags: (jnp.where((flags[4] & flags[5]) >= 0, i, 0), 0)),
                whole(*lower.shape),
                whole(*inverse.shape),
                whole(*l10t.shape),
            ],
            out_specs=[
                pl.BlockSpec((B, columns), lambda i, flags: (i, 0)),
                pl.BlockSpec((2 * half, B), lambda i, flags: (0, i)),
            ],
            scratch_shapes=[
                pltpu.VMEM((columns, width), BF16),
                pltpu.VMEM((2 * half, width), F32),
                pltpu.VMEM((2 * half, 6 * B), BF16),
            ],
        ),
        out_shape=[jax.ShapeDtypeStruct((rows, columns), F32), jax.ShapeDtypeStruct((2 * half, rows), F32)],
        compiler_params=pltpu.CompilerParams(vmem_limit_bytes=VMEM_BYTES),
        cost_estimate=pl.CostEstimate(flops=5 * 10**9, bytes_accessed=20_000_000, transcendentals=0),
    )(flags, covariance, along, across, relaid, panels, lower, inverse, l10t)


def per_device(covariance, innovations, block_owner, panel_index, *, n_row, n_col):
    local_rows, local_cols = covariance.shape
    row_blocks, column_blocks = local_rows // B, local_cols // B
    r, c = lax.axis_index("row"), lax.axis_index("col")
    targets = panel_index[0] + jnp.arange(2, dtype=jnp.int32)
    positions = jnp.arange(block_owner.shape[0], dtype=jnp.int32)
    slot = jnp.sum(jnp.where(block_owner[None, :] == targets[:, None], positions[None, :], 0), axis=1)
    row_root, column_root = slot // row_blocks, slot // column_blocks
    row_slot, column_slot = slot % row_blocks, slot % column_blocks
    levels = jnp.sum((block_owner[:, None] > targets[None, :]).astype(jnp.int32), axis=1)
    steps = n_row // 4
    shift, core = c // 2, r % 2
    flags = jnp.concatenate(
        [
            shift[None],
            core[None],
            jnp.where(row_root == r, row_slot, -1),
            jnp.where(column_root == c, column_slot, -1),
            (row_slot + shift) % steps,
            lax.dynamic_slice_in_dim(levels, c * column_blocks, column_blocks),
            lax.dynamic_slice_in_dim(levels, r * row_blocks, row_blocks),
        ]
    ).astype(jnp.int32)
    across_axes = [
        (a * n_col + b, ((b // 2 + a // 4) % steps * 4 + b % 2 * 2 + a % 2) * n_col + a // 2)
        for a in range(n_row)
        for b in range(n_col)
    ]

    chosen = jnp.where(r == row_root[0], row_slot[0], row_slot[1])
    where = jnp.concatenate([chosen[None], column_slot]).astype(jnp.int32)
    tiles = pick_tiles(where, covariance).reshape(n_row * n_col, 8, 128)
    tiles = lax.all_to_all(tiles, ("row", "col"), split_axis=0, concat_axis=0, tiled=True)
    source = jnp.where(c % 4 < 2, column_root[0], column_root[1])
    tiles = jnp.concatenate(
        [lax.dynamic_index_in_dim(tiles, row_root[n] * n_col + source, 0, keepdims=False) for n in range(2)], axis=0
    )
    tiles = lax.all_to_all(
        jnp.broadcast_to(tiles[None], (n_row * n_col,) + tiles.shape),
        ("row", "col"),
        split_axis=0,
        concat_axis=0,
        tiled=True,
    )
    inverse, l10t, lower = factor_diagonal(tiles)

    picked = pick_columns(column_slot.astype(jnp.int32), covariance, n_col)
    picked, _ = lax.optimization_barrier((picked, tiles))
    parts = lax.all_to_all(picked, "col", split_axis=0, concat_axis=0, tiled=True)
    part = parts.shape[2]
    piece = jnp.concatenate(
        [
            lax.dynamic_slice(parts, (column_root[n], 0, 0, n * B), (1, row_blocks, part, B))[0]
            for n in range(2)
        ],
        axis=-1,
    )

    fold = innovations.shape[0] // 2
    wanted = [lax.dynamic_index_in_dim(innovations, row_root[n], 1, keepdims=False) for n in range(2)]
    wanted = jnp.concatenate([w[h * fold : (h + 1) * fold] for h in range(2) for w in wanted], axis=1)
    high = lax.reduce_precision(wanted, 8, 7)
    middle = lax.reduce_precision(wanted - high, 8, 7)
    wanted = jnp.stack([high, middle, wanted - high - middle]).astype(BF16)

    along, across = solve_piece(flags, piece, inverse, l10t, n_col)
    across = lax.ppermute(jnp.concatenate([across, wanted], axis=0), ("row", "col"), across_axes)
    across_all = lax.all_gather(across, "row", axis=0)
    along = lax.all_to_all(along, "col", split_axis=0, concat_axis=0, tiled=True)

    groups, _ = lax.optimization_barrier((jnp.transpose(innovations, (1, 0, 2)), across))
    groups = lax.ppermute(groups, ("row", "col"), across_axes)
    along, groups = lax.optimization_barrier((along, groups))
    relaid = lax.all_to_all(groups, "row", split_axis=0, concat_axis=0, tiled=True)
    panels = solve_panels(flags, covariance, along, inverse, l10t)
    return update(flags, covariance, along, across_all, relaid, panels, lower, inverse, l10t)


def solution(mesh):
    placed = (P("row", "col"), P("row", None, "col"), P(), P())
    return jax.shard_map(
        functools.partial(per_device, n_row=mesh.shape["row"], n_col=mesh.shape["col"]),
        mesh=mesh,
        in_specs=placed,
        out_specs=(P("row", "col"), P("col", "row")),
        check_vma=False,
    )
```

```python
import functools

import jax
import jax.numpy as jnp
from jax import lax
from jax.experimental import pallas as pl
from jax.experimental.pallas import tpu as pltpu
from jax.sharding import PartitionSpec as P

B = 256
S = 64
VMEM_BYTES = 60 * 1024 * 1024
F32 = jnp.float32
BF16 = jnp.bfloat16
HIGH = lax.Precision.HIGHEST
VMEM_SPEC = pl.BlockSpec(memory_space=pltpu.VMEM)
SMEM_SPEC = pl.BlockSpec(memory_space=pltpu.SMEM)


def dot(a, b, dims, precision=None):
    return lax.dot_general(a, b, (dims, ((), ())), precision=precision, preferred_element_type=F32)


NN = ((1,), (0,))
NT = ((1,), (1,))
TN = ((0,), (0,))


def pick_kernel(slots, cov_ref, out_ref):
    parts, blocks, part, width = out_ref.shape
    for b in range(blocks):
        out_ref[:, b] = cov_ref[b * B : (b + 1) * B, :].reshape(parts, part, width)


def pick_columns(slots, covariance, parts):
    rows = covariance.shape[0]
    blocks = rows // B
    part = B // parts
    return pl.pallas_call(
        pick_kernel,
        grid_spec=pltpu.PrefetchScalarGridSpec(
            num_scalar_prefetch=1,
            grid=(2, blocks // 2),
            in_specs=[pl.BlockSpec((2 * B, B), lambda j, b, slots: (b, slots[j]))],
            out_specs=pl.BlockSpec((parts, 2, part, B), lambda j, b, slots: (0, b, 0, j)),
        ),
        out_shape=jax.ShapeDtypeStruct((parts, blocks, part, 2 * B), F32),
    )(slots, covariance)


def tiles_kernel(owner_ref, panel_ref, cov_ref, out_ref, held, arrived):
    slots = [jnp.int32(0), jnp.int32(0)]
    for place in range(owner_ref.shape[0]):
        for n in range(2):
            slots[n] = jnp.where(owner_ref[place] == panel_ref[0] + n, place, slots[n])
    row_blocks, column_blocks = cov_ref.shape[0] // B, cov_ref.shape[1] // B
    first_here = lax.div(slots[0], row_blocks) == lax.axis_index("row")
    row = lax.rem(jnp.where(first_here, slots[0], slots[1]), row_blocks)
    copies = []
    for n in range(2):
        column = lax.rem(slots[n], column_blocks)
        copies.append(
            pltpu.make_async_copy(
                cov_ref.at[pl.ds(pl.multiple_of(row * B, B), B), pl.ds(pl.multiple_of(column * B, B), B)],
                held.at[n],
                arrived.at[n],
            )
        )
        copies[n].start()
    for n in range(2):
        copies[n].wait()
        for i in range(B // 8):
            for j in range(2):
                out_ref[i, 2 * n + j] = held[n, 8 * i : 8 * i + 8, 128 * j : 128 * j + 128]


def pick_tiles(block_owner, panel_index, covariance):
    return pl.pallas_call(
        tiles_kernel,
        in_specs=[SMEM_SPEC, SMEM_SPEC, pl.BlockSpec(memory_space=pl.ANY)],
        out_specs=VMEM_SPEC,
        out_shape=jax.ShapeDtypeStruct((B // 8, 4, 8, 128), F32),
        scratch_shapes=[pltpu.VMEM((2, B, B), F32), pltpu.SemaphoreType.DMA((2,))],
    )(block_owner, panel_index, covariance)


def lanes(tile, j):
    return jnp.broadcast_to(tile[:, j : j + 1], (8, 128))


def eliminate(tiles):
    sub = lax.broadcasted_iota(jnp.int32, (8, 128), 0)
    scales = []
    for t in range(8):
        own = tiles[t]
        cols = [lanes(own, 8 * t + j) for j in range(8)]
        inv, cross = [], {}
        pivots = jnp.ones((8, 128), F32)
        for j in range(8):
            pivot = jnp.broadcast_to(cols[j][j : j + 1, :], (8, 128))
            pivots = jnp.where(sub == j, pivot, pivots)
            r = 1.0 / pivot
            inv.append(r)
            if j == 7:
                break
            m = jnp.where(sub > j, cols[j] * r, 0.0)
            for k in range(j + 1, 8):
                cross[j, k] = jnp.broadcast_to(cols[k][j : j + 1, :], (8, 128))
                cols[k] = cols[k] - m * cross[j, k]
            own = own - m * jnp.broadcast_to(own[j : j + 1, :], (8, 128))
        tiles[t] = own
        scales.append(lax.rsqrt(pivots))
        rows = [jnp.broadcast_to(own[j : j + 1, :], (8, 128)) for j in range(8)]
        for i in range(t + 1, 8):
            low = tiles[i]
            cols = [lanes(low, 8 * t + j) for j in range(8)]
            for j in range(8):
                m = cols[j] * inv[j]
                for k in range(j + 1, 8):
                    cols[k] = cols[k] - m * cross[j, k]
                low = low - m * rows[j]
            tiles[i] = low
    return tiles, scales


def factor_block(work, small, inverse_small):
    for b in range(B // S):
        lo, hi = b * S, (b + 1) * S
        small[:, 0:S] = work[lo:hi, lo:hi]
        row = lax.broadcasted_iota(jnp.int32, (S, S), 0)
        col = lax.broadcasted_iota(jnp.int32, (S, S), 1)
        small[:, S : 2 * S] = jnp.where(row == col, 1.0, 0.0)
        tiles, scales = eliminate([small[8 * i : 8 * i + 8, :] for i in range(8)])
        for i in range(8):
            small[8 * i : 8 * i + 8, :] = tiles[i] * scales[i]
        inverse_small[...] = small[:, S : 2 * S]
        top = dot(inverse_small[...], work[lo:hi, :], NN, HIGH)
        work[lo:hi, :] = top
        if hi < B:
            work[hi:B, :] = work[hi:B, :] - dot(top[:, hi:B], top, TN, HIGH)


def split(a):
    high = a.astype(BF16)
    rest = a - high.astype(F32)
    middle = rest.astype(BF16)
    return high, middle, (rest - middle.astype(F32)).astype(BF16)


def write_left(ref, a):
    high, middle, low = split(a)
    for n, term in enumerate((high, high, middle, high, low, middle)):
        ref[:, n * B : (n + 1) * B] = term


def write_right(ref, start, a):
    high, middle, low = split(a)
    for n, term in enumerate((high, middle, high, low, high, middle)):
        ref[:, start + n * B : start + (n + 1) * B] = term


def factor_kernel(tiles_ref, inverse_ref, l10t_ref, lower_ref, diag_ref, work, small, inverse_small):
    for i in range(B // 8):
        for j in range(4):
            diag_ref[8 * i : 8 * i + 8, 128 * j : 128 * j + 128] = tiles_ref[4 * i + j, 0:8]
        for j in range(2):
            diag_ref[8 * i : 8 * i + 8, 512 + 128 * j : 640 + 128 * j] = tiles_ref[4 * i + 2 + j, 8:16]
    row = lax.broadcasted_iota(jnp.int32, (B, B), 0)
    col = lax.broadcasted_iota(jnp.int32, (B, B), 1)
    eye = jnp.where(row == col, 1.0, 0.0)
    work[:, 0:B] = diag_ref[:, 0:B]
    work[:, B : 2 * B] = eye
    factor_block(work, small, inverse_small)
    x0 = work[:, B : 2 * B]
    write_right(inverse_ref, 0, x0)
    lower_ref[:, 0:B] = jnp.where(row <= col, work[:, 0:B], 0.0).T
    l10t = dot(x0, diag_ref[:, B : 2 * B], NN, HIGH).astype(BF16)
    l10t_ref[...] = l10t
    work[:, 0:B] = diag_ref[:, 2 * B : 3 * B] - dot(l10t, l10t, TN)
    work[:, B : 2 * B] = eye
    factor_block(work, small, inverse_small)
    write_right(inverse_ref, 6 * B, work[:, B : 2 * B])
    lower_ref[:, B : 2 * B] = jnp.where(row <= col, work[:, 0:B], 0.0).T


def factor_diagonal(tiles):
    return pl.pallas_call(
        factor_kernel,
        in_specs=[VMEM_SPEC],
        out_specs=[VMEM_SPEC] * 3,
        out_shape=[
            jax.ShapeDtypeStruct((B, 12 * B), BF16),
            jax.ShapeDtypeStruct((B, B), BF16),
            jax.ShapeDtypeStruct((B, 2 * B), F32),
        ],
        scratch_shapes=[
            pltpu.VMEM((B, 3 * B), F32),
            pltpu.VMEM((B, 2 * B), F32),
            pltpu.VMEM((S, 2 * S), F32),
            pltpu.VMEM((S, S), F32),
        ],
        compiler_params=pltpu.CompilerParams(vmem_limit_bytes=VMEM_BYTES // 4),
        cost_estimate=pl.CostEstimate(flops=2 * 10**10, bytes_accessed=80_000_000, transcendentals=0),
    )(tiles)


def solve_rows(first, second, wide, inverse_ref, l10t_ref):
    write_left(wide, first)
    p0 = dot(wide[...], inverse_ref[:, 0 : 6 * B], NT)
    write_left(wide, second - dot(p0.astype(BF16), l10t_ref[...], NN))
    p1 = dot(wide[...], inverse_ref[:, 6 * B : 12 * B], NT)
    return p0, p1


def piece_kernel(flags, first_ref, second_ref, inverse_ref, l10t_ref, along_ref, across_ref, wide):
    blocks, part = first_ref.shape[1:3]
    solved = solve_rows(
        first_ref[0].reshape(blocks * part, B), second_ref[0].reshape(blocks * part, B), wide, inverse_ref, l10t_ref
    )
    for panel, p in enumerate(solved):
        cut = slice(panel * B, (panel + 1) * B)
        for b in range(blocks):
            mine = p[b * part : (b + 1) * part].astype(BF16)
            mine = jnp.where(flags[16 + b] > panel, mine, jnp.zeros_like(mine))
            across_ref[b, :, cut] = mine
            for q in range(along_ref.shape[0]):
                along_ref[q, b, :, cut] = mine


def solve_piece(flags, parts, inverse, l10t):
    count, blocks, part = parts.shape[:3]
    return pl.pallas_call(
        piece_kernel,
        grid_spec=pltpu.PrefetchScalarGridSpec(
            num_scalar_prefetch=1,
            grid=(1,),
            in_specs=[
                pl.BlockSpec((1, blocks, part, B), lambda i, flags: (flags[20], 0, 0, 0)),
                pl.BlockSpec((1, blocks, part, B), lambda i, flags: (flags[21], 0, 0, 1)),
                whole(*inverse.shape),
                whole(*l10t.shape),
            ],
            out_specs=[whole(count, blocks, part, 2 * B), whole(blocks, part, 2 * B)],
            scratch_shapes=[pltpu.VMEM((blocks * part, 6 * B), BF16)],
        ),
        out_shape=[
            jax.ShapeDtypeStruct((count, blocks, part, 2 * B), BF16),
            jax.ShapeDtypeStruct((blocks, part, 2 * B), BF16),
        ],
        compiler_params=pltpu.CompilerParams(vmem_limit_bytes=VMEM_BYTES // 4),
        cost_estimate=pl.CostEstimate(flops=10**9, bytes_accessed=4_000_000, transcendentals=0),
    )(flags, parts, parts, inverse, l10t)


def whole(*shape):
    return pl.BlockSpec(shape, lambda i, flags: (0,) * len(shape))


def panel_kernel(flags, first_ref, second_ref, along_ref, inverse_ref, l10t_ref, out_ref, wide):
    level = flags[16 + pl.program_id(0)]
    parts, _, part = along_ref.shape[:3]

    @pl.when(flags[4] >= 0)
    def _():
        write_left(wide, first_ref[...])
        p = dot(wide[...], inverse_ref[:, 0 : 6 * B], NT)
        out_ref[:, 0:B] = jnp.where(level > 0, p, 0.0)

    @pl.when(flags[5] >= 0)
    def _():
        before = along_ref[:, 0, :, 0:B].reshape(parts * part, B)
        write_left(wide, second_ref[...] - dot(before, l10t_ref[...], NN))
        p = dot(wide[...], inverse_ref[:, 6 * B : 12 * B], NT)
        out_ref[:, B : 2 * B] = jnp.where(level > 1, p, 0.0)


def solve_panels(flags, covariance, along, inverse, l10t):
    rows = covariance.shape[0]
    parts, blocks, part, width = along.shape
    return pl.pallas_call(
        panel_kernel,
        grid_spec=pltpu.PrefetchScalarGridSpec(
            num_scalar_prefetch=1,
            grid=(blocks,),
            in_specs=[
                pl.BlockSpec((B, B), lambda i, flags: (i, jnp.maximum(flags[4], 0))),
                pl.BlockSpec((B, B), lambda i, flags: (i, jnp.maximum(flags[5], 0))),
                pl.BlockSpec((parts, 1, part, width), lambda i, flags: (0, i, 0, 0)),
                whole(*inverse.shape),
                whole(*l10t.shape),
            ],
            out_specs=pl.BlockSpec((B, 2 * B), lambda i, flags: (i, 0)),
            scratch_shapes=[pltpu.VMEM((B, 6 * B), BF16)],
        ),
        out_shape=jax.ShapeDtypeStruct((rows, 2 * B), F32),
        compiler_params=pltpu.CompilerParams(vmem_limit_bytes=VMEM_BYTES // 4),
        cost_estimate=pl.CostEstimate(flops=10**9, bytes_accessed=4_000_000, transcendentals=0),
    )(flags, covariance, covariance, along, inverse, l10t)


def update_kernel(
    flags,
    cov_ref,
    along_ref,
    across_ref,
    relaid_ref,
    panel_ref,
    lower_ref,
    inverse_ref,
    l10t_ref,
    out_ref,
    solved_ref,
    columns,
    terms_ref,
    white_ref,
    wide,
    arrived,
):
    i = pl.program_id(0)
    parts, _, part = along_ref.shape[:3]
    blocks = across_ref.shape[1] - 3
    steps = parts // 2
    column_blocks = 2 * blocks
    half = relaid_ref.shape[1]
    fold = half // 2

    @pl.when(i == 0)
    def _():
        copies = []
        for panel in range(2):
            for n in range(4):
                source = across_ref.at[4 * flags[6 + panel] + n, pl.ds(blocks, 3)]
                copies.append(pltpu.make_async_copy(source, terms_ref.at[panel, n], arrived.at[len(copies)]))
        for q in range(parts):
            first = 4 * lax.rem(q // 2 + flags[0], steps) + 2 * (q % 2)
            for parity in range(2):
                source = across_ref.at[first + parity, pl.ds(0, blocks)]
                copies.append(pltpu.make_async_copy(source, columns.at[parity, :, q], arrived.at[len(copies)]))
        for copy in copies:
            copy.start()
        for copy in copies:
            copy.wait()
        for panel in range(2):
            for h in range(2):
                for parity in range(2):
                    for f in range(2):
                        lane = (2 * f + panel) * 128
                        terms = [
                            terms_ref[panel, 2 * h + parity, t, :, lane : lane + 128].astype(F32) for t in range(3)
                        ]
                        top = (2 * parity + f) * fold
                        white_ref[top : top + fold, panel * B + h * 128 : panel * B + (h + 1) * 128] = (
                            terms[0] + terms[1]
                        ) + terms[2]
        w0, w1 = solve_rows(white_ref[:, 0:B], white_ref[:, B : 2 * B], wide, inverse_ref, l10t_ref)
        white_ref[:, 0:B] = w0
        white_ref[:, B : 2 * B] = w1

    level = flags[16 + i]
    own = along_ref[:, 0].reshape(parts * part, 2 * B)
    for n in range(column_blocks):
        cut = slice(n * B, (n + 1) * B)
        out_ref[:, cut] = cov_ref[:, cut] - dot(own, columns[n // blocks, n % blocks].reshape(B, 2 * B), NT)

    for panel in range(2):
        is_row = i == flags[2 + panel]
        for n in range(column_blocks):

            @pl.when(is_row & (flags[8 + n] > panel))
            def _():
                out_ref[:, n * B : (n + 1) * B] = jnp.zeros((B, B), F32)

        column = flags[4 + panel]
        place = pl.ds(pl.multiple_of(jnp.maximum(column, 0) * B, B), B)

        @pl.when((column >= 0) & (level > panel))
        def _():
            out_ref[:, place] = panel_ref[:, panel * B : (panel + 1) * B]

        @pl.when((column >= 0) & is_row)
        def _():
            out_ref[:, place] = lower_ref[:, panel * B : (panel + 1) * B]

    product = dot(white_ref[...].astype(BF16), own, NT)
    for parity in range(2):
        for h in range(2):
            there = (slice(parity * half, (parity + 1) * half), slice(h * 128, (h + 1) * 128))
            solved_ref[there] = relaid_ref[2 * h + parity] - product[there]
    for panel in range(2):

        @pl.when(i == flags[2 + panel])
        def _():
            solved_ref[...] = white_ref[:, panel * B : (panel + 1) * B]


def update(flags, covariance, along, across, relaid, panels, lower, inverse, l10t):
    rows, columns = covariance.shape
    parts, blocks, part, width = along.shape
    half = relaid.shape[1]
    return pl.pallas_call(
        update_kernel,
        grid_spec=pltpu.PrefetchScalarGridSpec(
            num_scalar_prefetch=1,
            grid=(blocks,),
            in_specs=[
                pl.BlockSpec((B, columns), lambda i, flags: (i, 0)),
                pl.BlockSpec((parts, 1, part, width), lambda i, flags: (0, i, 0, 0)),
                pl.BlockSpec(memory_space=pl.ANY),
                pl.BlockSpec((4, half, 128), lambda i, flags: (lax.rem(i + flags[0], blocks), 0, 0)),
                pl.BlockSpec((B, width), lambda i, flags: (jnp.where((flags[4] & flags[5]) >= 0, i, 0), 0)),
                whole(*lower.shape),
                whole(*inverse.shape),
                whole(*l10t.shape),
            ],
            out_specs=[
                pl.BlockSpec((B, columns), lambda i, flags: (i, 0)),
                pl.BlockSpec((2 * half, B), lambda i, flags: (0, i)),
            ],
            scratch_shapes=[
                pltpu.VMEM((2, columns // (2 * B), parts, part, width), BF16),
                pltpu.VMEM((2, 4, 3, part, width), BF16),
                pltpu.VMEM((2 * half, width), F32),
                pltpu.VMEM((2 * half, 6 * B), BF16),
                pltpu.SemaphoreType.DMA((2 * parts + 8,)),
            ],
        ),
        out_shape=[jax.ShapeDtypeStruct((rows, columns), F32), jax.ShapeDtypeStruct((2 * half, rows), F32)],
        compiler_params=pltpu.CompilerParams(vmem_limit_bytes=VMEM_BYTES),
        cost_estimate=pl.CostEstimate(flops=5 * 10**9, bytes_accessed=20_000_000, transcendentals=0),
    )(flags, covariance, along, across, relaid, panels, lower, inverse, l10t)


def per_device(covariance, innovations, block_owner, panel_index, *, n_row, n_col):
    local_rows, local_cols = covariance.shape
    row_blocks, column_blocks = local_rows // B, local_cols // B
    r, c = lax.axis_index("row"), lax.axis_index("col")
    targets = panel_index[0] + jnp.arange(2, dtype=jnp.int32)
    positions = jnp.arange(block_owner.shape[0], dtype=jnp.int32)
    slot = jnp.sum(jnp.where(block_owner[None, :] == targets[:, None], positions[None, :], 0), axis=1)
    row_root, column_root = slot // row_blocks, slot // column_blocks
    row_slot, column_slot = slot % row_blocks, slot % column_blocks
    levels = jnp.sum((block_owner[:, None] > targets[None, :]).astype(jnp.int32), axis=1)
    steps = n_row // 4
    shift, core = c // 2, r % 2
    flags = jnp.concatenate(
        [
            shift[None],
            core[None],
            jnp.where(row_root == r, row_slot, -1),
            jnp.where(column_root == c, column_slot, -1),
            (row_slot + shift) % steps,
            lax.dynamic_slice_in_dim(levels, c * column_blocks, column_blocks),
            lax.dynamic_slice_in_dim(levels, r * row_blocks, row_blocks),
            column_root,
        ]
    ).astype(jnp.int32)
    across_axes = [
        (a * n_col + b, ((b // 2 + a // 4) % steps * 4 + b % 2 * 2 + a % 2) * n_col + a // 2)
        for a in range(n_row)
        for b in range(n_col)
    ]

    groups = lax.ppermute(jnp.transpose(innovations, (1, 0, 2)), ("row", "col"), across_axes)

    tiles = pick_tiles(block_owner, panel_index, covariance).reshape(n_row * n_col, 8, 128)
    tiles = lax.all_to_all(tiles, ("row", "col"), split_axis=0, concat_axis=0, tiled=True)
    source = jnp.where(c % 4 < 2, column_root[0], column_root[1])
    tiles = jnp.concatenate(
        [lax.dynamic_index_in_dim(tiles, row_root[n] * n_col + source, 0, keepdims=False) for n in range(2)], axis=0
    )
    tiles, groups = lax.optimization_barrier((tiles, groups))
    tiles = lax.all_to_all(
        jnp.broadcast_to(tiles[None], (n_row * n_col,) + tiles.shape),
        ("row", "col"),
        split_axis=0,
        concat_axis=0,
        tiled=True,
    )
    inverse, l10t, lower = factor_diagonal(tiles)

    picked = pick_columns(column_slot.astype(jnp.int32), covariance, n_col)
    picked, _ = lax.optimization_barrier((picked, tiles))
    parts = lax.all_to_all(picked, "col", split_axis=0, concat_axis=0, tiled=True)

    fold = innovations.shape[0] // 2
    wanted = [lax.dynamic_index_in_dim(groups, row_root[n], 0, keepdims=False) for n in range(2)]
    wanted = jnp.concatenate([w[h * fold : (h + 1) * fold] for h in range(2) for w in wanted], axis=1)
    high = lax.reduce_precision(wanted, 8, 7)
    middle = lax.reduce_precision(wanted - high, 8, 7)
    wanted = jnp.stack([high, middle, wanted - high - middle]).astype(BF16)

    along, across = solve_piece(flags, parts, inverse, l10t)
    across = lax.ppermute(across, ("row", "col"), across_axes)
    across = lax.all_gather(jnp.concatenate([across, wanted], axis=0), "row", axis=0)
    along = lax.all_to_all(along, "col", split_axis=0, concat_axis=0, tiled=True)
    along, groups = lax.optimization_barrier((along, groups))
    relaid = lax.all_to_all(groups, "row", split_axis=0, concat_axis=0, tiled=True)
    panels = solve_panels(flags, covariance, along, inverse, l10t)
    return update(flags, covariance, along, across, relaid, panels, lower, inverse, l10t)


def solution(mesh):
    placed = (P("row", "col"), P("row", None, "col"), P(), P())
    return jax.shard_map(
        functools.partial(per_device, n_row=mesh.shape["row"], n_col=mesh.shape["col"]),
        mesh=mesh,
        in_specs=placed,
        out_specs=(P("row", "col"), P("col", "row")),
        check_vma=False,
    )
```

```python
import functools

import jax
import jax.numpy as jnp
from jax import lax
from jax.experimental import pallas as pl
from jax.experimental.pallas import tpu as pltpu
from jax.sharding import PartitionSpec as P

B = 256
S = 64
VMEM_BYTES = 60 * 1024 * 1024
F32 = jnp.float32
BF16 = jnp.bfloat16
HIGH = lax.Precision.HIGHEST
VMEM_SPEC = pl.BlockSpec(memory_space=pltpu.VMEM)
SMEM_SPEC = pl.BlockSpec(memory_space=pltpu.SMEM)


def dot(a, b, dims, precision=None):
    return lax.dot_general(a, b, (dims, ((), ())), precision=precision, preferred_element_type=F32)


NN = ((1,), (0,))
NT = ((1,), (1,))
TN = ((0,), (0,))


def pick_kernel(slots, cov_ref, out_ref):
    parts, blocks, part, width = out_ref.shape
    for b in range(blocks):
        out_ref[:, b] = cov_ref[b * B : (b + 1) * B, :].reshape(parts, part, width)


def pick_columns(slots, covariance, parts):
    rows = covariance.shape[0]
    blocks = rows // B
    part = B // parts
    return pl.pallas_call(
        pick_kernel,
        grid_spec=pltpu.PrefetchScalarGridSpec(
            num_scalar_prefetch=1,
            grid=(2, blocks // 2),
            in_specs=[pl.BlockSpec((2 * B, B), lambda j, b, slots: (b, slots[j]))],
            out_specs=pl.BlockSpec((parts, 2, part, B), lambda j, b, slots: (0, b, 0, j)),
        ),
        out_shape=jax.ShapeDtypeStruct((parts, blocks, part, 2 * B), F32),
    )(slots, covariance)


def tiles_kernel(owner_ref, panel_ref, cov_ref, out_ref, held, arrived):
    slots = [jnp.int32(0), jnp.int32(0)]
    for place in range(owner_ref.shape[0]):
        for n in range(2):
            slots[n] = jnp.where(owner_ref[place] == panel_ref[0] + n, place, slots[n])
    row_blocks, column_blocks = cov_ref.shape[0] // B, cov_ref.shape[1] // B
    first_here = lax.div(slots[0], row_blocks) == lax.axis_index("row")
    row = lax.rem(jnp.where(first_here, slots[0], slots[1]), row_blocks)
    copies = []
    for n in range(2):
        column = lax.rem(slots[n], column_blocks)
        copies.append(
            pltpu.make_async_copy(
                cov_ref.at[pl.ds(pl.multiple_of(row * B, B), B), pl.ds(pl.multiple_of(column * B, B), B)],
                held.at[n],
                arrived.at[n],
            )
        )
        copies[n].start()
    for n in range(2):
        copies[n].wait()
        for i in range(B // 8):
            for j in range(2):
                out_ref[i, 2 * n + j] = held[n, 8 * i : 8 * i + 8, 128 * j : 128 * j + 128]


def pick_tiles(block_owner, panel_index, covariance):
    return pl.pallas_call(
        tiles_kernel,
        in_specs=[SMEM_SPEC, SMEM_SPEC, pl.BlockSpec(memory_space=pl.ANY)],
        out_specs=VMEM_SPEC,
        out_shape=jax.ShapeDtypeStruct((B // 8, 4, 8, 128), F32),
        scratch_shapes=[pltpu.VMEM((2, B, B), F32), pltpu.SemaphoreType.DMA((2,))],
    )(block_owner, panel_index, covariance)


def lanes(tile, j):
    return jnp.broadcast_to(tile[:, j : j + 1], (8, 128))


def eliminate(tiles):
    sub = lax.broadcasted_iota(jnp.int32, (8, 128), 0)
    scales = []
    for t in range(8):
        own = tiles[t]
        cols = [lanes(own, 8 * t + j) for j in range(8)]
        inv, cross = [], {}
        pivots = jnp.ones((8, 128), F32)
        for j in range(8):
            pivot = jnp.broadcast_to(cols[j][j : j + 1, :], (8, 128))
            pivots = jnp.where(sub == j, pivot, pivots)
            r = 1.0 / pivot
            inv.append(r)
            if j == 7:
                break
            m = jnp.where(sub > j, cols[j] * r, 0.0)
            for k in range(j + 1, 8):
                cross[j, k] = jnp.broadcast_to(cols[k][j : j + 1, :], (8, 128))
                cols[k] = cols[k] - m * cross[j, k]
            own = own - m * jnp.broadcast_to(own[j : j + 1, :], (8, 128))
        tiles[t] = own
        scales.append(lax.rsqrt(pivots))
        rows = [jnp.broadcast_to(own[j : j + 1, :], (8, 128)) for j in range(8)]
        for i in range(t + 1, 8):
            low = tiles[i]
            cols = [lanes(low, 8 * t + j) for j in range(8)]
            for j in range(8):
                m = cols[j] * inv[j]
                for k in range(j + 1, 8):
                    cols[k] = cols[k] - m * cross[j, k]
                low = low - m * rows[j]
            tiles[i] = low
    return tiles, scales


def factor_block(work, small, inverse_small):
    for b in range(B // S):
        lo, hi = b * S, (b + 1) * S
        small[:, 0:S] = work[lo:hi, lo:hi]
        row = lax.broadcasted_iota(jnp.int32, (S, S), 0)
        col = lax.broadcasted_iota(jnp.int32, (S, S), 1)
        small[:, S : 2 * S] = jnp.where(row == col, 1.0, 0.0)
        tiles, scales = eliminate([small[8 * i : 8 * i + 8, :] for i in range(8)])
        for i in range(8):
            small[8 * i : 8 * i + 8, :] = tiles[i] * scales[i]
        inverse_small[...] = small[:, S : 2 * S]
        top = dot(inverse_small[...], work[lo:hi, :], NN, HIGH)
        work[lo:hi, :] = top
        if hi < B:
            work[hi:B, :] = work[hi:B, :] - dot(top[:, hi:B], top, TN, HIGH)


def split(a):
    high = a.astype(BF16)
    rest = a - high.astype(F32)
    middle = rest.astype(BF16)
    return high, middle, (rest - middle.astype(F32)).astype(BF16)


def write_left(ref, a):
    high, middle, low = split(a)
    for n, term in enumerate((high, high, middle, high, low, middle)):
        ref[:, n * B : (n + 1) * B] = term


def write_right(ref, start, a):
    high, middle, low = split(a)
    for n, term in enumerate((high, middle, high, low, high, middle)):
        ref[:, start + n * B : start + (n + 1) * B] = term


def factor_kernel(tiles_ref, inverse_ref, l10t_ref, lower_ref, diag_ref, work, small, inverse_small):
    for i in range(B // 8):
        for j in range(4):
            diag_ref[8 * i : 8 * i + 8, 128 * j : 128 * j + 128] = tiles_ref[4 * i + j, 0:8]
        for j in range(2):
            diag_ref[8 * i : 8 * i + 8, 512 + 128 * j : 640 + 128 * j] = tiles_ref[4 * i + 2 + j, 8:16]
    row = lax.broadcasted_iota(jnp.int32, (B, B), 0)
    col = lax.broadcasted_iota(jnp.int32, (B, B), 1)
    eye = jnp.where(row == col, 1.0, 0.0)
    work[:, 0:B] = diag_ref[:, 0:B]
    work[:, B : 2 * B] = eye
    factor_block(work, small, inverse_small)
    x0 = work[:, B : 2 * B]
    write_right(inverse_ref, 0, x0)
    lower_ref[:, 0:B] = jnp.where(row <= col, work[:, 0:B], 0.0).T
    l10t = dot(x0, diag_ref[:, B : 2 * B], NN, HIGH).astype(BF16)
    l10t_ref[...] = l10t
    work[:, 0:B] = diag_ref[:, 2 * B : 3 * B] - dot(l10t, l10t, TN)
    work[:, B : 2 * B] = eye
    factor_block(work, small, inverse_small)
    write_right(inverse_ref, 6 * B, work[:, B : 2 * B])
    lower_ref[:, B : 2 * B] = jnp.where(row <= col, work[:, 0:B], 0.0).T


def factor_diagonal(tiles):
    return pl.pallas_call(
        factor_kernel,
        in_specs=[VMEM_SPEC],
        out_specs=[VMEM_SPEC] * 3,
        out_shape=[
            jax.ShapeDtypeStruct((B, 12 * B), BF16),
            jax.ShapeDtypeStruct((B, B), BF16),
            jax.ShapeDtypeStruct((B, 2 * B), F32),
        ],
        scratch_shapes=[
            pltpu.VMEM((B, 3 * B), F32),
            pltpu.VMEM((B, 2 * B), F32),
            pltpu.VMEM((S, 2 * S), F32),
            pltpu.VMEM((S, S), F32),
        ],
        compiler_params=pltpu.CompilerParams(vmem_limit_bytes=VMEM_BYTES),
        cost_estimate=pl.CostEstimate(flops=2 * 10**10, bytes_accessed=80_000_000, transcendentals=0),
    )(tiles)


def solve_rows(first, second, wide, inverse_ref, l10t_ref):
    write_left(wide, first)
    p0 = dot(wide[...], inverse_ref[:, 0 : 6 * B], NT)
    write_left(wide, second - dot(p0.astype(BF16), l10t_ref[...], NN))
    p1 = dot(wide[...], inverse_ref[:, 6 * B : 12 * B], NT)
    return p0, p1


def piece_kernel(flags, first_ref, second_ref, inverse_ref, l10t_ref, along_ref, across_ref, wide):
    blocks, part = first_ref.shape[1:3]
    solved = solve_rows(
        first_ref[0].reshape(blocks * part, B), second_ref[0].reshape(blocks * part, B), wide, inverse_ref, l10t_ref
    )
    for panel, p in enumerate(solved):
        cut = slice(panel * B, (panel + 1) * B)
        for b in range(blocks):
            mine = p[b * part : (b + 1) * part].astype(BF16)
            mine = jnp.where(flags[16 + b] > panel, mine, jnp.zeros_like(mine))
            across_ref[b, :, cut] = mine
            for q in range(along_ref.shape[0]):
                along_ref[q, b, :, cut] = mine


def solve_piece(flags, parts, inverse, l10t):
    count, blocks, part = parts.shape[:3]
    return pl.pallas_call(
        piece_kernel,
        grid_spec=pltpu.PrefetchScalarGridSpec(
            num_scalar_prefetch=1,
            grid=(1,),
            in_specs=[
                pl.BlockSpec((1, blocks, part, B), lambda i, flags: (flags[20], 0, 0, 0)),
                pl.BlockSpec((1, blocks, part, B), lambda i, flags: (flags[21], 0, 0, 1)),
                whole(*inverse.shape),
                whole(*l10t.shape),
            ],
            out_specs=[whole(count, blocks, part, 2 * B), whole(blocks, part, 2 * B)],
            scratch_shapes=[pltpu.VMEM((blocks * part, 6 * B), BF16)],
        ),
        out_shape=[
            jax.ShapeDtypeStruct((count, blocks, part, 2 * B), BF16),
            jax.ShapeDtypeStruct((blocks, part, 2 * B), BF16),
        ],
        compiler_params=pltpu.CompilerParams(vmem_limit_bytes=VMEM_BYTES),
        cost_estimate=pl.CostEstimate(flops=10**9, bytes_accessed=4_000_000, transcendentals=0),
    )(flags, parts, parts, inverse, l10t)


def whole(*shape):
    return pl.BlockSpec(shape, lambda i, flags: (0,) * len(shape))


def panel_kernel(flags, first_ref, second_ref, along_ref, inverse_ref, l10t_ref, out_ref, wide):
    level = flags[16 + pl.program_id(0)]
    parts, _, part = along_ref.shape[:3]

    @pl.when(flags[4] >= 0)
    def _():
        write_left(wide, first_ref[...])
        p = dot(wide[...], inverse_ref[:, 0 : 6 * B], NT)
        out_ref[:, 0:B] = jnp.where(level > 0, p, 0.0)

    @pl.when(flags[5] >= 0)
    def _():
        before = along_ref[:, 0, :, 0:B].reshape(parts * part, B)
        write_left(wide, second_ref[...] - dot(before, l10t_ref[...], NN))
        p = dot(wide[...], inverse_ref[:, 6 * B : 12 * B], NT)
        out_ref[:, B : 2 * B] = jnp.where(level > 1, p, 0.0)


def solve_panels(flags, covariance, along, inverse, l10t):
    rows = covariance.shape[0]
    parts, blocks, part, width = along.shape
    return pl.pallas_call(
        panel_kernel,
        grid_spec=pltpu.PrefetchScalarGridSpec(
            num_scalar_prefetch=1,
            grid=(blocks,),
            in_specs=[
                pl.BlockSpec((B, B), lambda i, flags: (i, jnp.maximum(flags[4], 0))),
                pl.BlockSpec((B, B), lambda i, flags: (i, jnp.maximum(flags[5], 0))),
                pl.BlockSpec((parts, 1, part, width), lambda i, flags: (0, i, 0, 0)),
                whole(*inverse.shape),
                whole(*l10t.shape),
            ],
            out_specs=pl.BlockSpec((B, 2 * B), lambda i, flags: (i, 0)),
            scratch_shapes=[pltpu.VMEM((B, 6 * B), BF16)],
        ),
        out_shape=jax.ShapeDtypeStruct((rows, 2 * B), F32),
        compiler_params=pltpu.CompilerParams(vmem_limit_bytes=VMEM_BYTES),
        cost_estimate=pl.CostEstimate(flops=10**9, bytes_accessed=4_000_000, transcendentals=0),
    )(flags, covariance, covariance, along, inverse, l10t)


def white_kernel(flags, exchanged_ref, inverse_ref, l10t_ref, white_ref, wide):
    half = white_ref.shape[0] // 2
    for panel in range(2):
        for h in range(2):
            for parity in range(2):
                there = (
                    slice(parity * half, (parity + 1) * half),
                    slice(panel * B + h * 128, panel * B + (h + 1) * 128),
                )
                white_ref[there] = exchanged_ref[
                    4 * flags[6 + panel] + 2 * h + parity, (1 + panel) * half : (2 + panel) * half, :
                ]
    w0, w1 = solve_rows(white_ref[:, 0:B], white_ref[:, B : 2 * B], wide, inverse_ref, l10t_ref)
    white_ref[:, 0:B] = w0
    white_ref[:, B : 2 * B] = w1


def solve_white(flags, exchanged, inverse, l10t):
    particles = exchanged.shape[1] // 3 * 2
    return pl.pallas_call(
        white_kernel,
        in_specs=[SMEM_SPEC] + [VMEM_SPEC] * 3,
        out_specs=VMEM_SPEC,
        out_shape=jax.ShapeDtypeStruct((particles, 2 * B), F32),
        scratch_shapes=[pltpu.VMEM((particles, 6 * B), BF16)],
        compiler_params=pltpu.CompilerParams(vmem_limit_bytes=VMEM_BYTES),
        cost_estimate=pl.CostEstimate(flops=10**9, bytes_accessed=4_000_000, transcendentals=0),
    )(flags, exchanged, inverse, l10t)


def update_kernel(
    flags,
    cov_ref,
    along_ref,
    across_ref,
    relaid_ref,
    panel_ref,
    lower_ref,
    white_ref,
    out_ref,
    solved_ref,
    columns,
    arrived,
):
    i = pl.program_id(0)
    parts, _, part = along_ref.shape[:3]
    blocks = across_ref.shape[1]
    steps = parts // 2
    column_blocks = 2 * blocks
    half = relaid_ref.shape[1]

    @pl.when(i == 0)
    def _():
        copies = []
        for q in range(parts):
            first = 4 * lax.rem(q // 2 + flags[0], steps) + 2 * (q % 2)
            for parity in range(2):
                source = across_ref.at[first + parity]
                copies.append(pltpu.make_async_copy(source, columns.at[parity, :, q], arrived.at[len(copies)]))
        for copy in copies:
            copy.start()
        for copy in copies:
            copy.wait()

    level = flags[16 + i]
    own = along_ref[:, 0].reshape(parts * part, 2 * B)
    for n in range(column_blocks):
        cut = slice(n * B, (n + 1) * B)
        out_ref[:, cut] = cov_ref[:, cut] - dot(own, columns[n // blocks, n % blocks].reshape(B, 2 * B), NT)

    for panel in range(2):
        is_row = i == flags[2 + panel]
        for n in range(column_blocks):

            @pl.when(is_row & (flags[8 + n] > panel))
            def _():
                out_ref[:, n * B : (n + 1) * B] = jnp.zeros((B, B), F32)

        column = flags[4 + panel]
        place = pl.ds(pl.multiple_of(jnp.maximum(column, 0) * B, B), B)

        @pl.when((column >= 0) & (level > panel))
        def _():
            out_ref[:, place] = panel_ref[:, panel * B : (panel + 1) * B]

        @pl.when((column >= 0) & is_row)
        def _():
            out_ref[:, place] = lower_ref[:, panel * B : (panel + 1) * B]

    product = dot(white_ref[...].astype(BF16), own, NT)
    for parity in range(2):
        for h in range(2):
            there = (slice(parity * half, (parity + 1) * half), slice(h * 128, (h + 1) * 128))
            solved_ref[there] = relaid_ref[2 * h + parity] - product[there]
    for panel in range(2):

        @pl.when(i == flags[2 + panel])
        def _():
            solved_ref[...] = white_ref[:, panel * B : (panel + 1) * B]


def update(flags, covariance, along, across, exchanged, panels, lower, white):
    rows, columns = covariance.shape
    parts, blocks, part, width = along.shape
    half = white.shape[0] // 2
    return pl.pallas_call(
        update_kernel,
        grid_spec=pltpu.PrefetchScalarGridSpec(
            num_scalar_prefetch=1,
            grid=(blocks,),
            in_specs=[
                pl.BlockSpec((B, columns), lambda i, flags: (i, 0)),
                pl.BlockSpec((parts, 1, part, width), lambda i, flags: (0, i, 0, 0)),
                pl.BlockSpec(memory_space=pl.ANY),
                pl.BlockSpec((4, half, 128), lambda i, flags: (lax.rem(i + flags[0], blocks), 0, 0)),
                pl.BlockSpec((B, width), lambda i, flags: (jnp.where((flags[4] & flags[5]) >= 0, i, 0), 0)),
                whole(*lower.shape),
                whole(*white.shape),
            ],
            out_specs=[
                pl.BlockSpec((B, columns), lambda i, flags: (i, 0)),
                pl.BlockSpec((2 * half, B), lambda i, flags: (0, i)),
            ],
            scratch_shapes=[
                pltpu.VMEM((2, columns // (2 * B), parts, part, width), BF16),
                pltpu.SemaphoreType.DMA((2 * parts,)),
            ],
        ),
        out_shape=[jax.ShapeDtypeStruct((rows, columns), F32), jax.ShapeDtypeStruct((2 * half, rows), F32)],
        compiler_params=pltpu.CompilerParams(vmem_limit_bytes=VMEM_BYTES),
        cost_estimate=pl.CostEstimate(flops=5 * 10**9, bytes_accessed=20_000_000, transcendentals=0),
    )(flags, covariance, along, across, exchanged, panels, lower, white)


def per_device(covariance, innovations, block_owner, panel_index, *, n_row, n_col):
    local_rows, local_cols = covariance.shape
    row_blocks, column_blocks = local_rows // B, local_cols // B
    r, c = lax.axis_index("row"), lax.axis_index("col")
    targets = panel_index[0] + jnp.arange(2, dtype=jnp.int32)
    positions = jnp.arange(block_owner.shape[0], dtype=jnp.int32)
    slot = jnp.sum(jnp.where(block_owner[None, :] == targets[:, None], positions[None, :], 0), axis=1)
    row_root, column_root = slot // row_blocks, slot // column_blocks
    row_slot, column_slot = slot % row_blocks, slot % column_blocks
    levels = jnp.sum((block_owner[:, None] > targets[None, :]).astype(jnp.int32), axis=1)
    steps = n_row // 4
    shift, core = c // 2, r % 2
    flags = jnp.concatenate(
        [
            shift[None],
            core[None],
            jnp.where(row_root == r, row_slot, -1),
            jnp.where(column_root == c, column_slot, -1),
            (row_slot + shift) % steps,
            lax.dynamic_slice_in_dim(levels, c * column_blocks, column_blocks),
            lax.dynamic_slice_in_dim(levels, r * row_blocks, row_blocks),
            column_root,
        ]
    ).astype(jnp.int32)
    across_axes = [
        (a * n_col + b, ((b // 2 + a // 4) % steps * 4 + b % 2 * 2 + a % 2) * n_col + a // 2)
        for a in range(n_row)
        for b in range(n_col)
    ]

    groups = lax.ppermute(jnp.transpose(innovations, (1, 0, 2)), ("row", "col"), across_axes)

    tiles = pick_tiles(block_owner, panel_index, covariance).reshape(n_row * n_col, 8, 128)
    tiles = lax.all_to_all(tiles, ("row", "col"), split_axis=0, concat_axis=0, tiled=True)
    source = jnp.where(c % 4 < 2, column_root[0], column_root[1])
    tiles = jnp.concatenate(
        [lax.dynamic_index_in_dim(tiles, row_root[n] * n_col + source, 0, keepdims=False) for n in range(2)], axis=0
    )
    tiles = lax.all_to_all(
        jnp.broadcast_to(tiles[None], (n_row * n_col,) + tiles.shape),
        ("row", "col"),
        split_axis=0,
        concat_axis=0,
        tiled=True,
    )
    tiles, groups = lax.optimization_barrier((tiles, groups))
    inverse, l10t, lower = factor_diagonal(tiles)

    picked = pick_columns(column_slot.astype(jnp.int32), covariance, n_col)
    picked, _ = lax.optimization_barrier((picked, tiles))
    parts = lax.all_to_all(picked, "col", split_axis=0, concat_axis=0, tiled=True)

    along, across = solve_piece(flags, parts, inverse, l10t)
    turned = lax.ppermute(across, ("row", "col"), across_axes)
    gathered = lax.all_gather(turned, "row", axis=0)

    wanted = [lax.dynamic_index_in_dim(groups, row_root[n], 0, keepdims=False) for n in range(2)]
    wanted = jnp.concatenate(wanted, axis=0)
    sent = jnp.concatenate([groups, jnp.broadcast_to(wanted[None], (n_row,) + wanted.shape)], axis=1)
    sent, _ = lax.optimization_barrier((sent, across))
    exchanged = lax.all_to_all(sent, "row", split_axis=0, concat_axis=0, tiled=True)
    along, exchanged = lax.optimization_barrier((along, exchanged))
    along = lax.all_to_all(along, "col", split_axis=0, concat_axis=0, tiled=True)

    white = solve_white(flags, exchanged, inverse, l10t)
    panels = solve_panels(flags, covariance, along, inverse, l10t)
    return update(flags, covariance, along, gathered, exchanged, panels, lower, white)


def solution(mesh):
    placed = (P("row", "col"), P("row", None, "col"), P(), P())
    return jax.shard_map(
        functools.partial(per_device, n_row=mesh.shape["row"], n_col=mesh.shape["col"]),
        mesh=mesh,
        in_specs=placed,
        out_specs=(P("row", "col"), P("col", "row")),
        check_vma=False,
    )
```

```python
import functools

import jax
import jax.numpy as jnp
from jax import lax
from jax.experimental import pallas as pl
from jax.experimental.pallas import tpu as pltpu
from jax.sharding import PartitionSpec as P

B = 256
S = 64
VMEM_BYTES = 60 * 1024 * 1024
F32 = jnp.float32
BF16 = jnp.bfloat16
HIGH = lax.Precision.HIGHEST
VMEM_SPEC = pl.BlockSpec(memory_space=pltpu.VMEM)
SMEM_SPEC = pl.BlockSpec(memory_space=pltpu.SMEM)


def dot(a, b, dims, precision=None):
    return lax.dot_general(a, b, (dims, ((), ())), precision=precision, preferred_element_type=F32)


NN = ((1,), (0,))
NT = ((1,), (1,))
TN = ((0,), (0,))


def pick_kernel(slots, cov_ref, out_ref):
    parts, blocks, part, width = out_ref.shape
    for b in range(blocks):
        out_ref[:, b] = cov_ref[b * B : (b + 1) * B, :].reshape(parts, part, width)


def pick_columns(slots, covariance, parts):
    rows = covariance.shape[0]
    blocks = rows // B
    part = B // parts
    return pl.pallas_call(
        pick_kernel,
        grid_spec=pltpu.PrefetchScalarGridSpec(
            num_scalar_prefetch=1,
            grid=(2, blocks // 2),
            in_specs=[pl.BlockSpec((2 * B, B), lambda j, b, slots: (b, slots[j]))],
            out_specs=pl.BlockSpec((parts, 2, part, B), lambda j, b, slots: (0, b, 0, j)),
        ),
        out_shape=jax.ShapeDtypeStruct((parts, blocks, part, 2 * B), F32),
    )(slots, covariance)


def lanes(tile, j):
    return jnp.broadcast_to(tile[:, j : j + 1], (8, 128))


def eliminate(tiles):
    sub = lax.broadcasted_iota(jnp.int32, (8, 128), 0)
    scales = []
    for t in range(8):
        own = tiles[t]
        cols = [lanes(own, 8 * t + j) for j in range(8)]
        inv, cross = [], {}
        pivots = jnp.ones((8, 128), F32)
        for j in range(8):
            pivot = jnp.broadcast_to(cols[j][j : j + 1, :], (8, 128))
            pivots = jnp.where(sub == j, pivot, pivots)
            r = 1.0 / pivot
            inv.append(r)
            if j == 7:
                break
            m = jnp.where(sub > j, cols[j] * r, 0.0)
            for k in range(j + 1, 8):
                cross[j, k] = jnp.broadcast_to(cols[k][j : j + 1, :], (8, 128))
                cols[k] = cols[k] - m * cross[j, k]
            own = own - m * jnp.broadcast_to(own[j : j + 1, :], (8, 128))
        tiles[t] = own
        scales.append(lax.rsqrt(pivots))
        rows = [jnp.broadcast_to(own[j : j + 1, :], (8, 128)) for j in range(8)]
        for i in range(t + 1, 8):
            low = tiles[i]
            cols = [lanes(low, 8 * t + j) for j in range(8)]
            for j in range(8):
                m = cols[j] * inv[j]
                for k in range(j + 1, 8):
                    cols[k] = cols[k] - m * cross[j, k]
                low = low - m * rows[j]
            tiles[i] = low
    return tiles, scales


def factor_block(work, small, inverse_small):
    for b in range(B // S):
        lo, hi = b * S, (b + 1) * S
        small[:, 0:S] = work[lo:hi, lo:hi]
        row = lax.broadcasted_iota(jnp.int32, (S, S), 0)
        col = lax.broadcasted_iota(jnp.int32, (S, S), 1)
        small[:, S : 2 * S] = jnp.where(row == col, 1.0, 0.0)
        tiles, scales = eliminate([small[8 * i : 8 * i + 8, :] for i in range(8)])
        for i in range(8):
            small[8 * i : 8 * i + 8, :] = tiles[i] * scales[i]
        inverse_small[...] = small[:, S : 2 * S]
        top = dot(inverse_small[...], work[lo:hi, :], NN, HIGH)
        work[lo:hi, :] = top
        if hi < B:
            work[hi:B, :] = work[hi:B, :] - dot(top[:, hi:B], top, TN, HIGH)


def split(a):
    high = a.astype(BF16)
    rest = a - high.astype(F32)
    middle = rest.astype(BF16)
    return high, middle, (rest - middle.astype(F32)).astype(BF16)


def write_left(ref, a):
    high, middle, low = split(a)
    for n, term in enumerate((high, high, middle, high, low, middle)):
        ref[:, n * B : (n + 1) * B] = term


def write_right(ref, start, a):
    high, middle, low = split(a)
    for n, term in enumerate((high, middle, high, low, high, middle)):
        ref[:, start + n * B : start + (n + 1) * B] = term


def factor_kernel(flags, near_ref, far_ref, inverse_ref, l10t_ref, lower_ref, diag_ref, work, small, inverse_small):
    parts, part = near_ref.shape[:2]
    for ref, first in ((near_ref, flags[1] * part), (far_ref, (1 - flags[1]) * part)):
        for q in range(parts):
            diag_ref[pl.ds(pl.multiple_of(q * 2 * part + first, part), part), :] = ref[q]
    row = lax.broadcasted_iota(jnp.int32, (B, B), 0)
    col = lax.broadcasted_iota(jnp.int32, (B, B), 1)
    eye = jnp.where(row == col, 1.0, 0.0)
    work[:, 0:B] = diag_ref[:, 0:B]
    work[:, B : 2 * B] = eye
    factor_block(work, small, inverse_small)
    x0 = work[:, B : 2 * B]
    write_right(inverse_ref, 0, x0)
    lower_ref[:, 0:B] = jnp.where(row <= col, work[:, 0:B], 0.0).T
    l10t = dot(x0, diag_ref[:, B : 2 * B], NN, HIGH).astype(BF16)
    l10t_ref[...] = l10t
    work[:, 0:B] = diag_ref[:, 2 * B : 3 * B] - dot(l10t, l10t, TN)
    work[:, B : 2 * B] = eye
    factor_block(work, small, inverse_small)
    write_right(inverse_ref, 6 * B, work[:, B : 2 * B])
    lower_ref[:, B : 2 * B] = jnp.where(row <= col, work[:, 0:B], 0.0).T


def factor_diagonal(flags, near, far):
    return pl.pallas_call(
        factor_kernel,
        in_specs=[SMEM_SPEC] + [VMEM_SPEC] * 2,
        out_specs=[VMEM_SPEC] * 3,
        out_shape=[
            jax.ShapeDtypeStruct((B, 12 * B), BF16),
            jax.ShapeDtypeStruct((B, B), BF16),
            jax.ShapeDtypeStruct((B, 2 * B), F32),
        ],
        scratch_shapes=[
            pltpu.VMEM((B, 3 * B), F32),
            pltpu.VMEM((B, 2 * B), F32),
            pltpu.VMEM((S, 2 * S), F32),
            pltpu.VMEM((S, S), F32),
        ],
        compiler_params=pltpu.CompilerParams(vmem_limit_bytes=VMEM_BYTES),
        cost_estimate=pl.CostEstimate(flops=2 * 10**10, bytes_accessed=80_000_000, transcendentals=0),
    )(flags, near, far)


def solve_rows(first, second, wide, inverse_ref, l10t_ref):
    write_left(wide, first)
    p0 = dot(wide[...], inverse_ref[:, 0 : 6 * B], NT)
    write_left(wide, second - dot(p0.astype(BF16), l10t_ref[...], NN))
    p1 = dot(wide[...], inverse_ref[:, 6 * B : 12 * B], NT)
    return p0, p1


def across_kernel(flags, across_ref, inverse_ref, l10t_ref, pc_ref, white_ref, raw, wide, wide_white):
    k = pl.program_id(0)
    part = pc_ref.shape[3]
    blocks = pc_ref.shape[1]
    held = blocks * part
    half = raw.shape[0] // 2
    fold = half // 2

    p0, p1 = solve_rows(
        across_ref[:, 0:held, 0:B].reshape(4 * held, B),
        across_ref[:, 0:held, B : 2 * B].reshape(4 * held, B),
        wide,
        inverse_ref,
        l10t_ref,
    )
    p0, p1 = p0.astype(BF16), p1.astype(BF16)
    for n in range(4):
        h, parity = n // 2, n % 2
        for b in range(blocks):
            here = slice(n * held + b * part, n * held + (b + 1) * part)
            level = flags[8 + parity * blocks + b]
            pc_ref[parity, b, h, :, 0:B] = jnp.where(level > 0, p0[here], jnp.zeros_like(p0[here]))
            pc_ref[parity, b, h, :, B : 2 * B] = jnp.where(level > 1, p1[here], jnp.zeros_like(p1[here]))

    for panel in range(2):

        @pl.when(k == flags[6 + panel])
        def _():
            for n in range(4):
                h, parity = n // 2, n % 2
                for f in range(2):
                    lane = (2 * f + panel) * 128
                    raw[
                        parity * half + f * fold : parity * half + (f + 1) * fold,
                        panel * B + h * 128 : panel * B + (h + 1) * 128,
                    ] = across_ref[n, held : held + fold, lane : lane + 128]

    @pl.when(k == pl.num_programs(0) - 1)
    def _():
        w0, w1 = solve_rows(raw[:, 0:B], raw[:, B : 2 * B], wide_white, inverse_ref, l10t_ref)
        white_ref[:, 0:B] = w0
        white_ref[:, B : 2 * B] = w1


def whole(*shape):
    return pl.BlockSpec(shape, lambda i, flags: (0,) * len(shape))


def solve_across(flags, across, inverse, l10t, blocks, parts, particles):
    part = B // parts
    steps = across.shape[0] // 4
    return pl.pallas_call(
        across_kernel,
        grid_spec=pltpu.PrefetchScalarGridSpec(
            num_scalar_prefetch=1,
            grid=(steps,),
            in_specs=[
                pl.BlockSpec((4,) + across.shape[1:], lambda k, flags: (k, 0, 0)),
                whole(*inverse.shape),
                whole(*l10t.shape),
            ],
            out_specs=[
                pl.BlockSpec(
                    (2, blocks, 2, part, 2 * B), lambda k, flags: (0, 0, lax.rem(k + steps - flags[0], steps), 0, 0)
                ),
                whole(particles, 2 * B),
            ],
            scratch_shapes=[
                pltpu.VMEM((particles, 2 * B), F32),
                pltpu.VMEM((4 * blocks * part, 6 * B), BF16),
                pltpu.VMEM((particles, 6 * B), BF16),
            ],
        ),
        out_shape=[
            jax.ShapeDtypeStruct((2, blocks, parts, part, 2 * B), BF16),
            jax.ShapeDtypeStruct((particles, 2 * B), F32),
        ],
        compiler_params=pltpu.CompilerParams(vmem_limit_bytes=VMEM_BYTES),
        cost_estimate=pl.CostEstimate(flops=6 * 10**9, bytes_accessed=8_000_000, transcendentals=0),
    )(flags, across, inverse, l10t)


def rows_kernel(flags, along_ref, inverse_ref, l10t_ref, panel_ref, rows_ref, wide):
    level = flags[16 + pl.program_id(0)]
    parts, _, part = along_ref.shape[:3]
    raw = along_ref[:, 0].reshape(parts * part, 2 * B)
    for panel, p in enumerate(solve_rows(raw[:, 0:B], raw[:, B : 2 * B], wide, inverse_ref, l10t_ref)):
        cut = slice(panel * B, (panel + 1) * B)
        p = jnp.where(level > panel, p, 0.0)
        panel_ref[:, cut] = p
        rows_ref[:, cut] = p.astype(BF16)


def solve_own(flags, along, inverse, l10t):
    parts, blocks, part, width = along.shape
    here = pl.BlockSpec((B, width), lambda i, flags: (i, 0))
    return pl.pallas_call(
        rows_kernel,
        grid_spec=pltpu.PrefetchScalarGridSpec(
            num_scalar_prefetch=1,
            grid=(blocks,),
            in_specs=[
                pl.BlockSpec((parts, 1, part, width), lambda i, flags: (0, i, 0, 0)),
                whole(*inverse.shape),
                whole(*l10t.shape),
            ],
            out_specs=[here, here],
            scratch_shapes=[pltpu.VMEM((B, 6 * B), BF16)],
        ),
        out_shape=[
            jax.ShapeDtypeStruct((blocks * B, width), F32),
            jax.ShapeDtypeStruct((blocks * B, width), BF16),
        ],
        compiler_params=pltpu.CompilerParams(vmem_limit_bytes=VMEM_BYTES),
        cost_estimate=pl.CostEstimate(flops=2 * 10**9, bytes_accessed=4_000_000, transcendentals=0),
    )(flags, along, inverse, l10t)


def update_kernel(
    flags, cov_ref, rows_ref, columns_ref, relaid_ref, white_ref, panel_ref, lower_ref, out_ref, solved_ref
):
    i = pl.program_id(0)
    column_blocks = columns_ref.shape[0] // B
    half = relaid_ref.shape[1]

    level = flags[16 + i]
    own = rows_ref[...]
    for n in range(column_blocks):
        cut = slice(n * B, (n + 1) * B)
        out_ref[:, cut] = cov_ref[:, cut] - dot(own, columns_ref[cut, :], NT)

    for panel in range(2):
        is_row = i == flags[2 + panel]
        for n in range(column_blocks):

            @pl.when(is_row & (flags[8 + n] > panel))
            def _():
                out_ref[:, n * B : (n + 1) * B] = jnp.zeros((B, B), F32)

        column = flags[4 + panel]
        place = pl.ds(pl.multiple_of(jnp.maximum(column, 0) * B, B), B)

        @pl.when((column >= 0) & (level > panel))
        def _():
            out_ref[:, place] = panel_ref[:, panel * B : (panel + 1) * B]

        @pl.when((column >= 0) & is_row)
        def _():
            out_ref[:, place] = lower_ref[:, panel * B : (panel + 1) * B]

    product = dot(white_ref[...].astype(BF16), own, NT)
    for parity in range(2):
        for h in range(2):
            there = (slice(parity * half, (parity + 1) * half), slice(h * 128, (h + 1) * 128))
            solved_ref[there] = relaid_ref[2 * h + parity] - product[there]
    for panel in range(2):

        @pl.when(i == flags[2 + panel])
        def _():
            solved_ref[...] = white_ref[:, panel * B : (panel + 1) * B]


def update(flags, covariance, own, across, relaid, white, panels, lower):
    rows, columns = covariance.shape
    width = own.shape[1]
    blocks = rows // B
    half = relaid.shape[1]
    return pl.pallas_call(
        update_kernel,
        grid_spec=pltpu.PrefetchScalarGridSpec(
            num_scalar_prefetch=1,
            grid=(blocks,),
            in_specs=[
                pl.BlockSpec((B, columns), lambda i, flags: (i, 0)),
                pl.BlockSpec((B, width), lambda i, flags: (i, 0)),
                whole(*across.shape),
                pl.BlockSpec((4, half, 128), lambda i, flags: (lax.rem(i + flags[0], blocks), 0, 0)),
                whole(*white.shape),
                pl.BlockSpec((B, width), lambda i, flags: (jnp.where((flags[4] & flags[5]) >= 0, i, 0), 0)),
                whole(*lower.shape),
            ],
            out_specs=[
                pl.BlockSpec((B, columns), lambda i, flags: (i, 0)),
                pl.BlockSpec((2 * half, B), lambda i, flags: (0, i)),
            ],
        ),
        out_shape=[jax.ShapeDtypeStruct((rows, columns), F32), jax.ShapeDtypeStruct((2 * half, rows), F32)],
        compiler_params=pltpu.CompilerParams(vmem_limit_bytes=VMEM_BYTES),
        cost_estimate=pl.CostEstimate(flops=5 * 10**9, bytes_accessed=20_000_000, transcendentals=0),
    )(flags, covariance, own, across, relaid, white, panels, lower)


def per_device(covariance, innovations, block_owner, panel_index, *, n_row, n_col):
    local_rows, local_cols = covariance.shape
    row_blocks, column_blocks = local_rows // B, local_cols // B
    r, c = lax.axis_index("row"), lax.axis_index("col")
    targets = panel_index[0] + jnp.arange(2, dtype=jnp.int32)
    positions = jnp.arange(block_owner.shape[0], dtype=jnp.int32)
    slot = jnp.sum(jnp.where(block_owner[None, :] == targets[:, None], positions[None, :], 0), axis=1)
    row_root, column_root = slot // row_blocks, slot // column_blocks
    row_slot, column_slot = slot % row_blocks, slot % column_blocks
    levels = jnp.sum((block_owner[:, None] > targets[None, :]).astype(jnp.int32), axis=1)
    steps = n_row // 4
    shift, core = c // 2, r % 2
    pairs = [(a, a ^ 1) for a in range(n_row)]
    same_core = [[a for a in range(n_row) if a % 2 == k] for k in range(2)]
    flags = jnp.concatenate(
        [
            shift[None],
            core[None],
            jnp.where(row_root == r, row_slot, -1),
            jnp.where(column_root == c, column_slot, -1),
            (row_slot + shift) % steps,
            lax.dynamic_slice_in_dim(levels, c * column_blocks, column_blocks),
            lax.dynamic_slice_in_dim(levels, r * row_blocks, row_blocks),
        ]
    ).astype(jnp.int32)
    across_axes = [
        (a * n_col + b, ((b // 2 + a // 4) % steps * 4 + b % 2 * 2 + a % 2) * n_col + a // 2)
        for a in range(n_row)
        for b in range(n_col)
    ]

    picked = pick_columns(column_slot.astype(jnp.int32), covariance, n_col)
    parts = lax.all_to_all(picked, "col", split_axis=0, concat_axis=0, tiled=True)
    part = parts.shape[2]
    piece = jnp.concatenate(
        [
            lax.dynamic_slice(parts, (column_root[n], 0, 0, n * B), (1, row_blocks, part, B))[0]
            for n in range(2)
        ],
        axis=-1,
    )

    chosen = jnp.where(r == row_root[0], row_slot[0], row_slot[1])
    mine = lax.dynamic_index_in_dim(piece, chosen, 0, keepdims=False)
    half = part // 2
    kept = lax.dynamic_slice_in_dim(mine, core * half, half, 0)
    given = lax.ppermute(lax.dynamic_slice_in_dim(mine, (1 - core) * half, half, 0), "row", pairs)
    both = jnp.concatenate([jnp.where(core == 0, kept, given), jnp.where(core == 0, given, kept)], axis=0)

    fold = innovations.shape[0] // 2
    wanted = [lax.dynamic_index_in_dim(innovations, row_root[n], 1, keepdims=False) for n in range(2)]
    wanted = jnp.concatenate([w[h * fold : (h + 1) * fold] for h in range(2) for w in wanted], axis=1)
    payload = jnp.concatenate([piece.reshape(row_blocks * part, 2 * B), wanted], axis=0)
    payload, both = lax.optimization_barrier((payload, both))
    payload = lax.ppermute(payload, ("row", "col"), across_axes)

    spread = lax.all_to_all(
        jnp.broadcast_to(both[None], (n_row // 2,) + both.shape),
        "row",
        split_axis=0,
        concat_axis=0,
        tiled=True,
        axis_index_groups=same_core,
    )
    upper = lax.dynamic_slice(spread, (row_root[0] // 2, row_root[0] % 2 * half, 0), (1, half, 2 * B))[0]
    lower = lax.dynamic_slice(spread, (row_root[1] // 2, row_root[1] % 2 * half, B), (1, half, B))[0]
    strip = jnp.concatenate([upper, lower], axis=-1)
    near = lax.all_to_all(
        jnp.broadcast_to(strip[None], (n_col,) + strip.shape), "col", split_axis=0, concat_axis=0, tiled=True
    )
    far = lax.ppermute(near, "row", pairs)

    payload, _ = lax.optimization_barrier((payload, near))
    across = lax.all_gather(payload, "row", axis=0)

    inverse, l10t, lower = factor_diagonal(flags, near, far)

    along = lax.all_to_all(
        jnp.broadcast_to(piece[None], (n_col,) + piece.shape), "col", split_axis=0, concat_axis=0, tiled=True
    )

    groups, _ = lax.optimization_barrier((jnp.transpose(innovations, (1, 0, 2)), near))
    turned = lax.ppermute(groups, ("row", "col"), across_axes)
    inverse, turned = lax.optimization_barrier((inverse, turned))
    turned, _ = lax.optimization_barrier((turned, along))
    relaid = lax.all_to_all(turned, "row", split_axis=0, concat_axis=0, tiled=True)

    panels, own = solve_own(flags, along, inverse, l10t)
    columns, white = solve_across(flags, across, inverse, l10t, row_blocks, n_col, 2 * innovations.shape[0])
    return update(
        flags, covariance, own, columns.reshape(local_cols, 2 * B), relaid, white, panels, lower
    )


def solution(mesh):
    placed = (P("row", "col"), P("row", None, "col"), P(), P())
    return jax.shard_map(
        functools.partial(per_device, n_row=mesh.shape["row"], n_col=mesh.shape["col"]),
        mesh=mesh,
        in_specs=placed,
        out_specs=(P("row", "col"), P("col", "row")),
        check_vma=False,
    )
```

```python
import functools

import jax
import jax.numpy as jnp
from jax import lax
from jax.experimental import pallas as pl
from jax.experimental.pallas import tpu as pltpu
from jax.sharding import PartitionSpec as P

B = 256
S = 64
VMEM_BYTES = 60 * 1024 * 1024
F32 = jnp.float32
BF16 = jnp.bfloat16
HIGH = lax.Precision.HIGHEST
VMEM_SPEC = pl.BlockSpec(memory_space=pltpu.VMEM)
SMEM_SPEC = pl.BlockSpec(memory_space=pltpu.SMEM)


def dot(a, b, dims, precision=None):
    return lax.dot_general(a, b, (dims, ((), ())), precision=precision, preferred_element_type=F32)


NN = ((1,), (0,))
NT = ((1,), (1,))
TN = ((0,), (0,))


def pick_kernel(slots, cov_ref, out_ref):
    parts, blocks, part, width = out_ref.shape
    for b in range(blocks):
        out_ref[:, b] = cov_ref[b * B : (b + 1) * B, :].reshape(parts, part, width)


def pick_columns(slots, covariance, parts):
    rows = covariance.shape[0]
    blocks = rows // B
    part = B // parts
    return pl.pallas_call(
        pick_kernel,
        grid_spec=pltpu.PrefetchScalarGridSpec(
            num_scalar_prefetch=1,
            grid=(2, blocks // 2),
            in_specs=[pl.BlockSpec((2 * B, B), lambda j, b, slots: (b, slots[j]))],
            out_specs=pl.BlockSpec((parts, 2, part, B), lambda j, b, slots: (0, b, 0, j)),
        ),
        out_shape=jax.ShapeDtypeStruct((parts, blocks, part, 2 * B), F32),
    )(slots, covariance)


def tiles_kernel(owner_ref, panel_ref, cov_ref, out_ref, held, arrived):
    slots = [jnp.int32(0), jnp.int32(0)]
    for place in range(owner_ref.shape[0]):
        for n in range(2):
            slots[n] = jnp.where(owner_ref[place] == panel_ref[0] + n, place, slots[n])
    row_blocks, column_blocks = cov_ref.shape[0] // B, cov_ref.shape[1] // B
    first_here = lax.div(slots[0], row_blocks) == lax.axis_index("row")
    row = lax.rem(jnp.where(first_here, slots[0], slots[1]), row_blocks)
    copies = []
    for n in range(2):
        column = lax.rem(slots[n], column_blocks)
        copies.append(
            pltpu.make_async_copy(
                cov_ref.at[pl.ds(pl.multiple_of(row * B, B), B), pl.ds(pl.multiple_of(column * B, B), B)],
                held.at[n],
                arrived.at[n],
            )
        )
        copies[n].start()
    for n in range(2):
        copies[n].wait()
        for i in range(B // 8):
            for j in range(2):
                out_ref[i, 2 * n + j] = held[n, 8 * i : 8 * i + 8, 128 * j : 128 * j + 128]


def pick_tiles(block_owner, panel_index, covariance):
    return pl.pallas_call(
        tiles_kernel,
        in_specs=[SMEM_SPEC, SMEM_SPEC, pl.BlockSpec(memory_space=pl.ANY)],
        out_specs=VMEM_SPEC,
        out_shape=jax.ShapeDtypeStruct((B // 8, 4, 8, 128), F32),
        scratch_shapes=[pltpu.VMEM((2, B, B), F32), pltpu.SemaphoreType.DMA((2,))],
    )(block_owner, panel_index, covariance)


def lanes(tile, j):
    return jnp.broadcast_to(tile[:, j : j + 1], (8, 128))


def eliminate(tiles):
    sub = lax.broadcasted_iota(jnp.int32, (8, 128), 0)
    scales = []
    for t in range(8):
        own = tiles[t]
        cols = [lanes(own, 8 * t + j) for j in range(8)]
        inv, cross = [], {}
        pivots = jnp.ones((8, 128), F32)
        for j in range(8):
            pivot = jnp.broadcast_to(cols[j][j : j + 1, :], (8, 128))
            pivots = jnp.where(sub == j, pivot, pivots)
            r = 1.0 / pivot
            inv.append(r)
            if j == 7:
                break
            m = jnp.where(sub > j, cols[j] * r, 0.0)
            for k in range(j + 1, 8):
                cross[j, k] = jnp.broadcast_to(cols[k][j : j + 1, :], (8, 128))
                cols[k] = cols[k] - m * cross[j, k]
            own = own - m * jnp.broadcast_to(own[j : j + 1, :], (8, 128))
        tiles[t] = own
        scales.append(lax.rsqrt(pivots))
        rows = [jnp.broadcast_to(own[j : j + 1, :], (8, 128)) for j in range(8)]
        for i in range(t + 1, 8):
            low = tiles[i]
            cols = [lanes(low, 8 * t + j) for j in range(8)]
            for j in range(8):
                m = cols[j] * inv[j]
                for k in range(j + 1, 8):
                    cols[k] = cols[k] - m * cross[j, k]
                low = low - m * rows[j]
            tiles[i] = low
    return tiles, scales


def factor_block(work, small, inverse_small):
    for b in range(B // S):
        lo, hi = b * S, (b + 1) * S
        small[:, 0:S] = work[lo:hi, lo:hi]
        row = lax.broadcasted_iota(jnp.int32, (S, S), 0)
        col = lax.broadcasted_iota(jnp.int32, (S, S), 1)
        small[:, S : 2 * S] = jnp.where(row == col, 1.0, 0.0)
        tiles, scales = eliminate([small[8 * i : 8 * i + 8, :] for i in range(8)])
        for i in range(8):
            small[8 * i : 8 * i + 8, :] = tiles[i] * scales[i]
        inverse_small[...] = small[:, S : 2 * S]
        top = dot(inverse_small[...], work[lo:hi, :], NN, HIGH)
        work[lo:hi, :] = top
        if hi < B:
            work[hi:B, :] = work[hi:B, :] - dot(top[:, hi:B], top, TN, HIGH)


def split(a):
    high = a.astype(BF16)
    rest = a - high.astype(F32)
    middle = rest.astype(BF16)
    return high, middle, (rest - middle.astype(F32)).astype(BF16)


def write_left(ref, a):
    high, middle, low = split(a)
    for n, term in enumerate((high, high, middle, high, low, middle)):
        ref[:, n * B : (n + 1) * B] = term


def write_right(ref, start, a):
    high, middle, low = split(a)
    for n, term in enumerate((high, middle, high, low, high, middle)):
        ref[:, start + n * B : start + (n + 1) * B] = term


def factor_kernel(tiles_ref, inverse_ref, l10t_ref, lower_ref, diag_ref, work, small, inverse_small):
    for i in range(B // 8):
        for j in range(4):
            diag_ref[8 * i : 8 * i + 8, 128 * j : 128 * j + 128] = tiles_ref[4 * i + j, 0:8]
        for j in range(2):
            diag_ref[8 * i : 8 * i + 8, 512 + 128 * j : 640 + 128 * j] = tiles_ref[4 * i + 2 + j, 8:16]
    row = lax.broadcasted_iota(jnp.int32, (B, B), 0)
    col = lax.broadcasted_iota(jnp.int32, (B, B), 1)
    eye = jnp.where(row == col, 1.0, 0.0)
    work[:, 0:B] = diag_ref[:, 0:B]
    work[:, B : 2 * B] = eye
    factor_block(work, small, inverse_small)
    x0 = work[:, B : 2 * B]
    write_right(inverse_ref, 0, x0)
    lower_ref[:, 0:B] = jnp.where(row <= col, work[:, 0:B], 0.0).T
    l10t = dot(x0, diag_ref[:, B : 2 * B], NN, HIGH).astype(BF16)
    l10t_ref[...] = l10t
    work[:, 0:B] = diag_ref[:, 2 * B : 3 * B] - dot(l10t, l10t, TN)
    work[:, B : 2 * B] = eye
    factor_block(work, small, inverse_small)
    write_right(inverse_ref, 6 * B, work[:, B : 2 * B])
    lower_ref[:, B : 2 * B] = jnp.where(row <= col, work[:, 0:B], 0.0).T


def factor_diagonal(tiles):
    return pl.pallas_call(
        factor_kernel,
        in_specs=[VMEM_SPEC],
        out_specs=[VMEM_SPEC] * 3,
        out_shape=[
            jax.ShapeDtypeStruct((B, 12 * B), BF16),
            jax.ShapeDtypeStruct((B, B), BF16),
            jax.ShapeDtypeStruct((B, 2 * B), F32),
        ],
        scratch_shapes=[
            pltpu.VMEM((B, 3 * B), F32),
            pltpu.VMEM((B, 2 * B), F32),
            pltpu.VMEM((S, 2 * S), F32),
            pltpu.VMEM((S, S), F32),
        ],
        compiler_params=pltpu.CompilerParams(vmem_limit_bytes=VMEM_BYTES),
        cost_estimate=pl.CostEstimate(flops=2 * 10**10, bytes_accessed=80_000_000, transcendentals=0),
    )(tiles)


def solve_rows(first, second, wide, inverse_ref, l10t_ref):
    write_left(wide, first)
    p0 = dot(wide[...], inverse_ref[:, 0 : 6 * B], NT)
    write_left(wide, second - dot(p0.astype(BF16), l10t_ref[...], NN))
    p1 = dot(wide[...], inverse_ref[:, 6 * B : 12 * B], NT)
    return p0, p1


def piece_kernel(flags, first_ref, second_ref, inverse_ref, l10t_ref, along_ref, across_ref, wide):
    blocks, part = first_ref.shape[1:3]
    solved = solve_rows(
        first_ref[0].reshape(blocks * part, B), second_ref[0].reshape(blocks * part, B), wide, inverse_ref, l10t_ref
    )
    for panel, p in enumerate(solved):
        cut = slice(panel * B, (panel + 1) * B)
        for b in range(blocks):
            mine = p[b * part : (b + 1) * part].astype(BF16)
            mine = jnp.where(flags[16 + b] > panel, mine, jnp.zeros_like(mine))
            across_ref[b, :, cut] = mine
            for q in range(along_ref.shape[0]):
                along_ref[q, b, :, cut] = mine


def solve_piece(flags, parts, inverse, l10t):
    count, blocks, part = parts.shape[:3]
    return pl.pallas_call(
        piece_kernel,
        grid_spec=pltpu.PrefetchScalarGridSpec(
            num_scalar_prefetch=1,
            grid=(1,),
            in_specs=[
                pl.BlockSpec((1, blocks, part, B), lambda i, flags: (flags[20], 0, 0, 0)),
                pl.BlockSpec((1, blocks, part, B), lambda i, flags: (flags[21], 0, 0, 1)),
                whole(*inverse.shape),
                whole(*l10t.shape),
            ],
            out_specs=[whole(count, blocks, part, 2 * B), whole(blocks, part, 2 * B)],
            scratch_shapes=[pltpu.VMEM((blocks * part, 6 * B), BF16)],
        ),
        out_shape=[
            jax.ShapeDtypeStruct((count, blocks, part, 2 * B), BF16),
            jax.ShapeDtypeStruct((blocks, part, 2 * B), BF16),
        ],
        compiler_params=pltpu.CompilerParams(vmem_limit_bytes=VMEM_BYTES),
        cost_estimate=pl.CostEstimate(flops=10**9, bytes_accessed=4_000_000, transcendentals=0),
    )(flags, parts, parts, inverse, l10t)


def whole(*shape):
    return pl.BlockSpec(shape, lambda i, flags: (0,) * len(shape))


def panel_kernel(flags, first_ref, second_ref, along_ref, inverse_ref, l10t_ref, out_ref, wide):
    level = flags[16 + pl.program_id(0)]
    parts, _, part = along_ref.shape[:3]

    @pl.when(flags[4] >= 0)
    def _():
        write_left(wide, first_ref[...])
        p = dot(wide[...], inverse_ref[:, 0 : 6 * B], NT)
        out_ref[:, 0:B] = jnp.where(level > 0, p, 0.0)

    @pl.when(flags[5] >= 0)
    def _():
        before = along_ref[:, 0, :, 0:B].reshape(parts * part, B)
        write_left(wide, second_ref[...] - dot(before, l10t_ref[...], NN))
        p = dot(wide[...], inverse_ref[:, 6 * B : 12 * B], NT)
        out_ref[:, B : 2 * B] = jnp.where(level > 1, p, 0.0)


def solve_panels(flags, covariance, along, inverse, l10t):
    rows = covariance.shape[0]
    parts, blocks, part, width = along.shape
    return pl.pallas_call(
        panel_kernel,
        grid_spec=pltpu.PrefetchScalarGridSpec(
            num_scalar_prefetch=1,
            grid=(blocks,),
            in_specs=[
                pl.BlockSpec((B, B), lambda i, flags: (i, jnp.maximum(flags[4], 0))),
                pl.BlockSpec((B, B), lambda i, flags: (i, jnp.maximum(flags[5], 0))),
                pl.BlockSpec((parts, 1, part, width), lambda i, flags: (0, i, 0, 0)),
                whole(*inverse.shape),
                whole(*l10t.shape),
            ],
            out_specs=pl.BlockSpec((B, 2 * B), lambda i, flags: (i, 0)),
            scratch_shapes=[pltpu.VMEM((B, 6 * B), BF16)],
        ),
        out_shape=jax.ShapeDtypeStruct((rows, 2 * B), F32),
        compiler_params=pltpu.CompilerParams(vmem_limit_bytes=VMEM_BYTES),
        cost_estimate=pl.CostEstimate(flops=10**9, bytes_accessed=4_000_000, transcendentals=0),
    )(flags, covariance, covariance, along, inverse, l10t)


def update_kernel(
    flags,
    cov_ref,
    along_ref,
    across_ref,
    relaid_ref,
    panel_ref,
    lower_ref,
    inverse_ref,
    l10t_ref,
    out_ref,
    solved_ref,
    columns,
    terms_ref,
    white_ref,
    wide,
    arrived,
):
    i = pl.program_id(0)
    parts, _, part = along_ref.shape[:3]
    blocks = across_ref.shape[1] - 3
    steps = parts // 2
    column_blocks = 2 * blocks
    half = relaid_ref.shape[1]
    fold = half // 2

    @pl.when(i == 0)
    def _():
        copies = []
        for panel in range(2):
            for n in range(4):
                source = across_ref.at[4 * flags[6 + panel] + n, pl.ds(blocks, 3)]
                copies.append(pltpu.make_async_copy(source, terms_ref.at[panel, n], arrived.at[len(copies)]))
        for q in range(parts):
            first = 4 * lax.rem(q // 2 + flags[0], steps) + 2 * (q % 2)
            for parity in range(2):
                source = across_ref.at[first + parity, pl.ds(0, blocks)]
                copies.append(pltpu.make_async_copy(source, columns.at[parity, :, q], arrived.at[len(copies)]))
        for copy in copies:
            copy.start()
        for copy in copies:
            copy.wait()
        for panel in range(2):
            for h in range(2):
                for parity in range(2):
                    for f in range(2):
                        lane = (2 * f + panel) * 128
                        terms = [
                            terms_ref[panel, 2 * h + parity, t, :, lane : lane + 128].astype(F32) for t in range(3)
                        ]
                        top = (2 * parity + f) * fold
                        white_ref[top : top + fold, panel * B + h * 128 : panel * B + (h + 1) * 128] = (
                            terms[0] + terms[1]
                        ) + terms[2]
        w0, w1 = solve_rows(white_ref[:, 0:B], white_ref[:, B : 2 * B], wide, inverse_ref, l10t_ref)
        white_ref[:, 0:B] = w0
        white_ref[:, B : 2 * B] = w1

    level = flags[16 + i]
    own = along_ref[:, 0].reshape(parts * part, 2 * B)
    for n in range(column_blocks):
        cut = slice(n * B, (n + 1) * B)
        out_ref[:, cut] = cov_ref[:, cut] - dot(own, columns[n // blocks, n % blocks].reshape(B, 2 * B), NT)

    for panel in range(2):
        is_row = i == flags[2 + panel]
        for n in range(column_blocks):

            @pl.when(is_row & (flags[8 + n] > panel))
            def _():
                out_ref[:, n * B : (n + 1) * B] = jnp.zeros((B, B), F32)

        column = flags[4 + panel]
        place = pl.ds(pl.multiple_of(jnp.maximum(column, 0) * B, B), B)

        @pl.when((column >= 0) & (level > panel))
        def _():
            out_ref[:, place] = panel_ref[:, panel * B : (panel + 1) * B]

        @pl.when((column >= 0) & is_row)
        def _():
            out_ref[:, place] = lower_ref[:, panel * B : (panel + 1) * B]

    product = dot(white_ref[...].astype(BF16), own, NT)
    for parity in range(2):
        for h in range(2):
            there = (slice(parity * half, (parity + 1) * half), slice(h * 128, (h + 1) * 128))
            solved_ref[there] = relaid_ref[2 * h + parity] - product[there]
    for panel in range(2):

        @pl.when(i == flags[2 + panel])
        def _():
            solved_ref[...] = white_ref[:, panel * B : (panel + 1) * B]


def update(flags, covariance, along, across, relaid, panels, lower, inverse, l10t):
    rows, columns = covariance.shape
    parts, blocks, part, width = along.shape
    half = relaid.shape[1]
    return pl.pallas_call(
        update_kernel,
        grid_spec=pltpu.PrefetchScalarGridSpec(
            num_scalar_prefetch=1,
            grid=(blocks,),
            in_specs=[
                pl.BlockSpec((B, columns), lambda i, flags: (i, 0)),
                pl.BlockSpec((parts, 1, part, width), lambda i, flags: (0, i, 0, 0)),
                pl.BlockSpec(memory_space=pl.ANY),
                pl.BlockSpec((4, half, 128), lambda i, flags: (i, 0, 0)),
                pl.BlockSpec((B, width), lambda i, flags: (jnp.where((flags[4] & flags[5]) >= 0, i, 0), 0)),
                whole(*lower.shape),
                whole(*inverse.shape),
                whole(*l10t.shape),
            ],
            out_specs=[
                pl.BlockSpec((B, columns), lambda i, flags: (i, 0)),
                pl.BlockSpec((2 * half, B), lambda i, flags: (0, i)),
            ],
            scratch_shapes=[
                pltpu.VMEM((2, columns // (2 * B), parts, part, width), BF16),
                pltpu.VMEM((2, 4, 3, part, width), BF16),
                pltpu.VMEM((2 * half, width), F32),
                pltpu.VMEM((2 * half, 6 * B), BF16),
                pltpu.SemaphoreType.DMA((2 * parts + 8,)),
            ],
        ),
        out_shape=[jax.ShapeDtypeStruct((rows, columns), F32), jax.ShapeDtypeStruct((2 * half, rows), F32)],
        compiler_params=pltpu.CompilerParams(vmem_limit_bytes=VMEM_BYTES),
        cost_estimate=pl.CostEstimate(flops=5 * 10**9, bytes_accessed=20_000_000, transcendentals=0),
    )(flags, covariance, along, across, relaid, panels, lower, inverse, l10t)


def per_device(covariance, innovations, block_owner, panel_index, *, n_row, n_col):
    local_rows, local_cols = covariance.shape
    row_blocks, column_blocks = local_rows // B, local_cols // B
    r, c = lax.axis_index("row"), lax.axis_index("col")
    targets = panel_index[0] + jnp.arange(2, dtype=jnp.int32)
    positions = jnp.arange(block_owner.shape[0], dtype=jnp.int32)
    slot = jnp.sum(jnp.where(block_owner[None, :] == targets[:, None], positions[None, :], 0), axis=1)
    row_root, column_root = slot // row_blocks, slot // column_blocks
    row_slot, column_slot = slot % row_blocks, slot % column_blocks
    levels = jnp.sum((block_owner[:, None] > targets[None, :]).astype(jnp.int32), axis=1)
    steps = n_row // 4
    shift, core = c // 2, r % 2
    flags = jnp.concatenate(
        [
            shift[None],
            core[None],
            jnp.where(row_root == r, row_slot, -1),
            jnp.where(column_root == c, column_slot, -1),
            (row_slot + shift) % steps,
            lax.dynamic_slice_in_dim(levels, c * column_blocks, column_blocks),
            lax.dynamic_slice_in_dim(levels, r * row_blocks, row_blocks),
            column_root,
        ]
    ).astype(jnp.int32)
    across_axes = [
        (a * n_col + b, ((b // 2 + a // 4) % steps * 4 + b % 2 * 2 + a % 2) * n_col + a // 2)
        for a in range(n_row)
        for b in range(n_col)
    ]

    fold = innovations.shape[0] // 2
    wanted = [lax.dynamic_index_in_dim(innovations, row_root[n], 1, keepdims=False) for n in range(2)]
    wanted = jnp.concatenate([w[h * fold : (h + 1) * fold] for h in range(2) for w in wanted], axis=1)
    wanted = lax.ppermute(wanted, ("row", "col"), across_axes)

    tiles = pick_tiles(block_owner, panel_index, covariance).reshape(n_row * n_col, 8, 128)
    tiles = lax.all_to_all(tiles, ("row", "col"), split_axis=0, concat_axis=0, tiled=True)
    source = jnp.where(c % 4 < 2, column_root[0], column_root[1])
    tiles = jnp.concatenate(
        [lax.dynamic_index_in_dim(tiles, row_root[n] * n_col + source, 0, keepdims=False) for n in range(2)], axis=0
    )
    tiles = lax.all_to_all(
        jnp.broadcast_to(tiles[None], (n_row * n_col,) + tiles.shape),
        ("row", "col"),
        split_axis=0,
        concat_axis=0,
        tiled=True,
    )
    tiles, wanted = lax.optimization_barrier((tiles, wanted))
    inverse, l10t, lower = factor_diagonal(tiles)

    picked = pick_columns(column_slot.astype(jnp.int32), covariance, n_col)
    picked, _ = lax.optimization_barrier((picked, tiles))
    parts = lax.all_to_all(picked, "col", split_axis=0, concat_axis=0, tiled=True)

    high = lax.reduce_precision(wanted, 8, 7)
    middle = lax.reduce_precision(wanted - high, 8, 7)
    wanted = jnp.stack([high, middle, wanted - high - middle]).astype(BF16)

    groups, _ = lax.optimization_barrier((jnp.transpose(innovations, (1, 0, 2)), parts))
    groups = lax.all_to_all(groups, "row", split_axis=0, concat_axis=0, tiled=True)

    along, across = solve_piece(flags, parts, inverse, l10t)
    across = lax.ppermute(across, ("row", "col"), across_axes)
    across, groups = lax.optimization_barrier((across, groups))
    across = lax.all_gather(jnp.concatenate([across, wanted], axis=0), "row", axis=0)
    along, groups = lax.optimization_barrier((along, groups))
    along = lax.all_to_all(along, "col", split_axis=0, concat_axis=0, tiled=True)
    along, groups = lax.optimization_barrier((along, groups))
    relaid = lax.all_to_all(groups, "col", split_axis=0, concat_axis=0, tiled=True)
    panels = solve_panels(flags, covariance, along, inverse, l10t)
    return update(flags, covariance, along, across, relaid, panels, lower, inverse, l10t)


def solution(mesh):
    placed = (P("row", "col"), P("row", None, "col"), P(), P())
    return jax.shard_map(
        functools.partial(per_device, n_row=mesh.shape["row"], n_col=mesh.shape["col"]),
        mesh=mesh,
        in_specs=placed,
        out_specs=(P("row", "col"), P("col", "row")),
        check_vma=False,
    )
```

```python
import functools

import jax
import jax.numpy as jnp
from jax import lax
from jax.experimental import pallas as pl
from jax.experimental.pallas import tpu as pltpu
from jax.sharding import PartitionSpec as P

B = 256
S = 64
VMEM_BYTES = 60 * 1024 * 1024
F32 = jnp.float32
BF16 = jnp.bfloat16
HIGH = lax.Precision.HIGHEST
VMEM_SPEC = pl.BlockSpec(memory_space=pltpu.VMEM)
SMEM_SPEC = pl.BlockSpec(memory_space=pltpu.SMEM)


def dot(a, b, dims, precision=None):
    return lax.dot_general(a, b, (dims, ((), ())), precision=precision, preferred_element_type=F32)


NN = ((1,), (0,))
NT = ((1,), (1,))
TN = ((0,), (0,))


def pick_kernel(slots, cov_ref, out_ref):
    parts, blocks, part, width = out_ref.shape
    for b in range(blocks):
        out_ref[:, b] = cov_ref[b * B : (b + 1) * B, :].reshape(parts, part, width)


def pick_columns(slots, covariance, parts):
    rows = covariance.shape[0]
    blocks = rows // B
    part = B // parts
    return pl.pallas_call(
        pick_kernel,
        grid_spec=pltpu.PrefetchScalarGridSpec(
            num_scalar_prefetch=1,
            grid=(2, blocks // 2),
            in_specs=[pl.BlockSpec((2 * B, B), lambda j, b, slots: (b, slots[j]))],
            out_specs=pl.BlockSpec((parts, 2, part, B), lambda j, b, slots: (0, b, 0, j)),
        ),
        out_shape=jax.ShapeDtypeStruct((parts, blocks, part, 2 * B), F32),
    )(slots, covariance)


def tiles_kernel(owner_ref, panel_ref, cov_ref, out_ref, held, arrived):
    slots = [jnp.int32(0), jnp.int32(0)]
    for place in range(owner_ref.shape[0]):
        for n in range(2):
            slots[n] = jnp.where(owner_ref[place] == panel_ref[0] + n, place, slots[n])
    row_blocks, column_blocks = cov_ref.shape[0] // B, cov_ref.shape[1] // B
    first_here = lax.div(slots[0], row_blocks) == lax.axis_index("row")
    row = lax.rem(jnp.where(first_here, slots[0], slots[1]), row_blocks)
    copies = []
    for n in range(2):
        column = lax.rem(slots[n], column_blocks)
        copies.append(
            pltpu.make_async_copy(
                cov_ref.at[pl.ds(pl.multiple_of(row * B, B), B), pl.ds(pl.multiple_of(column * B, B), B)],
                held.at[n],
                arrived.at[n],
            )
        )
        copies[n].start()
    for n in range(2):
        copies[n].wait()
        for i in range(B // 8):
            for j in range(2):
                out_ref[i, 2 * n + j] = held[n, 8 * i : 8 * i + 8, 128 * j : 128 * j + 128]


def pick_tiles(block_owner, panel_index, covariance):
    return pl.pallas_call(
        tiles_kernel,
        in_specs=[SMEM_SPEC, SMEM_SPEC, pl.BlockSpec(memory_space=pl.ANY)],
        out_specs=VMEM_SPEC,
        out_shape=jax.ShapeDtypeStruct((B // 8, 4, 8, 128), F32),
        scratch_shapes=[pltpu.VMEM((2, B, B), F32), pltpu.SemaphoreType.DMA((2,))],
    )(block_owner, panel_index, covariance)


def lanes(tile, j):
    return jnp.broadcast_to(tile[:, j : j + 1], (8, 128))


def eliminate(tiles):
    sub = lax.broadcasted_iota(jnp.int32, (8, 128), 0)
    scales = []
    for t in range(8):
        own = tiles[t]
        cols = [lanes(own, 8 * t + j) for j in range(8)]
        inv, cross = [], {}
        pivots = jnp.ones((8, 128), F32)
        for j in range(8):
            pivot = jnp.broadcast_to(cols[j][j : j + 1, :], (8, 128))
            pivots = jnp.where(sub == j, pivot, pivots)
            r = 1.0 / pivot
            inv.append(r)
            if j == 7:
                break
            m = jnp.where(sub > j, cols[j] * r, 0.0)
            for k in range(j + 1, 8):
                cross[j, k] = jnp.broadcast_to(cols[k][j : j + 1, :], (8, 128))
                cols[k] = cols[k] - m * cross[j, k]
            own = own - m * jnp.broadcast_to(own[j : j + 1, :], (8, 128))
        tiles[t] = own
        scales.append(lax.rsqrt(pivots))
        rows = [jnp.broadcast_to(own[j : j + 1, :], (8, 128)) for j in range(8)]
        for i in range(t + 1, 8):
            low = tiles[i]
            cols = [lanes(low, 8 * t + j) for j in range(8)]
            for j in range(8):
                m = cols[j] * inv[j]
                for k in range(j + 1, 8):
                    cols[k] = cols[k] - m * cross[j, k]
                low = low - m * rows[j]
            tiles[i] = low
    return tiles, scales


def factor_block(work, small, inverse_small):
    for b in range(B // S):
        lo, hi = b * S, (b + 1) * S
        small[:, 0:S] = work[lo:hi, lo:hi]
        row = lax.broadcasted_iota(jnp.int32, (S, S), 0)
        col = lax.broadcasted_iota(jnp.int32, (S, S), 1)
        small[:, S : 2 * S] = jnp.where(row == col, 1.0, 0.0)
        tiles, scales = eliminate([small[8 * i : 8 * i + 8, :] for i in range(8)])
        for i in range(8):
            small[8 * i : 8 * i + 8, :] = tiles[i] * scales[i]
        inverse_small[...] = small[:, S : 2 * S]
        top = dot(inverse_small[...], work[lo:hi, :], NN, HIGH)
        work[lo:hi, :] = top
        if hi < B:
            work[hi:B, :] = work[hi:B, :] - dot(top[:, hi:B], top, TN, HIGH)


def split(a):
    high = a.astype(BF16)
    rest = a - high.astype(F32)
    middle = rest.astype(BF16)
    return high, middle, (rest - middle.astype(F32)).astype(BF16)


def write_left(ref, a):
    high, middle, low = split(a)
    for n, term in enumerate((high, high, middle, high, low, middle)):
        ref[:, n * B : (n + 1) * B] = term


def write_right(ref, start, a):
    high, middle, low = split(a)
    for n, term in enumerate((high, middle, high, low, high, middle)):
        ref[:, start + n * B : start + (n + 1) * B] = term


def factor_kernel(tiles_ref, inverse_ref, l10t_ref, lower_ref, diag_ref, work, small, inverse_small):
    for i in range(B // 8):
        for j in range(4):
            diag_ref[8 * i : 8 * i + 8, 128 * j : 128 * j + 128] = tiles_ref[4 * i + j, 0:8]
        for j in range(2):
            diag_ref[8 * i : 8 * i + 8, 512 + 128 * j : 640 + 128 * j] = tiles_ref[4 * i + 2 + j, 8:16]
    row = lax.broadcasted_iota(jnp.int32, (B, B), 0)
    col = lax.broadcasted_iota(jnp.int32, (B, B), 1)
    eye = jnp.where(row == col, 1.0, 0.0)
    work[:, 0:B] = diag_ref[:, 0:B]
    work[:, B : 2 * B] = eye
    factor_block(work, small, inverse_small)
    x0 = work[:, B : 2 * B]
    write_right(inverse_ref, 0, x0)
    lower_ref[:, 0:B] = jnp.where(row <= col, work[:, 0:B], 0.0).T
    l10t = dot(x0, diag_ref[:, B : 2 * B], NN, HIGH).astype(BF16)
    l10t_ref[...] = l10t
    work[:, 0:B] = diag_ref[:, 2 * B : 3 * B] - dot(l10t, l10t, TN)
    work[:, B : 2 * B] = eye
    factor_block(work, small, inverse_small)
    write_right(inverse_ref, 6 * B, work[:, B : 2 * B])
    lower_ref[:, B : 2 * B] = jnp.where(row <= col, work[:, 0:B], 0.0).T


def factor_diagonal(tiles):
    return pl.pallas_call(
        factor_kernel,
        in_specs=[VMEM_SPEC],
        out_specs=[VMEM_SPEC] * 3,
        out_shape=[
            jax.ShapeDtypeStruct((B, 12 * B), BF16),
            jax.ShapeDtypeStruct((B, B), BF16),
            jax.ShapeDtypeStruct((B, 2 * B), F32),
        ],
        scratch_shapes=[
            pltpu.VMEM((B, 3 * B), F32),
            pltpu.VMEM((B, 2 * B), F32),
            pltpu.VMEM((S, 2 * S), F32),
            pltpu.VMEM((S, S), F32),
        ],
        compiler_params=pltpu.CompilerParams(vmem_limit_bytes=VMEM_BYTES),
        cost_estimate=pl.CostEstimate(flops=2 * 10**10, bytes_accessed=80_000_000, transcendentals=0),
    )(tiles)


def solve_rows(first, second, wide, inverse_ref, l10t_ref):
    write_left(wide, first)
    p0 = dot(wide[...], inverse_ref[:, 0 : 6 * B], NT)
    write_left(wide, second - dot(p0.astype(BF16), l10t_ref[...], NN))
    p1 = dot(wide[...], inverse_ref[:, 6 * B : 12 * B], NT)
    return p0, p1


def piece_kernel(flags, first_ref, second_ref, inverse_ref, l10t_ref, along_ref, across_ref, wide):
    blocks, part = first_ref.shape[1:3]
    solved = solve_rows(
        first_ref[0].reshape(blocks * part, B), second_ref[0].reshape(blocks * part, B), wide, inverse_ref, l10t_ref
    )
    for panel, p in enumerate(solved):
        cut = slice(panel * B, (panel + 1) * B)
        for b in range(blocks):
            mine = p[b * part : (b + 1) * part].astype(BF16)
            mine = jnp.where(flags[16 + b] > panel, mine, jnp.zeros_like(mine))
            across_ref[b, :, cut] = mine
            for q in range(along_ref.shape[0]):
                along_ref[q, b, :, cut] = mine


def solve_piece(flags, parts, inverse, l10t):
    count, blocks, part = parts.shape[:3]
    return pl.pallas_call(
        piece_kernel,
        grid_spec=pltpu.PrefetchScalarGridSpec(
            num_scalar_prefetch=1,
            grid=(1,),
            in_specs=[
                pl.BlockSpec((1, blocks, part, B), lambda i, flags: (flags[20], 0, 0, 0)),
                pl.BlockSpec((1, blocks, part, B), lambda i, flags: (flags[21], 0, 0, 1)),
                whole(*inverse.shape),
                whole(*l10t.shape),
            ],
            out_specs=[whole(count, blocks, part, 2 * B), whole(blocks, part, 2 * B)],
            scratch_shapes=[pltpu.VMEM((blocks * part, 6 * B), BF16)],
        ),
        out_shape=[
            jax.ShapeDtypeStruct((count, blocks, part, 2 * B), BF16),
            jax.ShapeDtypeStruct((blocks, part, 2 * B), BF16),
        ],
        compiler_params=pltpu.CompilerParams(vmem_limit_bytes=VMEM_BYTES),
        cost_estimate=pl.CostEstimate(flops=10**9, bytes_accessed=4_000_000, transcendentals=0),
    )(flags, parts, parts, inverse, l10t)


def whole(*shape):
    return pl.BlockSpec(shape, lambda i, flags: (0,) * len(shape))


def panel_kernel(flags, first_ref, second_ref, along_ref, inverse_ref, l10t_ref, out_ref, wide):
    level = flags[16 + pl.program_id(0)]
    parts, _, part = along_ref.shape[:3]

    @pl.when(flags[4] >= 0)
    def _():
        write_left(wide, first_ref[...])
        p = dot(wide[...], inverse_ref[:, 0 : 6 * B], NT)
        out_ref[:, 0:B] = jnp.where(level > 0, p, 0.0)

    @pl.when(flags[5] >= 0)
    def _():
        before = along_ref[:, 0, :, 0:B].reshape(parts * part, B)
        write_left(wide, second_ref[...] - dot(before, l10t_ref[...], NN))
        p = dot(wide[...], inverse_ref[:, 6 * B : 12 * B], NT)
        out_ref[:, B : 2 * B] = jnp.where(level > 1, p, 0.0)


def solve_panels(flags, covariance, along, inverse, l10t):
    rows = covariance.shape[0]
    parts, blocks, part, width = along.shape
    return pl.pallas_call(
        panel_kernel,
        grid_spec=pltpu.PrefetchScalarGridSpec(
            num_scalar_prefetch=1,
            grid=(blocks,),
            in_specs=[
                pl.BlockSpec((B, B), lambda i, flags: (i, jnp.maximum(flags[4], 0))),
                pl.BlockSpec((B, B), lambda i, flags: (i, jnp.maximum(flags[5], 0))),
                pl.BlockSpec((parts, 1, part, width), lambda i, flags: (0, i, 0, 0)),
                whole(*inverse.shape),
                whole(*l10t.shape),
            ],
            out_specs=pl.BlockSpec((B, 2 * B), lambda i, flags: (i, 0)),
            scratch_shapes=[pltpu.VMEM((B, 6 * B), BF16)],
        ),
        out_shape=jax.ShapeDtypeStruct((rows, 2 * B), F32),
        compiler_params=pltpu.CompilerParams(vmem_limit_bytes=VMEM_BYTES),
        cost_estimate=pl.CostEstimate(flops=10**9, bytes_accessed=4_000_000, transcendentals=0),
    )(flags, covariance, covariance, along, inverse, l10t)


def update_kernel(
    flags,
    cov_ref,
    along_ref,
    across_ref,
    relaid_ref,
    panel_ref,
    lower_ref,
    inverse_ref,
    l10t_ref,
    out_ref,
    solved_ref,
    columns,
    terms_ref,
    white_ref,
    wide,
    arrived,
):
    i = pl.program_id(0)
    parts, _, part = along_ref.shape[:3]
    blocks = across_ref.shape[1] - 3
    steps = parts // 2
    column_blocks = 2 * blocks
    half = relaid_ref.shape[1]
    fold = half // 2

    @pl.when(i == 0)
    def _():
        copies = []
        for panel in range(2):
            for n in range(4):
                source = across_ref.at[4 * flags[6 + panel] + n, pl.ds(blocks, 3)]
                copies.append(pltpu.make_async_copy(source, terms_ref.at[panel, n], arrived.at[len(copies)]))
        for q in range(parts):
            first = 4 * lax.rem(q // 2 + flags[0], steps) + 2 * (q % 2)
            for parity in range(2):
                source = across_ref.at[first + parity, pl.ds(0, blocks)]
                copies.append(pltpu.make_async_copy(source, columns.at[parity, :, q], arrived.at[len(copies)]))
        for copy in copies:
            copy.start()
        for copy in copies:
            copy.wait()
        for panel in range(2):
            for h in range(2):
                for parity in range(2):
                    for f in range(2):
                        lane = (2 * f + panel) * 128
                        terms = [
                            terms_ref[panel, 2 * h + parity, t, :, lane : lane + 128].astype(F32) for t in range(3)
                        ]
                        top = (2 * parity + f) * fold
                        white_ref[top : top + fold, panel * B + h * 128 : panel * B + (h + 1) * 128] = (
                            terms[0] + terms[1]
                        ) + terms[2]
        w0, w1 = solve_rows(white_ref[:, 0:B], white_ref[:, B : 2 * B], wide, inverse_ref, l10t_ref)
        white_ref[:, 0:B] = w0
        white_ref[:, B : 2 * B] = w1

    level = flags[16 + i]
    own = along_ref[:, 0].reshape(parts * part, 2 * B)
    for n in range(column_blocks):
        cut = slice(n * B, (n + 1) * B)
        out_ref[:, cut] = cov_ref[:, cut] - dot(own, columns[n // blocks, n % blocks].reshape(B, 2 * B), NT)

    for panel in range(2):
        is_row = i == flags[2 + panel]
        for n in range(column_blocks):

            @pl.when(is_row & (flags[8 + n] > panel))
            def _():
                out_ref[:, n * B : (n + 1) * B] = jnp.zeros((B, B), F32)

        column = flags[4 + panel]
        place = pl.ds(pl.multiple_of(jnp.maximum(column, 0) * B, B), B)

        @pl.when((column >= 0) & (level > panel))
        def _():
            out_ref[:, place] = panel_ref[:, panel * B : (panel + 1) * B]

        @pl.when((column >= 0) & is_row)
        def _():
            out_ref[:, place] = lower_ref[:, panel * B : (panel + 1) * B]

    product = dot(white_ref[...].astype(BF16), own, NT)
    for parity in range(2):
        for h in range(2):
            there = (slice(parity * half, (parity + 1) * half), slice(h * 128, (h + 1) * 128))
            solved_ref[there] = relaid_ref[2 * h + parity] - product[there]
    for panel in range(2):

        @pl.when(i == flags[2 + panel])
        def _():
            solved_ref[...] = white_ref[:, panel * B : (panel + 1) * B]


def update(flags, covariance, along, across, relaid, panels, lower, inverse, l10t):
    rows, columns = covariance.shape
    parts, blocks, part, width = along.shape
    half = relaid.shape[1]
    return pl.pallas_call(
        update_kernel,
        grid_spec=pltpu.PrefetchScalarGridSpec(
            num_scalar_prefetch=1,
            grid=(blocks,),
            in_specs=[
                pl.BlockSpec((B, columns), lambda i, flags: (i, 0)),
                pl.BlockSpec((parts, 1, part, width), lambda i, flags: (0, i, 0, 0)),
                pl.BlockSpec(memory_space=pl.ANY),
                pl.BlockSpec((4, half, 128), lambda i, flags: (i, 0, 0)),
                pl.BlockSpec((B, width), lambda i, flags: (jnp.where((flags[4] & flags[5]) >= 0, i, 0), 0)),
                whole(*lower.shape),
                whole(*inverse.shape),
                whole(*l10t.shape),
            ],
            out_specs=[
                pl.BlockSpec((B, columns), lambda i, flags: (i, 0)),
                pl.BlockSpec((2 * half, B), lambda i, flags: (0, i)),
            ],
            scratch_shapes=[
                pltpu.VMEM((2, columns // (2 * B), parts, part, width), BF16),
                pltpu.VMEM((2, 4, 3, part, width), BF16),
                pltpu.VMEM((2 * half, width), F32),
                pltpu.VMEM((2 * half, 6 * B), BF16),
                pltpu.SemaphoreType.DMA((2 * parts + 8,)),
            ],
        ),
        out_shape=[jax.ShapeDtypeStruct((rows, columns), F32), jax.ShapeDtypeStruct((2 * half, rows), F32)],
        compiler_params=pltpu.CompilerParams(vmem_limit_bytes=VMEM_BYTES),
        cost_estimate=pl.CostEstimate(flops=5 * 10**9, bytes_accessed=20_000_000, transcendentals=0),
    )(flags, covariance, along, across, relaid, panels, lower, inverse, l10t)


def per_device(covariance, innovations, block_owner, panel_index, *, n_row, n_col):
    local_rows, local_cols = covariance.shape
    row_blocks, column_blocks = local_rows // B, local_cols // B
    r, c = lax.axis_index("row"), lax.axis_index("col")
    targets = panel_index[0] + jnp.arange(2, dtype=jnp.int32)
    positions = jnp.arange(block_owner.shape[0], dtype=jnp.int32)
    slot = jnp.sum(jnp.where(block_owner[None, :] == targets[:, None], positions[None, :], 0), axis=1)
    row_root, column_root = slot // row_blocks, slot // column_blocks
    row_slot, column_slot = slot % row_blocks, slot % column_blocks
    levels = jnp.sum((block_owner[:, None] > targets[None, :]).astype(jnp.int32), axis=1)
    steps = n_row // 4
    shift, core = c // 2, r % 2
    flags = jnp.concatenate(
        [
            shift[None],
            core[None],
            jnp.where(row_root == r, row_slot, -1),
            jnp.where(column_root == c, column_slot, -1),
            (row_slot + shift) % steps,
            lax.dynamic_slice_in_dim(levels, c * column_blocks, column_blocks),
            lax.dynamic_slice_in_dim(levels, r * row_blocks, row_blocks),
            column_root,
        ]
    ).astype(jnp.int32)
    across_axes = [
        (a * n_col + b, ((b // 2 + a // 4) % steps * 4 + b % 2 * 2 + a % 2) * n_col + a // 2)
        for a in range(n_row)
        for b in range(n_col)
    ]

    fold = innovations.shape[0] // 2
    wanted = [lax.dynamic_index_in_dim(innovations, row_root[n], 1, keepdims=False) for n in range(2)]
    wanted = jnp.concatenate([w[h * fold : (h + 1) * fold] for h in range(2) for w in wanted], axis=1)
    wanted = lax.ppermute(wanted, ("row", "col"), across_axes)

    tiles = pick_tiles(block_owner, panel_index, covariance).reshape(n_row * n_col, 8, 128)
    tiles = lax.all_to_all(tiles, ("row", "col"), split_axis=0, concat_axis=0, tiled=True)
    source = jnp.where(c % 4 < 2, column_root[0], column_root[1])
    tiles = jnp.concatenate(
        [lax.dynamic_index_in_dim(tiles, row_root[n] * n_col + source, 0, keepdims=False) for n in range(2)], axis=0
    )
    tiles = lax.all_to_all(
        jnp.broadcast_to(tiles[None], (n_row * n_col,) + tiles.shape),
        ("row", "col"),
        split_axis=0,
        concat_axis=0,
        tiled=True,
    )
    tiles, wanted = lax.optimization_barrier((tiles, wanted))
    inverse, l10t, lower = factor_diagonal(tiles)

    picked = pick_columns(column_slot.astype(jnp.int32), covariance, n_col)
    picked, _ = lax.optimization_barrier((picked, tiles))
    parts = lax.all_to_all(picked, "col", split_axis=0, concat_axis=0, tiled=True)

    high = lax.reduce_precision(wanted, 8, 7)
    middle = lax.reduce_precision(wanted - high, 8, 7)
    wanted = jnp.stack([high, middle, wanted - high - middle]).astype(BF16)

    groups, _, _ = lax.optimization_barrier((jnp.transpose(innovations, (1, 0, 2)), parts, l10t))
    groups = lax.all_to_all(groups, "row", split_axis=0, concat_axis=0, tiled=True)

    along, across = solve_piece(flags, parts, inverse, l10t)
    across = lax.ppermute(across, ("row", "col"), across_axes)
    across, groups = lax.optimization_barrier((across, groups))
    across = lax.all_gather(jnp.concatenate([across, wanted], axis=0), "row", axis=0)
    along, groups = lax.optimization_barrier((along, groups))
    along = lax.all_to_all(along, "col", split_axis=0, concat_axis=0, tiled=True)
    along, groups = lax.optimization_barrier((along, groups))
    relaid = lax.all_to_all(groups, "col", split_axis=0, concat_axis=0, tiled=True)
    panels = solve_panels(flags, covariance, along, inverse, l10t)
    return update(flags, covariance, along, across, relaid, panels, lower, inverse, l10t)


def solution(mesh):
    placed = (P("row", "col"), P("row", None, "col"), P(), P())
    return jax.shard_map(
        functools.partial(per_device, n_row=mesh.shape["row"], n_col=mesh.shape["col"]),
        mesh=mesh,
        in_specs=placed,
        out_specs=(P("row", "col"), P("col", "row")),
        check_vma=False,
    )
```

```python
import functools

import jax
import jax.numpy as jnp
from jax import lax
from jax.experimental import pallas as pl
from jax.experimental.pallas import tpu as pltpu
from jax.sharding import PartitionSpec as P

B = 256
S = 64
VMEM_BYTES = 60 * 1024 * 1024
F32 = jnp.float32
BF16 = jnp.bfloat16
HIGH = lax.Precision.HIGHEST
VMEM_SPEC = pl.BlockSpec(memory_space=pltpu.VMEM)
SMEM_SPEC = pl.BlockSpec(memory_space=pltpu.SMEM)


def dot(a, b, dims, precision=None):
    return lax.dot_general(a, b, (dims, ((), ())), precision=precision, preferred_element_type=F32)


NN = ((1,), (0,))
NT = ((1,), (1,))
TN = ((0,), (0,))


def pick_kernel(slots, cov_ref, out_ref):
    parts, blocks, part, width = out_ref.shape
    for b in range(blocks):
        out_ref[:, b] = cov_ref[b * B : (b + 1) * B, :].reshape(parts, part, width)


def pick_columns(slots, covariance, parts):
    rows = covariance.shape[0]
    blocks = rows // B
    part = B // parts
    return pl.pallas_call(
        pick_kernel,
        grid_spec=pltpu.PrefetchScalarGridSpec(
            num_scalar_prefetch=1,
            grid=(2, blocks // 2),
            in_specs=[pl.BlockSpec((2 * B, B), lambda j, b, slots: (b, slots[j]))],
            out_specs=pl.BlockSpec((parts, 2, part, B), lambda j, b, slots: (0, b, 0, j)),
        ),
        out_shape=jax.ShapeDtypeStruct((parts, blocks, part, 2 * B), F32),
    )(slots, covariance)


def tiles_kernel(owner_ref, panel_ref, cov_ref, out_ref, held, arrived):
    slots = [jnp.int32(0), jnp.int32(0)]
    for place in range(owner_ref.shape[0]):
        for n in range(2):
            slots[n] = jnp.where(owner_ref[place] == panel_ref[0] + n, place, slots[n])
    row_blocks, column_blocks = cov_ref.shape[0] // B, cov_ref.shape[1] // B
    first_here = lax.div(slots[0], row_blocks) == lax.axis_index("row")
    row = lax.rem(jnp.where(first_here, slots[0], slots[1]), row_blocks)
    copies = []
    for n in range(2):
        column = lax.rem(slots[n], column_blocks)
        copies.append(
            pltpu.make_async_copy(
                cov_ref.at[pl.ds(pl.multiple_of(row * B, B), B), pl.ds(pl.multiple_of(column * B, B), B)],
                held.at[n],
                arrived.at[n],
            )
        )
        copies[n].start()
    for n in range(2):
        copies[n].wait()
        for i in range(B // 8):
            for j in range(2):
                out_ref[i, 2 * n + j] = held[n, 8 * i : 8 * i + 8, 128 * j : 128 * j + 128]


def pick_tiles(block_owner, panel_index, covariance):
    return pl.pallas_call(
        tiles_kernel,
        in_specs=[SMEM_SPEC, SMEM_SPEC, pl.BlockSpec(memory_space=pl.ANY)],
        out_specs=VMEM_SPEC,
        out_shape=jax.ShapeDtypeStruct((B // 8, 4, 8, 128), F32),
        scratch_shapes=[pltpu.VMEM((2, B, B), F32), pltpu.SemaphoreType.DMA((2,))],
    )(block_owner, panel_index, covariance)


def lanes(tile, j):
    return jnp.broadcast_to(tile[:, j : j + 1], (8, 128))


def eliminate(tiles):
    sub = lax.broadcasted_iota(jnp.int32, (8, 128), 0)
    scales = []
    for t in range(8):
        own = tiles[t]
        cols = [lanes(own, 8 * t + j) for j in range(8)]
        inv, cross = [], {}
        pivots = jnp.ones((8, 128), F32)
        for j in range(8):
            pivot = jnp.broadcast_to(cols[j][j : j + 1, :], (8, 128))
            pivots = jnp.where(sub == j, pivot, pivots)
            r = 1.0 / pivot
            inv.append(r)
            if j == 7:
                break
            m = jnp.where(sub > j, cols[j] * r, 0.0)
            for k in range(j + 1, 8):
                cross[j, k] = jnp.broadcast_to(cols[k][j : j + 1, :], (8, 128))
                cols[k] = cols[k] - m * cross[j, k]
            own = own - m * jnp.broadcast_to(own[j : j + 1, :], (8, 128))
        tiles[t] = own
        scales.append(lax.rsqrt(pivots))
        rows = [jnp.broadcast_to(own[j : j + 1, :], (8, 128)) for j in range(8)]
        for i in range(t + 1, 8):
            low = tiles[i]
            cols = [lanes(low, 8 * t + j) for j in range(8)]
            for j in range(8):
                m = cols[j] * inv[j]
                for k in range(j + 1, 8):
                    cols[k] = cols[k] - m * cross[j, k]
                low = low - m * rows[j]
            tiles[i] = low
    return tiles, scales


def factor_block(work, small, inverse_small):
    for b in range(B // S):
        lo, hi = b * S, (b + 1) * S
        small[:, 0:S] = work[lo:hi, lo:hi]
        row = lax.broadcasted_iota(jnp.int32, (S, S), 0)
        col = lax.broadcasted_iota(jnp.int32, (S, S), 1)
        small[:, S : 2 * S] = jnp.where(row == col, 1.0, 0.0)
        tiles, scales = eliminate([small[8 * i : 8 * i + 8, :] for i in range(8)])
        for i in range(8):
            small[8 * i : 8 * i + 8, :] = tiles[i] * scales[i]
        inverse_small[...] = small[:, S : 2 * S]
        top = dot(inverse_small[...], work[lo:hi, :], NN, HIGH)
        work[lo:hi, :] = top
        if hi < B:
            work[hi:B, :] = work[hi:B, :] - dot(top[:, hi:B], top, TN, HIGH)


def split(a):
    high = a.astype(BF16)
    rest = a - high.astype(F32)
    middle = rest.astype(BF16)
    return high, middle, (rest - middle.astype(F32)).astype(BF16)


def write_left(ref, a):
    high, middle, low = split(a)
    for n, term in enumerate((high, high, middle, high, low, middle)):
        ref[:, n * B : (n + 1) * B] = term


def write_right(ref, start, a):
    high, middle, low = split(a)
    for n, term in enumerate((high, middle, high, low, high, middle)):
        ref[:, start + n * B : start + (n + 1) * B] = term


def factor_kernel(tiles_ref, inverse_ref, l10t_ref, lower_ref, diag_ref, work, small, inverse_small):
    for i in range(B // 8):
        for j in range(4):
            diag_ref[8 * i : 8 * i + 8, 128 * j : 128 * j + 128] = tiles_ref[4 * i + j, 0:8]
        for j in range(2):
            diag_ref[8 * i : 8 * i + 8, 512 + 128 * j : 640 + 128 * j] = tiles_ref[4 * i + 2 + j, 8:16]
    row = lax.broadcasted_iota(jnp.int32, (B, B), 0)
    col = lax.broadcasted_iota(jnp.int32, (B, B), 1)
    eye = jnp.where(row == col, 1.0, 0.0)
    work[:, 0:B] = diag_ref[:, 0:B]
    work[:, B : 2 * B] = eye
    factor_block(work, small, inverse_small)
    x0 = work[:, B : 2 * B]
    write_right(inverse_ref, 0, x0)
    lower_ref[:, 0:B] = jnp.where(row <= col, work[:, 0:B], 0.0).T
    l10t = dot(x0, diag_ref[:, B : 2 * B], NN, HIGH).astype(BF16)
    l10t_ref[...] = l10t
    work[:, 0:B] = diag_ref[:, 2 * B : 3 * B] - dot(l10t, l10t, TN)
    work[:, B : 2 * B] = eye
    factor_block(work, small, inverse_small)
    write_right(inverse_ref, 6 * B, work[:, B : 2 * B])
    lower_ref[:, B : 2 * B] = jnp.where(row <= col, work[:, 0:B], 0.0).T


def factor_diagonal(tiles):
    return pl.pallas_call(
        factor_kernel,
        in_specs=[VMEM_SPEC],
        out_specs=[VMEM_SPEC] * 3,
        out_shape=[
            jax.ShapeDtypeStruct((B, 12 * B), BF16),
            jax.ShapeDtypeStruct((B, B), BF16),
            jax.ShapeDtypeStruct((B, 2 * B), F32),
        ],
        scratch_shapes=[
            pltpu.VMEM((B, 3 * B), F32),
            pltpu.VMEM((B, 2 * B), F32),
            pltpu.VMEM((S, 2 * S), F32),
            pltpu.VMEM((S, S), F32),
        ],
        compiler_params=pltpu.CompilerParams(vmem_limit_bytes=VMEM_BYTES),
        cost_estimate=pl.CostEstimate(flops=2 * 10**10, bytes_accessed=80_000_000, transcendentals=0),
    )(tiles)


def solve_rows(first, second, wide, inverse_ref, l10t_ref):
    write_left(wide, first)
    p0 = dot(wide[...], inverse_ref[:, 0 : 6 * B], NT)
    write_left(wide, second - dot(p0.astype(BF16), l10t_ref[...], NN))
    p1 = dot(wide[...], inverse_ref[:, 6 * B : 12 * B], NT)
    return p0, p1


def piece_kernel(flags, first_ref, second_ref, inverse_ref, l10t_ref, along_ref, across_ref, wide):
    blocks, part = first_ref.shape[1:3]
    solved = solve_rows(
        first_ref[0].reshape(blocks * part, B), second_ref[0].reshape(blocks * part, B), wide, inverse_ref, l10t_ref
    )
    for panel, p in enumerate(solved):
        cut = slice(panel * B, (panel + 1) * B)
        for b in range(blocks):
            mine = p[b * part : (b + 1) * part].astype(BF16)
            mine = jnp.where(flags[16 + b] > panel, mine, jnp.zeros_like(mine))
            across_ref[b, :, cut] = mine
            for q in range(along_ref.shape[0]):
                along_ref[q, b, :, cut] = mine


def solve_piece(flags, parts, inverse, l10t):
    count, blocks, part = parts.shape[:3]
    return pl.pallas_call(
        piece_kernel,
        grid_spec=pltpu.PrefetchScalarGridSpec(
            num_scalar_prefetch=1,
            grid=(1,),
            in_specs=[
                pl.BlockSpec((1, blocks, part, B), lambda i, flags: (flags[20], 0, 0, 0)),
                pl.BlockSpec((1, blocks, part, B), lambda i, flags: (flags[21], 0, 0, 1)),
                whole(*inverse.shape),
                whole(*l10t.shape),
            ],
            out_specs=[whole(count, blocks, part, 2 * B), whole(blocks, part, 2 * B)],
            scratch_shapes=[pltpu.VMEM((blocks * part, 6 * B), BF16)],
        ),
        out_shape=[
            jax.ShapeDtypeStruct((count, blocks, part, 2 * B), BF16),
            jax.ShapeDtypeStruct((blocks, part, 2 * B), BF16),
        ],
        compiler_params=pltpu.CompilerParams(vmem_limit_bytes=VMEM_BYTES),
        cost_estimate=pl.CostEstimate(flops=10**9, bytes_accessed=4_000_000, transcendentals=0),
    )(flags, parts, parts, inverse, l10t)


def whole(*shape):
    return pl.BlockSpec(shape, lambda i, flags: (0,) * len(shape))


def panel_kernel(flags, first_ref, second_ref, along_ref, inverse_ref, l10t_ref, out_ref, wide):
    level = flags[16 + pl.program_id(0)]
    parts, _, part = along_ref.shape[:3]

    @pl.when(flags[4] >= 0)
    def _():
        write_left(wide, first_ref[...])
        p = dot(wide[...], inverse_ref[:, 0 : 6 * B], NT)
        out_ref[:, 0:B] = jnp.where(level > 0, p, 0.0)

    @pl.when(flags[5] >= 0)
    def _():
        before = along_ref[:, 0, :, 0:B].reshape(parts * part, B)
        write_left(wide, second_ref[...] - dot(before, l10t_ref[...], NN))
        p = dot(wide[...], inverse_ref[:, 6 * B : 12 * B], NT)
        out_ref[:, B : 2 * B] = jnp.where(level > 1, p, 0.0)


def solve_panels(flags, covariance, along, inverse, l10t):
    rows = covariance.shape[0]
    parts, blocks, part, width = along.shape
    turn = lambda i, flags: jnp.where((flags[4] & flags[5]) >= 0, i, 0)
    return pl.pallas_call(
        panel_kernel,
        grid_spec=pltpu.PrefetchScalarGridSpec(
            num_scalar_prefetch=1,
            grid=(blocks,),
            in_specs=[
                pl.BlockSpec((B, B), lambda i, flags: (turn(i, flags), jnp.maximum(flags[4], 0))),
                pl.BlockSpec((B, B), lambda i, flags: (turn(i, flags), jnp.maximum(flags[5], 0))),
                pl.BlockSpec((parts, 1, part, width), lambda i, flags: (0, turn(i, flags), 0, 0)),
                whole(*inverse.shape),
                whole(*l10t.shape),
            ],
            out_specs=pl.BlockSpec((B, 2 * B), lambda i, flags: (turn(i, flags), 0)),
            scratch_shapes=[pltpu.VMEM((B, 6 * B), BF16)],
        ),
        out_shape=jax.ShapeDtypeStruct((rows, 2 * B), F32),
        compiler_params=pltpu.CompilerParams(vmem_limit_bytes=VMEM_BYTES),
        cost_estimate=pl.CostEstimate(flops=10**9, bytes_accessed=4_000_000, transcendentals=0),
    )(flags, covariance, covariance, along, inverse, l10t)


def update_kernel(
    flags,
    cov_ref,
    along_ref,
    across_ref,
    relaid_ref,
    panel_ref,
    lower_ref,
    inverse_ref,
    l10t_ref,
    out_ref,
    solved_ref,
    columns,
    terms_ref,
    white_ref,
    wide,
    arrived,
):
    i = pl.program_id(0)
    parts, _, part = along_ref.shape[:3]
    blocks = across_ref.shape[1] - 3
    steps = parts // 2
    column_blocks = 2 * blocks
    half = relaid_ref.shape[1]
    fold = half // 2

    @pl.when(i == 0)
    def _():
        copies = []
        for panel in range(2):
            for n in range(4):
                source = across_ref.at[4 * flags[6 + panel] + n, pl.ds(blocks, 3)]
                copies.append(pltpu.make_async_copy(source, terms_ref.at[panel, n], arrived.at[len(copies)]))
        for q in range(parts):
            first = 4 * lax.rem(q // 2 + flags[0], steps) + 2 * (q % 2)
            for parity in range(2):
                source = across_ref.at[first + parity, pl.ds(0, blocks)]
                copies.append(pltpu.make_async_copy(source, columns.at[parity, :, q], arrived.at[len(copies)]))
        for copy in copies:
            copy.start()
        for copy in copies[:8]:
            copy.wait()
        for panel in range(2):
            for h in range(2):
                for parity in range(2):
                    for f in range(2):
                        lane = (2 * f + panel) * 128
                        terms = [
                            terms_ref[panel, 2 * h + parity, t, :, lane : lane + 128].astype(F32) for t in range(3)
                        ]
                        top = (2 * parity + f) * fold
                        white_ref[top : top + fold, panel * B + h * 128 : panel * B + (h + 1) * 128] = (
                            terms[0] + terms[1]
                        ) + terms[2]
        w0, w1 = solve_rows(white_ref[:, 0:B], white_ref[:, B : 2 * B], wide, inverse_ref, l10t_ref)
        white_ref[:, 0:B] = w0
        white_ref[:, B : 2 * B] = w1
        for copy in copies[8:]:
            copy.wait()

    level = flags[16 + i]
    own = along_ref[:, 0].reshape(parts * part, 2 * B)
    for n in range(column_blocks):
        cut = slice(n * B, (n + 1) * B)
        out_ref[:, cut] = cov_ref[:, cut] - dot(own, columns[n // blocks, n % blocks].reshape(B, 2 * B), NT)

    for panel in range(2):
        is_row = i == flags[2 + panel]
        for n in range(column_blocks):

            @pl.when(is_row & (flags[8 + n] > panel))
            def _():
                out_ref[:, n * B : (n + 1) * B] = jnp.zeros((B, B), F32)

        column = flags[4 + panel]
        place = pl.ds(pl.multiple_of(jnp.maximum(column, 0) * B, B), B)

        @pl.when((column >= 0) & (level > panel))
        def _():
            out_ref[:, place] = panel_ref[:, panel * B : (panel + 1) * B]

        @pl.when((column >= 0) & is_row)
        def _():
            out_ref[:, place] = lower_ref[:, panel * B : (panel + 1) * B]

    product = dot(white_ref[...].astype(BF16), own, NT)
    for parity in range(2):
        for h in range(2):
            there = (slice(parity * half, (parity + 1) * half), slice(h * 128, (h + 1) * 128))
            solved_ref[there] = relaid_ref[2 * h + parity] - product[there]
    for panel in range(2):

        @pl.when(i == flags[2 + panel])
        def _():
            solved_ref[...] = white_ref[:, panel * B : (panel + 1) * B]


def update(flags, covariance, along, across, relaid, panels, lower, inverse, l10t):
    rows, columns = covariance.shape
    parts, blocks, part, width = along.shape
    half = relaid.shape[1]
    return pl.pallas_call(
        update_kernel,
        grid_spec=pltpu.PrefetchScalarGridSpec(
            num_scalar_prefetch=1,
            grid=(blocks,),
            in_specs=[
                pl.BlockSpec((B, columns), lambda i, flags: (i, 0)),
                pl.BlockSpec((parts, 1, part, width), lambda i, flags: (0, i, 0, 0)),
                pl.BlockSpec(memory_space=pl.ANY),
                pl.BlockSpec((4, half, 128), lambda i, flags: (i, 0, 0)),
                pl.BlockSpec((B, width), lambda i, flags: (jnp.where((flags[4] & flags[5]) >= 0, i, 0), 0)),
                whole(*lower.shape),
                whole(*inverse.shape),
                whole(*l10t.shape),
            ],
            out_specs=[
                pl.BlockSpec((B, columns), lambda i, flags: (i, 0)),
                pl.BlockSpec((2 * half, B), lambda i, flags: (0, i)),
            ],
            scratch_shapes=[
                pltpu.VMEM((2, columns // (2 * B), parts, part, width), BF16),
                pltpu.VMEM((2, 4, 3, part, width), BF16),
                pltpu.VMEM((2 * half, width), F32),
                pltpu.VMEM((2 * half, 6 * B), BF16),
                pltpu.SemaphoreType.DMA((2 * parts + 8,)),
            ],
        ),
        out_shape=[jax.ShapeDtypeStruct((rows, columns), F32), jax.ShapeDtypeStruct((2 * half, rows), F32)],
        compiler_params=pltpu.CompilerParams(vmem_limit_bytes=VMEM_BYTES),
        cost_estimate=pl.CostEstimate(flops=5 * 10**9, bytes_accessed=20_000_000, transcendentals=0),
    )(flags, covariance, along, across, relaid, panels, lower, inverse, l10t)


def per_device(covariance, innovations, block_owner, panel_index, *, n_row, n_col):
    local_rows, local_cols = covariance.shape
    row_blocks, column_blocks = local_rows // B, local_cols // B
    r, c = lax.axis_index("row"), lax.axis_index("col")
    targets = panel_index[0] + jnp.arange(2, dtype=jnp.int32)
    positions = jnp.arange(block_owner.shape[0], dtype=jnp.int32)
    slot = jnp.sum(jnp.where(block_owner[None, :] == targets[:, None], positions[None, :], 0), axis=1)
    row_root, column_root = slot // row_blocks, slot // column_blocks
    row_slot, column_slot = slot % row_blocks, slot % column_blocks
    levels = jnp.sum((block_owner[:, None] > targets[None, :]).astype(jnp.int32), axis=1)
    steps = n_row // 4
    shift, core = c // 2, r % 2
    flags = jnp.concatenate(
        [
            shift[None],
            core[None],
            jnp.where(row_root == r, row_slot, -1),
            jnp.where(column_root == c, column_slot, -1),
            (row_slot + shift) % steps,
            lax.dynamic_slice_in_dim(levels, c * column_blocks, column_blocks),
            lax.dynamic_slice_in_dim(levels, r * row_blocks, row_blocks),
            column_root,
        ]
    ).astype(jnp.int32)
    across_axes = [
        (a * n_col + b, ((b // 2 + a // 4) % steps * 4 + b % 2 * 2 + a % 2) * n_col + a // 2)
        for a in range(n_row)
        for b in range(n_col)
    ]

    fold = innovations.shape[0] // 2
    wanted = [lax.dynamic_index_in_dim(innovations, row_root[n], 1, keepdims=False) for n in range(2)]
    wanted = jnp.concatenate([w[h * fold : (h + 1) * fold] for h in range(2) for w in wanted], axis=1)
    wanted = lax.ppermute(wanted, ("row", "col"), across_axes)

    tiles = pick_tiles(block_owner, panel_index, covariance).reshape(n_row * n_col, 8, 128)
    tiles = lax.all_to_all(tiles, ("row", "col"), split_axis=0, concat_axis=0, tiled=True)
    source = jnp.where(c % 4 < 2, column_root[0], column_root[1])
    tiles = jnp.concatenate(
        [lax.dynamic_index_in_dim(tiles, row_root[n] * n_col + source, 0, keepdims=False) for n in range(2)], axis=0
    )
    tiles = lax.all_to_all(
        jnp.broadcast_to(tiles[None], (n_row * n_col,) + tiles.shape),
        ("row", "col"),
        split_axis=0,
        concat_axis=0,
        tiled=True,
    )
    tiles, wanted = lax.optimization_barrier((tiles, wanted))
    inverse, l10t, lower = factor_diagonal(tiles)

    picked = pick_columns(column_slot.astype(jnp.int32), covariance, n_col)
    picked, _ = lax.optimization_barrier((picked, tiles))
    parts = lax.all_to_all(picked, "col", split_axis=0, concat_axis=0, tiled=True)

    high = lax.reduce_precision(wanted, 8, 7)
    middle = lax.reduce_precision(wanted - high, 8, 7)
    wanted = jnp.stack([high, middle, wanted - high - middle]).astype(BF16)

    groups, _, _ = lax.optimization_barrier((jnp.transpose(innovations, (1, 0, 2)), parts, l10t))
    groups = lax.all_to_all(groups, "row", split_axis=0, concat_axis=0, tiled=True)

    along, across = solve_piece(flags, parts, inverse, l10t)
    across = lax.ppermute(across, ("row", "col"), across_axes)
    across, groups = lax.optimization_barrier((across, groups))
    across = lax.all_gather(jnp.concatenate([across, wanted], axis=0), "row", axis=0)
    along, groups = lax.optimization_barrier((along, groups))
    along = lax.all_to_all(along, "col", split_axis=0, concat_axis=0, tiled=True)
    along, groups = lax.optimization_barrier((along, groups))
    relaid = lax.all_to_all(groups, "col", split_axis=0, concat_axis=0, tiled=True)
    panels = solve_panels(flags, covariance, along, inverse, l10t)
    return update(flags, covariance, along, across, relaid, panels, lower, inverse, l10t)


def solution(mesh):
    placed = (P("row", "col"), P("row", None, "col"), P(), P())
    return jax.shard_map(
        functools.partial(per_device, n_row=mesh.shape["row"], n_col=mesh.shape["col"]),
        mesh=mesh,
        in_specs=placed,
        out_specs=(P("row", "col"), P("col", "row")),
        check_vma=False,
    )
```

```python
import functools

import jax
import jax.numpy as jnp
from jax import lax
from jax.experimental import pallas as pl
from jax.experimental.pallas import tpu as pltpu
from jax.sharding import PartitionSpec as P

B = 256
S = 64
VMEM_BYTES = 60 * 1024 * 1024
F32 = jnp.float32
BF16 = jnp.bfloat16
HIGH = lax.Precision.HIGHEST
VMEM_SPEC = pl.BlockSpec(memory_space=pltpu.VMEM)
SMEM_SPEC = pl.BlockSpec(memory_space=pltpu.SMEM)


def dot(a, b, dims, precision=None):
    return lax.dot_general(a, b, (dims, ((), ())), precision=precision, preferred_element_type=F32)


NN = ((1,), (0,))
NT = ((1,), (1,))
TN = ((0,), (0,))


def pick_kernel(slots, cov_ref, out_ref):
    parts, blocks, part, width = out_ref.shape
    for b in range(blocks):
        out_ref[:, b] = cov_ref[b * B : (b + 1) * B, :].reshape(parts, part, width)


def pick_columns(slots, covariance, parts):
    rows = covariance.shape[0]
    blocks = rows // B
    part = B // parts
    return pl.pallas_call(
        pick_kernel,
        grid_spec=pltpu.PrefetchScalarGridSpec(
            num_scalar_prefetch=1,
            grid=(2, blocks // 2),
            in_specs=[pl.BlockSpec((2 * B, B), lambda j, b, slots: (b, slots[j]))],
            out_specs=pl.BlockSpec((parts, 2, part, B), lambda j, b, slots: (0, b, 0, j)),
        ),
        out_shape=jax.ShapeDtypeStruct((parts, blocks, part, 2 * B), F32),
    )(slots, covariance)


def tiles_kernel(owner_ref, panel_ref, cov_ref, out_ref, held, arrived):
    slots = [jnp.int32(0), jnp.int32(0)]
    for place in range(owner_ref.shape[0]):
        for n in range(2):
            slots[n] = jnp.where(owner_ref[place] == panel_ref[0] + n, place, slots[n])
    row_blocks, column_blocks = cov_ref.shape[0] // B, cov_ref.shape[1] // B
    first_here = lax.div(slots[0], row_blocks) == lax.axis_index("row")
    row = lax.rem(jnp.where(first_here, slots[0], slots[1]), row_blocks)
    copies = []
    for n in range(2):
        column = lax.rem(slots[n], column_blocks)
        copies.append(
            pltpu.make_async_copy(
                cov_ref.at[pl.ds(pl.multiple_of(row * B, B), B), pl.ds(pl.multiple_of(column * B, B), B)],
                held.at[n],
                arrived.at[n],
            )
        )
        copies[n].start()
    for n in range(2):
        copies[n].wait()
        for i in range(B // 8):
            for j in range(2):
                out_ref[i, 2 * n + j] = held[n, 8 * i : 8 * i + 8, 128 * j : 128 * j + 128]


def pick_tiles(block_owner, panel_index, covariance):
    return pl.pallas_call(
        tiles_kernel,
        in_specs=[SMEM_SPEC, SMEM_SPEC, pl.BlockSpec(memory_space=pl.ANY)],
        out_specs=VMEM_SPEC,
        out_shape=jax.ShapeDtypeStruct((B // 8, 4, 8, 128), F32),
        scratch_shapes=[pltpu.VMEM((2, B, B), F32), pltpu.SemaphoreType.DMA((2,))],
    )(block_owner, panel_index, covariance)


def lanes(tile, j):
    return jnp.broadcast_to(tile[:, j : j + 1], (8, 128))


def eliminate(tiles):
    sub = lax.broadcasted_iota(jnp.int32, (8, 128), 0)
    scales = []
    for t in range(8):
        own = tiles[t]
        cols = [lanes(own, 8 * t + j) for j in range(8)]
        inv, cross = [], {}
        pivots = jnp.ones((8, 128), F32)
        for j in range(8):
            pivot = jnp.broadcast_to(cols[j][j : j + 1, :], (8, 128))
            pivots = jnp.where(sub == j, pivot, pivots)
            r = 1.0 / pivot
            inv.append(r)
            if j == 7:
                break
            m = jnp.where(sub > j, cols[j] * r, 0.0)
            for k in range(j + 1, 8):
                cross[j, k] = jnp.broadcast_to(cols[k][j : j + 1, :], (8, 128))
                cols[k] = cols[k] - m * cross[j, k]
            own = own - m * jnp.broadcast_to(own[j : j + 1, :], (8, 128))
        tiles[t] = own
        scales.append(lax.rsqrt(pivots))
        rows = [jnp.broadcast_to(own[j : j + 1, :], (8, 128)) for j in range(8)]
        for i in range(t + 1, 8):
            low = tiles[i]
            cols = [lanes(low, 8 * t + j) for j in range(8)]
            for j in range(8):
                m = cols[j] * inv[j]
                for k in range(j + 1, 8):
                    cols[k] = cols[k] - m * cross[j, k]
                low = low - m * rows[j]
            tiles[i] = low
    return tiles, scales


def factor_block(work, small, inverse_small):
    for b in range(B // S):
        lo, hi = b * S, (b + 1) * S
        small[:, 0:S] = work[lo:hi, lo:hi]
        row = lax.broadcasted_iota(jnp.int32, (S, S), 0)
        col = lax.broadcasted_iota(jnp.int32, (S, S), 1)
        small[:, S : 2 * S] = jnp.where(row == col, 1.0, 0.0)
        tiles, scales = eliminate([small[8 * i : 8 * i + 8, :] for i in range(8)])
        for i in range(8):
            small[8 * i : 8 * i + 8, :] = tiles[i] * scales[i]
        inverse_small[...] = small[:, S : 2 * S]
        top = dot(inverse_small[...], work[lo:hi, :], NN, HIGH)
        work[lo:hi, :] = top
        if hi < B:
            work[hi:B, :] = work[hi:B, :] - dot(top[:, hi:B], top, TN, HIGH)


def split(a):
    high = a.astype(BF16)
    rest = a - high.astype(F32)
    middle = rest.astype(BF16)
    return high, middle, (rest - middle.astype(F32)).astype(BF16)


def write_left(ref, a):
    high, middle, low = split(a)
    for n, term in enumerate((high, high, middle, high, low, middle)):
        ref[:, n * B : (n + 1) * B] = term


def write_right(ref, start, a):
    high, middle, low = split(a)
    for n, term in enumerate((high, middle, high, low, high, middle)):
        ref[:, start + n * B : start + (n + 1) * B] = term


def factor_kernel(tiles_ref, inverse_ref, l10t_ref, lower_ref, diag_ref, work, small, inverse_small):
    for i in range(B // 8):
        for j in range(4):
            diag_ref[8 * i : 8 * i + 8, 128 * j : 128 * j + 128] = tiles_ref[4 * i + j, 0:8]
        for j in range(2):
            diag_ref[8 * i : 8 * i + 8, 512 + 128 * j : 640 + 128 * j] = tiles_ref[4 * i + 2 + j, 8:16]
    row = lax.broadcasted_iota(jnp.int32, (B, B), 0)
    col = lax.broadcasted_iota(jnp.int32, (B, B), 1)
    eye = jnp.where(row == col, 1.0, 0.0)
    work[:, 0:B] = diag_ref[:, 0:B]
    work[:, B : 2 * B] = eye
    factor_block(work, small, inverse_small)
    x0 = work[:, B : 2 * B]
    write_right(inverse_ref, 0, x0)
    lower_ref[:, 0:B] = jnp.where(row <= col, work[:, 0:B], 0.0).T
    l10t = dot(x0, diag_ref[:, B : 2 * B], NN, HIGH).astype(BF16)
    l10t_ref[...] = l10t
    work[:, 0:B] = diag_ref[:, 2 * B : 3 * B] - dot(l10t, l10t, TN)
    work[:, B : 2 * B] = eye
    factor_block(work, small, inverse_small)
    write_right(inverse_ref, 6 * B, work[:, B : 2 * B])
    lower_ref[:, B : 2 * B] = jnp.where(row <= col, work[:, 0:B], 0.0).T


def factor_diagonal(tiles):
    return pl.pallas_call(
        factor_kernel,
        in_specs=[VMEM_SPEC],
        out_specs=[VMEM_SPEC] * 3,
        out_shape=[
            jax.ShapeDtypeStruct((B, 12 * B), BF16),
            jax.ShapeDtypeStruct((B, B), BF16),
            jax.ShapeDtypeStruct((B, 2 * B), F32),
        ],
        scratch_shapes=[
            pltpu.VMEM((B, 3 * B), F32),
            pltpu.VMEM((B, 2 * B), F32),
            pltpu.VMEM((S, 2 * S), F32),
            pltpu.VMEM((S, S), F32),
        ],
        compiler_params=pltpu.CompilerParams(vmem_limit_bytes=VMEM_BYTES),
        cost_estimate=pl.CostEstimate(flops=2 * 10**10, bytes_accessed=80_000_000, transcendentals=0),
    )(tiles)


def solve_rows(first, second, wide, inverse_ref, l10t_ref):
    write_left(wide, first)
    p0 = dot(wide[...], inverse_ref[:, 0 : 6 * B], NT)
    write_left(wide, second - dot(p0.astype(BF16), l10t_ref[...], NN))
    p1 = dot(wide[...], inverse_ref[:, 6 * B : 12 * B], NT)
    return p0, p1


def piece_kernel(flags, first_ref, second_ref, inverse_ref, l10t_ref, along_ref, across_ref, wide):
    blocks, part = first_ref.shape[1:3]
    solved = solve_rows(
        first_ref[0].reshape(blocks * part, B), second_ref[0].reshape(blocks * part, B), wide, inverse_ref, l10t_ref
    )
    for panel, p in enumerate(solved):
        cut = slice(panel * B, (panel + 1) * B)
        for b in range(blocks):
            mine = p[b * part : (b + 1) * part].astype(BF16)
            mine = jnp.where(flags[16 + b] > panel, mine, jnp.zeros_like(mine))
            across_ref[b, :, cut] = mine
            for q in range(along_ref.shape[0]):
                along_ref[q, b, :, cut] = mine


def solve_piece(flags, parts, inverse, l10t):
    count, blocks, part = parts.shape[:3]
    return pl.pallas_call(
        piece_kernel,
        grid_spec=pltpu.PrefetchScalarGridSpec(
            num_scalar_prefetch=1,
            grid=(1,),
            in_specs=[
                pl.BlockSpec((1, blocks, part, B), lambda i, flags: (flags[20], 0, 0, 0)),
                pl.BlockSpec((1, blocks, part, B), lambda i, flags: (flags[21], 0, 0, 1)),
                whole(*inverse.shape),
                whole(*l10t.shape),
            ],
            out_specs=[whole(count, blocks, part, 2 * B), whole(blocks, part, 2 * B)],
            scratch_shapes=[pltpu.VMEM((blocks * part, 6 * B), BF16)],
        ),
        out_shape=[
            jax.ShapeDtypeStruct((count, blocks, part, 2 * B), BF16),
            jax.ShapeDtypeStruct((blocks, part, 2 * B), BF16),
        ],
        compiler_params=pltpu.CompilerParams(vmem_limit_bytes=VMEM_BYTES),
        cost_estimate=pl.CostEstimate(flops=10**9, bytes_accessed=4_000_000, transcendentals=0),
    )(flags, parts, parts, inverse, l10t)


def whole(*shape):
    return pl.BlockSpec(shape, lambda i, flags: (0,) * len(shape))


def panel_kernel(flags, first_ref, second_ref, along_ref, inverse_ref, l10t_ref, out_ref, wide):
    level = flags[16 + pl.program_id(0)]
    parts, _, part = along_ref.shape[:3]

    @pl.when(flags[4] >= 0)
    def _():
        write_left(wide, first_ref[...])
        p = dot(wide[...], inverse_ref[:, 0 : 6 * B], NT)
        out_ref[:, 0:B] = jnp.where(level > 0, p, 0.0)

    @pl.when(flags[5] >= 0)
    def _():
        before = along_ref[:, 0, :, 0:B].reshape(parts * part, B)
        write_left(wide, second_ref[...] - dot(before, l10t_ref[...], NN))
        p = dot(wide[...], inverse_ref[:, 6 * B : 12 * B], NT)
        out_ref[:, B : 2 * B] = jnp.where(level > 1, p, 0.0)


def solve_panels(flags, covariance, along, inverse, l10t):
    rows = covariance.shape[0]
    parts, _, part, width = along.shape
    blocks = rows // B
    turn = lambda i, flags: jnp.where((flags[4] & flags[5]) >= 0, i, 0)
    return pl.pallas_call(
        panel_kernel,
        grid_spec=pltpu.PrefetchScalarGridSpec(
            num_scalar_prefetch=1,
            grid=(blocks,),
            in_specs=[
                pl.BlockSpec((B, B), lambda i, flags: (turn(i, flags), jnp.maximum(flags[4], 0))),
                pl.BlockSpec((B, B), lambda i, flags: (turn(i, flags), jnp.maximum(flags[5], 0))),
                pl.BlockSpec((parts, 1, part, width), lambda i, flags: (0, turn(i, flags), 0, 0)),
                whole(*inverse.shape),
                whole(*l10t.shape),
            ],
            out_specs=pl.BlockSpec((B, 2 * B), lambda i, flags: (turn(i, flags), 0)),
            scratch_shapes=[pltpu.VMEM((B, 6 * B), BF16)],
        ),
        out_shape=jax.ShapeDtypeStruct((rows, 2 * B), F32),
        compiler_params=pltpu.CompilerParams(vmem_limit_bytes=VMEM_BYTES),
        cost_estimate=pl.CostEstimate(flops=10**9, bytes_accessed=4_000_000, transcendentals=0),
    )(flags, covariance, covariance, along, inverse, l10t)


def update_kernel(
    flags,
    cov_ref,
    along_ref,
    across_ref,
    high_ref,
    middle_ref,
    low_ref,
    panel_ref,
    lower_ref,
    inverse_ref,
    l10t_ref,
    out_ref,
    solved_ref,
    columns,
    terms_ref,
    white_ref,
    wide,
    arrived,
):
    i = pl.program_id(0)
    parts, _, part = along_ref.shape[:3]
    blocks = across_ref.shape[1] - 3
    steps = parts // 2
    column_blocks = 2 * blocks
    fold = high_ref.shape[2]
    half = 2 * fold

    @pl.when(i == 0)
    def _():
        copies = []
        for panel in range(2):
            for n in range(4):
                source = across_ref.at[4 * flags[6 + panel] + n, pl.ds(blocks, 3)]
                copies.append(pltpu.make_async_copy(source, terms_ref.at[panel, n], arrived.at[len(copies)]))
        for q in range(parts):
            first = 4 * lax.rem(q // 2 + flags[0], steps) + 2 * (q % 2)
            for parity in range(2):
                source = across_ref.at[first + parity, pl.ds(0, blocks)]
                copies.append(pltpu.make_async_copy(source, columns.at[parity, :, q], arrived.at[len(copies)]))
        for copy in copies:
            copy.start()
        for copy in copies[:8]:
            copy.wait()
        for panel in range(2):
            for h in range(2):
                for parity in range(2):
                    for f in range(2):
                        lane = (2 * f + panel) * 128
                        terms = [
                            terms_ref[panel, 2 * h + parity, t, :, lane : lane + 128].astype(F32) for t in range(3)
                        ]
                        top = (2 * parity + f) * fold
                        white_ref[top : top + fold, panel * B + h * 128 : panel * B + (h + 1) * 128] = (
                            terms[0] + terms[1]
                        ) + terms[2]
        w0, w1 = solve_rows(white_ref[:, 0:B], white_ref[:, B : 2 * B], wide, inverse_ref, l10t_ref)
        white_ref[:, 0:B] = w0
        white_ref[:, B : 2 * B] = w1
        for copy in copies[8:]:
            copy.wait()

    level = flags[16 + i]
    own = along_ref[:, 0].reshape(parts * part, 2 * B)
    for n in range(column_blocks):
        cut = slice(n * B, (n + 1) * B)
        out_ref[:, cut] = cov_ref[:, cut] - dot(own, columns[n // blocks, n % blocks].reshape(B, 2 * B), NT)

    for panel in range(2):
        is_row = i == flags[2 + panel]
        for n in range(column_blocks):

            @pl.when(is_row & (flags[8 + n] > panel))
            def _():
                out_ref[:, n * B : (n + 1) * B] = jnp.zeros((B, B), F32)

        column = flags[4 + panel]
        place = pl.ds(pl.multiple_of(jnp.maximum(column, 0) * B, B), B)

        @pl.when((column >= 0) & (level > panel))
        def _():
            out_ref[:, place] = panel_ref[:, panel * B : (panel + 1) * B]

        @pl.when((column >= 0) & is_row)
        def _():
            out_ref[:, place] = lower_ref[:, panel * B : (panel + 1) * B]

    product = dot(white_ref[...].astype(BF16), own, NT)
    for parity in range(2):
        for h in range(2):
            for f in range(2):
                top, lane = parity * half + f * fold, (2 * parity + f) * 128
                there = (slice(top, top + fold), slice(h * 128, (h + 1) * 128))
                cut = (h, 0, slice(None), slice(lane, lane + 128))
                held = (high_ref[cut].astype(F32) + middle_ref[cut].astype(F32)) + low_ref[cut].astype(F32)
                solved_ref[there] = held - product[there]
    for panel in range(2):

        @pl.when(i == flags[2 + panel])
        def _():
            solved_ref[...] = white_ref[:, panel * B : (panel + 1) * B]


def update(flags, covariance, along, across, panels, lower, inverse, l10t):
    rows, columns = covariance.shape
    parts, _, part, width = along.shape
    blocks = rows // B
    half = 2 * part
    return pl.pallas_call(
        update_kernel,
        grid_spec=pltpu.PrefetchScalarGridSpec(
            num_scalar_prefetch=1,
            grid=(blocks,),
            in_specs=[
                pl.BlockSpec((B, columns), lambda i, flags: (i, 0)),
                pl.BlockSpec((parts, 1, part, width), lambda i, flags: (0, i, 0, 0)),
                pl.BlockSpec(memory_space=pl.ANY),
                pl.BlockSpec((2, 1, part, width), lambda i, flags: (i, blocks, 0, 0)),
                pl.BlockSpec((2, 1, part, width), lambda i, flags: (i, blocks + 1, 0, 0)),
                pl.BlockSpec((2, 1, part, width), lambda i, flags: (i, blocks + 2, 0, 0)),
                pl.BlockSpec((B, width), lambda i, flags: (jnp.where((flags[4] & flags[5]) >= 0, i, 0), 0)),
                whole(*lower.shape),
                whole(*inverse.shape),
                whole(*l10t.shape),
            ],
            out_specs=[
                pl.BlockSpec((B, columns), lambda i, flags: (i, 0)),
                pl.BlockSpec((2 * half, B), lambda i, flags: (0, i)),
            ],
            scratch_shapes=[
                pltpu.VMEM((2, columns // (2 * B), parts, part, width), BF16),
                pltpu.VMEM((2, 4, 3, part, width), BF16),
                pltpu.VMEM((2 * half, width), F32),
                pltpu.VMEM((2 * half, 6 * B), BF16),
                pltpu.SemaphoreType.DMA((2 * parts + 8,)),
            ],
        ),
        out_shape=[jax.ShapeDtypeStruct((rows, columns), F32), jax.ShapeDtypeStruct((2 * half, rows), F32)],
        compiler_params=pltpu.CompilerParams(vmem_limit_bytes=VMEM_BYTES),
        cost_estimate=pl.CostEstimate(flops=5 * 10**9, bytes_accessed=20_000_000, transcendentals=0),
    )(flags, covariance, along, across, along, along, along, panels, lower, inverse, l10t)


def per_device(covariance, innovations, block_owner, panel_index, *, n_row, n_col):
    local_rows, local_cols = covariance.shape
    row_blocks, column_blocks = local_rows // B, local_cols // B
    r, c = lax.axis_index("row"), lax.axis_index("col")
    targets = panel_index[0] + jnp.arange(2, dtype=jnp.int32)
    positions = jnp.arange(block_owner.shape[0], dtype=jnp.int32)
    slot = jnp.sum(jnp.where(block_owner[None, :] == targets[:, None], positions[None, :], 0), axis=1)
    row_root, column_root = slot // row_blocks, slot // column_blocks
    row_slot, column_slot = slot % row_blocks, slot % column_blocks
    levels = jnp.sum((block_owner[:, None] > targets[None, :]).astype(jnp.int32), axis=1)
    steps = n_row // 4
    shift, core = c // 2, r % 2
    flags = jnp.concatenate(
        [
            shift[None],
            core[None],
            jnp.where(row_root == r, row_slot, -1),
            jnp.where(column_root == c, column_slot, -1),
            (row_slot + shift) % steps,
            lax.dynamic_slice_in_dim(levels, c * column_blocks, column_blocks),
            lax.dynamic_slice_in_dim(levels, r * row_blocks, row_blocks),
            column_root,
        ]
    ).astype(jnp.int32)
    across_axes = [
        (a * n_col + b, ((b // 2 + a // 4) % steps * 4 + b % 2 * 2 + a % 2) * n_col + a // 2)
        for a in range(n_row)
        for b in range(n_col)
    ]

    fold = innovations.shape[0] // 2
    wanted = [lax.dynamic_index_in_dim(innovations, row_root[n], 1, keepdims=False) for n in range(2)]
    wanted = jnp.concatenate([w[h * fold : (h + 1) * fold] for h in range(2) for w in wanted], axis=1)
    wanted = lax.ppermute(wanted, ("row", "col"), across_axes)

    tiles = pick_tiles(block_owner, panel_index, covariance).reshape(n_row * n_col, 8, 128)
    tiles = lax.all_to_all(tiles, ("row", "col"), split_axis=0, concat_axis=0, tiled=True)
    source = jnp.where(c % 4 < 2, column_root[0], column_root[1])
    tiles = jnp.concatenate(
        [lax.dynamic_index_in_dim(tiles, row_root[n] * n_col + source, 0, keepdims=False) for n in range(2)], axis=0
    )
    tiles = lax.all_to_all(
        jnp.broadcast_to(tiles[None], (n_row * n_col,) + tiles.shape),
        ("row", "col"),
        split_axis=0,
        concat_axis=0,
        tiled=True,
    )
    tiles, wanted = lax.optimization_barrier((tiles, wanted))
    inverse, l10t, lower = factor_diagonal(tiles)

    picked = pick_columns(column_slot.astype(jnp.int32), covariance, n_col)
    picked, _ = lax.optimization_barrier((picked, tiles))
    parts = lax.all_to_all(picked, "col", split_axis=0, concat_axis=0, tiled=True)

    high = lax.reduce_precision(wanted, 8, 7)
    middle = lax.reduce_precision(wanted - high, 8, 7)
    wanted = jnp.stack([high, middle, wanted - high - middle]).astype(BF16)

    groups, _, _ = lax.optimization_barrier((jnp.transpose(innovations, (1, 0, 2)), parts, l10t))
    groups = lax.all_to_all(groups, "row", split_axis=0, concat_axis=0, tiled=True)

    along, across = solve_piece(flags, parts, inverse, l10t)
    across = lax.ppermute(across, ("row", "col"), across_axes)
    across, groups = lax.optimization_barrier((across, groups))
    across = lax.all_gather(jnp.concatenate([across, wanted], axis=0), "row", axis=0)
    groups = groups.reshape(n_col, 2, 2 * fold, 128)
    groups = jnp.concatenate(
        [groups[:, parity, f * fold : (f + 1) * fold] for parity in range(2) for f in range(2)], axis=2
    )
    high = lax.reduce_precision(groups, 8, 7)
    middle = lax.reduce_precision(groups - high, 8, 7)
    terms = jnp.stack([high, middle, groups - high - middle], axis=1).astype(BF16)
    along = jnp.concatenate([along, terms], axis=1)
    along = lax.all_to_all(along, "col", split_axis=0, concat_axis=0, tiled=True)
    panels = solve_panels(flags, covariance, along, inverse, l10t)
    return update(flags, covariance, along, across, panels, lower, inverse, l10t)


def solution(mesh):
    placed = (P("row", "col"), P("row", None, "col"), P(), P())
    return jax.shard_map(
        functools.partial(per_device, n_row=mesh.shape["row"], n_col=mesh.shape["col"]),
        mesh=mesh,
        in_specs=placed,
        out_specs=(P("row", "col"), P("col", "row")),
        check_vma=False,
    )
```

```python
import functools

import jax
import jax.numpy as jnp
from jax import lax
from jax.experimental import pallas as pl
from jax.experimental.pallas import tpu as pltpu
from jax.sharding import PartitionSpec as P

B = 256
S = 64
VMEM_BYTES = 60 * 1024 * 1024
F32 = jnp.float32
BF16 = jnp.bfloat16
HIGH = lax.Precision.HIGHEST
VMEM_SPEC = pl.BlockSpec(memory_space=pltpu.VMEM)
SMEM_SPEC = pl.BlockSpec(memory_space=pltpu.SMEM)


def dot(a, b, dims, precision=None):
    return lax.dot_general(a, b, (dims, ((), ())), precision=precision, preferred_element_type=F32)


NN = ((1,), (0,))
NT = ((1,), (1,))
TN = ((0,), (0,))


def pick_kernel(slots, cov_ref, out_ref):
    parts, blocks, part, width = out_ref.shape
    for b in range(blocks):
        out_ref[:, b] = cov_ref[b * B : (b + 1) * B, :].reshape(parts, part, width)


def pick_columns(slots, covariance, parts):
    rows = covariance.shape[0]
    blocks = rows // B
    part = B // parts
    return pl.pallas_call(
        pick_kernel,
        grid_spec=pltpu.PrefetchScalarGridSpec(
            num_scalar_prefetch=1,
            grid=(2, blocks // 2),
            in_specs=[pl.BlockSpec((2 * B, B), lambda j, b, slots: (b, slots[j]))],
            out_specs=pl.BlockSpec((parts, 2, part, B), lambda j, b, slots: (0, b, 0, j)),
        ),
        out_shape=jax.ShapeDtypeStruct((parts, blocks, part, 2 * B), F32),
    )(slots, covariance)


def tiles_kernel(owner_ref, panel_ref, cov_ref, out_ref, held, arrived):
    slots = [jnp.int32(0), jnp.int32(0)]
    for place in range(owner_ref.shape[0]):
        for n in range(2):
            slots[n] = jnp.where(owner_ref[place] == panel_ref[0] + n, place, slots[n])
    row_blocks, column_blocks = cov_ref.shape[0] // B, cov_ref.shape[1] // B
    first_here = lax.div(slots[0], row_blocks) == lax.axis_index("row")
    row = lax.rem(jnp.where(first_here, slots[0], slots[1]), row_blocks)
    copies = []
    for n in range(2):
        column = lax.rem(slots[n], column_blocks)
        copies.append(
            pltpu.make_async_copy(
                cov_ref.at[pl.ds(pl.multiple_of(row * B, B), B), pl.ds(pl.multiple_of(column * B, B), B)],
                held.at[n],
                arrived.at[n],
            )
        )
        copies[n].start()
    for n in range(2):
        copies[n].wait()
        for i in range(B // 8):
            for j in range(2):
                out_ref[i, 2 * n + j] = held[n, 8 * i : 8 * i + 8, 128 * j : 128 * j + 128]


def pick_tiles(block_owner, panel_index, covariance):
    return pl.pallas_call(
        tiles_kernel,
        in_specs=[SMEM_SPEC, SMEM_SPEC, pl.BlockSpec(memory_space=pl.ANY)],
        out_specs=VMEM_SPEC,
        out_shape=jax.ShapeDtypeStruct((B // 8, 4, 8, 128), F32),
        scratch_shapes=[pltpu.VMEM((2, B, B), F32), pltpu.SemaphoreType.DMA((2,))],
    )(block_owner, panel_index, covariance)


def lanes(tile, j):
    return jnp.broadcast_to(tile[:, j : j + 1], (8, 128))


def eliminate(tiles):
    sub = lax.broadcasted_iota(jnp.int32, (8, 128), 0)
    scales = []
    for t in range(8):
        own = tiles[t]
        cols = [lanes(own, 8 * t + j) for j in range(8)]
        inv, cross = [], {}
        pivots = jnp.ones((8, 128), F32)
        for j in range(8):
            pivot = jnp.broadcast_to(cols[j][j : j + 1, :], (8, 128))
            pivots = jnp.where(sub == j, pivot, pivots)
            r = 1.0 / pivot
            inv.append(r)
            if j == 7:
                break
            m = jnp.where(sub > j, cols[j] * r, 0.0)
            for k in range(j + 1, 8):
                cross[j, k] = jnp.broadcast_to(cols[k][j : j + 1, :], (8, 128))
                cols[k] = cols[k] - m * cross[j, k]
            own = own - m * jnp.broadcast_to(own[j : j + 1, :], (8, 128))
        tiles[t] = own
        scales.append(lax.rsqrt(pivots))
        rows = [jnp.broadcast_to(own[j : j + 1, :], (8, 128)) for j in range(8)]
        for i in range(t + 1, 8):
            low = tiles[i]
            cols = [lanes(low, 8 * t + j) for j in range(8)]
            for j in range(8):
                m = cols[j] * inv[j]
                for k in range(j + 1, 8):
                    cols[k] = cols[k] - m * cross[j, k]
                low = low - m * rows[j]
            tiles[i] = low
    return tiles, scales


def factor_block(work, small, inverse_small):
    for b in range(B // S):
        lo, hi = b * S, (b + 1) * S
        small[:, 0:S] = work[lo:hi, lo:hi]
        row = lax.broadcasted_iota(jnp.int32, (S, S), 0)
        col = lax.broadcasted_iota(jnp.int32, (S, S), 1)
        small[:, S : 2 * S] = jnp.where(row == col, 1.0, 0.0)
        tiles, scales = eliminate([small[8 * i : 8 * i + 8, :] for i in range(8)])
        for i in range(8):
            small[8 * i : 8 * i + 8, :] = tiles[i] * scales[i]
        inverse_small[...] = small[:, S : 2 * S]
        top = dot(inverse_small[...], work[lo:hi, :], NN, HIGH)
        work[lo:hi, :] = top
        if hi < B:
            work[hi:B, :] = work[hi:B, :] - dot(top[:, hi:B], top, TN, HIGH)


def split(a):
    high = a.astype(BF16)
    rest = a - high.astype(F32)
    middle = rest.astype(BF16)
    return high, middle, (rest - middle.astype(F32)).astype(BF16)


def write_left(ref, a):
    high, middle, low = split(a)
    for n, term in enumerate((high, high, middle, high, low, middle)):
        ref[:, n * B : (n + 1) * B] = term


def write_right(ref, start, a):
    high, middle, low = split(a)
    for n, term in enumerate((high, middle, high, low, high, middle)):
        ref[:, start + n * B : start + (n + 1) * B] = term


def factor_kernel(tiles_ref, inverse_ref, l10t_ref, lower_ref, diag_ref, work, small, inverse_small):
    for i in range(B // 8):
        for j in range(4):
            diag_ref[8 * i : 8 * i + 8, 128 * j : 128 * j + 128] = tiles_ref[4 * i + j, 0:8]
        for j in range(2):
            diag_ref[8 * i : 8 * i + 8, 512 + 128 * j : 640 + 128 * j] = tiles_ref[4 * i + 2 + j, 8:16]
    row = lax.broadcasted_iota(jnp.int32, (B, B), 0)
    col = lax.broadcasted_iota(jnp.int32, (B, B), 1)
    eye = jnp.where(row == col, 1.0, 0.0)
    work[:, 0:B] = diag_ref[:, 0:B]
    work[:, B : 2 * B] = eye
    factor_block(work, small, inverse_small)
    x0 = work[:, B : 2 * B]
    write_right(inverse_ref, 0, x0)
    lower_ref[:, 0:B] = jnp.where(row <= col, work[:, 0:B], 0.0).T
    l10t = dot(x0, diag_ref[:, B : 2 * B], NN, HIGH).astype(BF16)
    l10t_ref[...] = l10t
    work[:, 0:B] = diag_ref[:, 2 * B : 3 * B] - dot(l10t, l10t, TN)
    work[:, B : 2 * B] = eye
    factor_block(work, small, inverse_small)
    write_right(inverse_ref, 6 * B, work[:, B : 2 * B])
    lower_ref[:, B : 2 * B] = jnp.where(row <= col, work[:, 0:B], 0.0).T


def factor_diagonal(tiles):
    return pl.pallas_call(
        factor_kernel,
        in_specs=[VMEM_SPEC],
        out_specs=[VMEM_SPEC] * 3,
        out_shape=[
            jax.ShapeDtypeStruct((B, 12 * B), BF16),
            jax.ShapeDtypeStruct((B, B), BF16),
            jax.ShapeDtypeStruct((B, 2 * B), F32),
        ],
        scratch_shapes=[
            pltpu.VMEM((B, 3 * B), F32),
            pltpu.VMEM((B, 2 * B), F32),
            pltpu.VMEM((S, 2 * S), F32),
            pltpu.VMEM((S, S), F32),
        ],
        compiler_params=pltpu.CompilerParams(vmem_limit_bytes=VMEM_BYTES),
        cost_estimate=pl.CostEstimate(flops=2 * 10**10, bytes_accessed=80_000_000, transcendentals=0),
    )(tiles)


def solve_rows(first, second, wide, inverse_ref, l10t_ref):
    write_left(wide, first)
    p0 = dot(wide[...], inverse_ref[:, 0 : 6 * B], NT)
    write_left(wide, second - dot(p0.astype(BF16), l10t_ref[...], NN))
    p1 = dot(wide[...], inverse_ref[:, 6 * B : 12 * B], NT)
    return p0, p1


def piece_kernel(flags, first_ref, second_ref, inverse_ref, l10t_ref, along_ref, across_ref, wide):
    blocks, part = first_ref.shape[1:3]
    solved = solve_rows(
        first_ref[0].reshape(blocks * part, B), second_ref[0].reshape(blocks * part, B), wide, inverse_ref, l10t_ref
    )
    for panel, p in enumerate(solved):
        cut = slice(panel * B, (panel + 1) * B)
        for b in range(blocks):
            mine = p[b * part : (b + 1) * part].astype(BF16)
            mine = jnp.where(flags[16 + b] > panel, mine, jnp.zeros_like(mine))
            across_ref[b, :, cut] = mine
            for q in range(along_ref.shape[0]):
                along_ref[q, b, :, cut] = mine


def solve_piece(flags, parts, inverse, l10t):
    count, blocks, part = parts.shape[:3]
    return pl.pallas_call(
        piece_kernel,
        grid_spec=pltpu.PrefetchScalarGridSpec(
            num_scalar_prefetch=1,
            grid=(1,),
            in_specs=[
                pl.BlockSpec((1, blocks, part, B), lambda i, flags: (flags[20], 0, 0, 0)),
                pl.BlockSpec((1, blocks, part, B), lambda i, flags: (flags[21], 0, 0, 1)),
                whole(*inverse.shape),
                whole(*l10t.shape),
            ],
            out_specs=[whole(count, blocks, part, 2 * B), whole(blocks, part, 2 * B)],
            scratch_shapes=[pltpu.VMEM((blocks * part, 6 * B), BF16)],
        ),
        out_shape=[
            jax.ShapeDtypeStruct((count, blocks, part, 2 * B), BF16),
            jax.ShapeDtypeStruct((blocks, part, 2 * B), BF16),
        ],
        compiler_params=pltpu.CompilerParams(vmem_limit_bytes=VMEM_BYTES),
        cost_estimate=pl.CostEstimate(flops=10**9, bytes_accessed=4_000_000, transcendentals=0),
    )(flags, parts, parts, inverse, l10t)


def whole(*shape):
    return pl.BlockSpec(shape, lambda i, flags: (0,) * len(shape))


def panel_kernel(flags, first_ref, second_ref, along_ref, inverse_ref, l10t_ref, out_ref, wide):
    level = flags[16 + pl.program_id(0)]
    parts, _, part = along_ref.shape[:3]

    @pl.when(flags[4] >= 0)
    def _():
        write_left(wide, first_ref[...])
        p = dot(wide[...], inverse_ref[:, 0 : 6 * B], NT)
        out_ref[:, 0:B] = jnp.where(level > 0, p, 0.0)

    @pl.when(flags[5] >= 0)
    def _():
        before = along_ref[:, 0, :, 0:B].reshape(parts * part, B)
        write_left(wide, second_ref[...] - dot(before, l10t_ref[...], NN))
        p = dot(wide[...], inverse_ref[:, 6 * B : 12 * B], NT)
        out_ref[:, B : 2 * B] = jnp.where(level > 1, p, 0.0)


def solve_panels(flags, covariance, along, inverse, l10t):
    rows = covariance.shape[0]
    parts, blocks, part, width = along.shape
    turn = lambda i, flags: jnp.where((flags[4] & flags[5]) >= 0, i, 0)
    return pl.pallas_call(
        panel_kernel,
        grid_spec=pltpu.PrefetchScalarGridSpec(
            num_scalar_prefetch=1,
            grid=(blocks,),
            in_specs=[
                pl.BlockSpec((B, B), lambda i, flags: (turn(i, flags), jnp.maximum(flags[4], 0))),
                pl.BlockSpec((B, B), lambda i, flags: (turn(i, flags), jnp.maximum(flags[5], 0))),
                pl.BlockSpec((parts, 1, part, width), lambda i, flags: (0, turn(i, flags), 0, 0)),
                whole(*inverse.shape),
                whole(*l10t.shape),
            ],
            out_specs=pl.BlockSpec((B, 2 * B), lambda i, flags: (turn(i, flags), 0)),
            scratch_shapes=[pltpu.VMEM((B, 6 * B), BF16)],
        ),
        out_shape=jax.ShapeDtypeStruct((rows, 2 * B), F32),
        compiler_params=pltpu.CompilerParams(vmem_limit_bytes=VMEM_BYTES),
        cost_estimate=pl.CostEstimate(flops=10**9, bytes_accessed=4_000_000, transcendentals=0),
    )(flags, covariance, covariance, along, inverse, l10t)


def update_kernel(
    flags,
    cov_ref,
    along_ref,
    across_ref,
    relaid_ref,
    panel_ref,
    lower_ref,
    inverse_ref,
    l10t_ref,
    out_ref,
    solved_ref,
    columns,
    terms_ref,
    white_ref,
    wide,
    arrived,
):
    i = pl.program_id(0)
    parts, _, part = along_ref.shape[:3]
    blocks = across_ref.shape[1] - 3
    steps = parts // 2
    column_blocks = 2 * blocks
    half = relaid_ref.shape[1]
    fold = half // 2

    @pl.when(i == 0)
    def _():
        copies = []
        for panel in range(2):
            for n in range(4):
                source = across_ref.at[4 * flags[6 + panel] + n, pl.ds(blocks, 3)]
                copies.append(pltpu.make_async_copy(source, terms_ref.at[panel, n], arrived.at[len(copies)]))
        for q in range(parts):
            first = 4 * lax.rem(q // 2 + flags[0], steps) + 2 * (q % 2)
            for parity in range(2):
                source = across_ref.at[first + parity, pl.ds(0, blocks)]
                copies.append(pltpu.make_async_copy(source, columns.at[parity, :, q], arrived.at[len(copies)]))
        for copy in copies:
            copy.start()
        for copy in copies[:8]:
            copy.wait()
        for panel in range(2):
            for h in range(2):
                for parity in range(2):
                    for f in range(2):
                        lane = (2 * f + panel) * 128
                        terms = [
                            terms_ref[panel, 2 * h + parity, t, :, lane : lane + 128].astype(F32) for t in range(3)
                        ]
                        top = (2 * parity + f) * fold
                        white_ref[top : top + fold, panel * B + h * 128 : panel * B + (h + 1) * 128] = (
                            terms[0] + terms[1]
                        ) + terms[2]
        w0, w1 = solve_rows(white_ref[:, 0:B], white_ref[:, B : 2 * B], wide, inverse_ref, l10t_ref)
        white_ref[:, 0:B] = w0
        white_ref[:, B : 2 * B] = w1
        for copy in copies[8:]:
            copy.wait()

    level = flags[16 + i]
    own = along_ref[:, 0].reshape(parts * part, 2 * B)
    for n in range(column_blocks):
        cut = slice(n * B, (n + 1) * B)
        out_ref[:, cut] = cov_ref[:, cut] - dot(own, columns[n // blocks, n % blocks].reshape(B, 2 * B), NT)

    for panel in range(2):
        is_row = i == flags[2 + panel]
        for n in range(column_blocks):

            @pl.when(is_row & (flags[8 + n] > panel))
            def _():
                out_ref[:, n * B : (n + 1) * B] = jnp.zeros((B, B), F32)

        column = flags[4 + panel]
        place = pl.ds(pl.multiple_of(jnp.maximum(column, 0) * B, B), B)

        @pl.when((column >= 0) & (level > panel))
        def _():
            out_ref[:, place] = panel_ref[:, panel * B : (panel + 1) * B]

        @pl.when((column >= 0) & is_row)
        def _():
            out_ref[:, place] = lower_ref[:, panel * B : (panel + 1) * B]

    product = dot(white_ref[...].astype(BF16), own, NT)
    for parity in range(2):
        for h in range(2):
            there = (slice(parity * half, (parity + 1) * half), slice(h * 128, (h + 1) * 128))
            solved_ref[there] = relaid_ref[2 * h + parity] - product[there]
    for panel in range(2):

        @pl.when(i == flags[2 + panel])
        def _():
            solved_ref[...] = white_ref[:, panel * B : (panel + 1) * B]


def update(flags, covariance, along, across, relaid, panels, lower, inverse, l10t):
    rows, columns = covariance.shape
    parts, blocks, part, width = along.shape
    half = relaid.shape[1]
    return pl.pallas_call(
        update_kernel,
        grid_spec=pltpu.PrefetchScalarGridSpec(
            num_scalar_prefetch=1,
            grid=(blocks,),
            in_specs=[
                pl.BlockSpec((B, columns), lambda i, flags: (i, 0)),
                pl.BlockSpec((parts, 1, part, width), lambda i, flags: (0, i, 0, 0)),
                pl.BlockSpec(memory_space=pl.ANY),
                pl.BlockSpec((4, half, 128), lambda i, flags: (i, 0, 0)),
                pl.BlockSpec((B, width), lambda i, flags: (jnp.where((flags[4] & flags[5]) >= 0, i, 0), 0)),
                whole(*lower.shape),
                whole(*inverse.shape),
                whole(*l10t.shape),
            ],
            out_specs=[
                pl.BlockSpec((B, columns), lambda i, flags: (i, 0)),
                pl.BlockSpec((2 * half, B), lambda i, flags: (0, i)),
            ],
            scratch_shapes=[
                pltpu.VMEM((2, columns // (2 * B), parts, part, width), BF16),
                pltpu.VMEM((2, 4, 3, part, width), BF16),
                pltpu.VMEM((2 * half, width), F32),
                pltpu.VMEM((2 * half, 6 * B), BF16),
                pltpu.SemaphoreType.DMA((2 * parts + 8,)),
            ],
        ),
        out_shape=[jax.ShapeDtypeStruct((rows, columns), F32), jax.ShapeDtypeStruct((2 * half, rows), F32)],
        compiler_params=pltpu.CompilerParams(vmem_limit_bytes=VMEM_BYTES),
        cost_estimate=pl.CostEstimate(flops=5 * 10**9, bytes_accessed=20_000_000, transcendentals=0),
    )(flags, covariance, along, across, relaid, panels, lower, inverse, l10t)


def per_device(covariance, innovations, block_owner, panel_index, *, n_row, n_col):
    local_rows, local_cols = covariance.shape
    row_blocks, column_blocks = local_rows // B, local_cols // B
    r, c = lax.axis_index("row"), lax.axis_index("col")
    targets = panel_index[0] + jnp.arange(2, dtype=jnp.int32)
    positions = jnp.arange(block_owner.shape[0], dtype=jnp.int32)
    slot = jnp.sum(jnp.where(block_owner[None, :] == targets[:, None], positions[None, :], 0), axis=1)
    row_root, column_root = slot // row_blocks, slot // column_blocks
    row_slot, column_slot = slot % row_blocks, slot % column_blocks
    levels = jnp.sum((block_owner[:, None] > targets[None, :]).astype(jnp.int32), axis=1)
    steps = n_row // 4
    shift, core = c // 2, r % 2
    flags = jnp.concatenate(
        [
            shift[None],
            core[None],
            jnp.where(row_root == r, row_slot, -1),
            jnp.where(column_root == c, column_slot, -1),
            (row_slot + shift) % steps,
            lax.dynamic_slice_in_dim(levels, c * column_blocks, column_blocks),
            lax.dynamic_slice_in_dim(levels, r * row_blocks, row_blocks),
            column_root,
        ]
    ).astype(jnp.int32)
    across_axes = [
        (a * n_col + b, ((b // 2 + a // 4) % steps * 4 + b % 2 * 2 + a % 2) * n_col + a // 2)
        for a in range(n_row)
        for b in range(n_col)
    ]

    fold = innovations.shape[0] // 2
    wanted = [lax.dynamic_index_in_dim(innovations, row_root[n], 1, keepdims=False) for n in range(2)]
    wanted = jnp.concatenate([w[h * fold : (h + 1) * fold] for h in range(2) for w in wanted], axis=1)
    wanted = lax.ppermute(wanted, ("row", "col"), across_axes)

    tiles = pick_tiles(block_owner, panel_index, covariance).reshape(n_row * n_col, 8, 128)
    tiles = lax.all_to_all(tiles, ("row", "col"), split_axis=0, concat_axis=0, tiled=True)
    source = jnp.where(c % 4 < 2, column_root[0], column_root[1])
    tiles = jnp.concatenate(
        [lax.dynamic_index_in_dim(tiles, row_root[n] * n_col + source, 0, keepdims=False) for n in range(2)], axis=0
    )
    tiles = lax.all_to_all(
        jnp.broadcast_to(tiles[None], (n_row * n_col,) + tiles.shape),
        ("row", "col"),
        split_axis=0,
        concat_axis=0,
        tiled=True,
    )
    tiles, wanted = lax.optimization_barrier((tiles, wanted))
    inverse, l10t, lower = factor_diagonal(tiles)

    picked = pick_columns(column_slot.astype(jnp.int32), covariance, n_col)
    picked, _ = lax.optimization_barrier((picked, tiles))
    parts = lax.all_to_all(picked, "col", split_axis=0, concat_axis=0, tiled=True)

    high = lax.reduce_precision(wanted, 8, 7)
    middle = lax.reduce_precision(wanted - high, 8, 7)
    wanted = jnp.stack([high, middle, wanted - high - middle]).astype(BF16)

    along, across = solve_piece(flags, parts, inverse, l10t)
    groups, _ = lax.optimization_barrier((jnp.transpose(innovations, (1, 0, 2)), across))
    groups = lax.all_to_all(groups, "row", split_axis=0, concat_axis=0, tiled=True)
    across = lax.ppermute(across, ("row", "col"), across_axes)
    across = lax.all_gather(jnp.concatenate([across, wanted], axis=0), "row", axis=0)
    along, groups = lax.optimization_barrier((along, groups))
    along = lax.all_to_all(along, "col", split_axis=0, concat_axis=0, tiled=True)
    along, groups = lax.optimization_barrier((along, groups))
    relaid = lax.all_to_all(groups, "col", split_axis=0, concat_axis=0, tiled=True)
    panels = solve_panels(flags, covariance, along, inverse, l10t)
    return update(flags, covariance, along, across, relaid, panels, lower, inverse, l10t)


def solution(mesh):
    placed = (P("row", "col"), P("row", None, "col"), P(), P())
    return jax.shard_map(
        functools.partial(per_device, n_row=mesh.shape["row"], n_col=mesh.shape["col"]),
        mesh=mesh,
        in_specs=placed,
        out_specs=(P("row", "col"), P("col", "row")),
        check_vma=False,
    )
```
